128 devices in a mesh: ctx: 64 (over z, x_lo, y, core), head: 2 (over x_hi).
Axes of the slice: x: 4 (x_hi: 2, x_lo: 2; x = x_hi * 2 + x_lo), y: 4, z: 4, core: 2. Of those that a mesh axis runs over, the one named last changes fastest.
Arguments:
- queries: bfloat16 [32768, 2048], P('ctx', 'head'), may hold values from -6 to 6
- keys: bfloat16 [32768, 2048], P('ctx', 'head'), may hold values from -6 to 6
- values: bfloat16 [32768, 2048], P('ctx', 'head'), may hold values from -6 to 6
- rates: float32 [32768, 2], P('ctx', 'head'), may hold values from 0.0002762136 to 0.0027621358
- w_up: bfloat16 [2, 1024, 512], P('head'), may hold values from -0.1875 to 0.1875
- w_gate: bfloat16 [2, 1024, 512], P('head'), may hold values from -0.1875 to 0.1875
- w_down: bfloat16 [2, 512, 1024], P('head'), may hold values from -0.25 to 0.25
- w_out: bfloat16 [2048, 5120], P('head'), may hold values from -0.125 to 0.125
Outputs:
- mixed: bfloat16 [32768, 5120], P('ctx', 'head')
The draws below stay inside these ranges and needn't reach their ends.
All inputs are finite; a program needn't handle non-finite values.
Results may differ from the reference program's by a relative error of at most 0.018.
Values may be sent and summed in bfloat16 or wider, within the bound.
No kernel may reach another device: no remote copies, remote signals or barrier semaphores. Data moves between devices by JAX's collectives and lax.ppermute only.
A program may use at most 128 MiB of HBM per device.

```python
import math
import jax
import jax.numpy as jnp
from jax import lax

D = 5120
FD = 1024
FH = 512
STEPS = 2
FHEADS = 2
TOKENS = 32768


def steps_of(own_key, shape, cuts, low, high):
    def one(position, shards_of):
        heights = jax.random.uniform(jax.random.fold_in(jax.random.fold_in(own_key, 6), position), (shards_of,), jnp.float32, low / len(cuts), high / len(cuts))
        return jnp.repeat(jnp.exp(heights), shape[position] // shards_of).reshape((-1,) + (1,) * (len(shape) - position - 1))

    loudness = one(*cuts[0])
    for cut in cuts[1:]:
        loudness = loudness * one(*cut)
    return loudness


def bell_draw(key, shape, spread, limit, cuts=(), held_as=jnp.bfloat16):
    entries = jax.random.normal(key, shape, jnp.float32) * spread
    if len(cuts) > 0:
        entries = steps_of(key, shape, cuts, -0.22, 0.18) * entries
    return jnp.clip(entries, min=-limit, max=limit).astype(held_as)


def setup_inputs(seed: int = 0) -> dict:
    key_of = jax.random.split(jax.random.key(seed), 9)
    return {
        "queries": bell_draw(key_of[0], (TOKENS, FHEADS * FD), 1.0, 6.0, ((0, 64), (1, 2))),
        "keys": bell_draw(key_of[1], (TOKENS, FHEADS * FD), 1.0, 6.0, ((0, 64), (1, 2))),
        "values": bell_draw(key_of[2], (TOKENS, FHEADS * FD), 1.0, 6.0, ((0, 64), (1, 2))),
        "rates": jnp.clip(jnp.exp(math.log(0.0027621358) - 2.30258503 * jax.random.uniform(key_of[3], (TOKENS, FHEADS), jnp.float32) ** steps_of(key_of[3], (TOKENS, FHEADS), ((0, 64), (1, 2)), -0.2, 0.2)), 0.0002762136, 0.0027621358),
        "w_up": bell_draw(key_of[4], (FHEADS, FD, FH), FD ** -0.5, 0.1875, ((0, 2),)),
        "w_gate": bell_draw(key_of[5], (FHEADS, FD, FH), FD ** -0.5, 0.1875, ((0, 2),)),
        "w_down": bell_draw(key_of[6], (FHEADS, FH, FD), FH ** -0.5, 0.25, ((0, 2),)),
        "w_out": bell_draw(key_of[7], (FHEADS * FD, D), (FHEADS * FD) ** -0.5, 0.125, ((0, 2),)),
    }


def frob(matrix):
    return jnp.sqrt(jnp.sum(matrix * matrix))

def tdot(left, right):
    return lax.dot_general(left, right, (((0,), (0,)), ((), ())), preferred_element_type=jnp.float32)

def one_head(keys_h, values_h, queries_h, rate, first, third, second):
    sizes = [frob(first), frob(third), frob(second)]
    targets = (rate[:, None] * values_h.astype(jnp.float32)).astype(jnp.bfloat16)
    weights = [first, third, second]
    for step in range(STEPS):
        b_one = weights[0].astype(jnp.bfloat16)
        b_three = weights[1].astype(jnp.bfloat16)
        b_two = weights[2].astype(jnp.bfloat16)
        act = jnp.dot(keys_h, b_one, preferred_element_type=jnp.float32)
        lin = jnp.dot(keys_h, b_three, preferred_element_type=jnp.float32)
        sig = jax.nn.sigmoid(act)
        hidden = (act * sig * lin).astype(jnp.bfloat16)
        err = lax.dot_general(targets, b_two, (((1,), (1,)), ((), ())), preferred_element_type=jnp.float32)
        pgrad = (err * lin * sig * (1.0 + act * (1.0 - sig))).astype(jnp.bfloat16)
        qgrad = (err * act * sig).astype(jnp.bfloat16)
        grads = [tdot(keys_h, pgrad), tdot(keys_h, qgrad), tdot(hidden, targets)]
        updated = []
        for weight, grad, size in zip(weights, grads, sizes):
            moved = weight + grad
            updated.append(moved * size / jnp.sqrt(jnp.sum(moved * moved) + 1e-06))
        weights = updated
    b_one = weights[0].astype(jnp.bfloat16)
    b_three = weights[1].astype(jnp.bfloat16)
    b_two = weights[2].astype(jnp.bfloat16)
    act = jnp.dot(queries_h, b_one, preferred_element_type=jnp.float32)
    lin = jnp.dot(queries_h, b_three, preferred_element_type=jnp.float32)
    hidq = (jax.nn.silu(act) * lin).astype(jnp.bfloat16)
    return jnp.dot(hidq, b_two, preferred_element_type=jnp.float32).astype(jnp.bfloat16)

def reference(queries, keys, values, rates, w_up, w_gate, w_down, w_out):
    pieces = []
    for head in range(FHEADS):
        lo = head * FD
        pieces.append(one_head(keys[:, lo:lo + FD], values[:, lo:lo + FD], queries[:, lo:lo + FD], rates[:, head], w_up[head].astype(jnp.float32), w_gate[head].astype(jnp.float32), w_down[head].astype(jnp.float32)))
    joined = jnp.concatenate(pieces, axis=1)
    return jnp.dot(joined, w_out, preferred_element_type=jnp.float32).astype(jnp.bfloat16)
```

```python
import functools

import jax
import jax.numpy as jnp
from jax import lax
from jax.experimental import pallas as pl
from jax.experimental.pallas import tpu as pltpu
from jax.sharding import Mesh
from jax.sharding import PartitionSpec as P

STEPS = 2
CTX = ("z", "xl", "y", "c")
CHIPS = ("z", "xl", "y")
SWAP = [(0, 1), (1, 0)]
ACROSS = [(0, 3), (3, 0), (1, 2), (2, 1)]
BF = jnp.bfloat16
F32 = jnp.float32
NT = (((1,), (1,)), ((), ()))
TN = (((0,), (0,)), ((), ()))
VMEM = pl.BlockSpec(memory_space=pltpu.VMEM)
SMEM = pl.BlockSpec(memory_space=pltpu.SMEM)
LIMIT = 48 * 1024 * 1024


def dot(x, y):
    return jnp.dot(x, y, preferred_element_type=F32)


def nt(x, y):
    return lax.dot_general(x, y, NT, preferred_element_type=F32)


def tn(x, y):
    return lax.dot_general(x, y, TN, preferred_element_type=F32)


def call(kernel, outs, n_in, flops, nbytes, smem=0, scratch=()):
    return pl.pallas_call(
        kernel,
        out_shape=outs,
        in_specs=[SMEM] * smem + [VMEM] * (n_in - smem),
        out_specs=jax.tree.map(lambda _: VMEM, outs),
        scratch_shapes=list(scratch),
        compiler_params=pltpu.CompilerParams(vmem_limit_bytes=LIMIT),
        cost_estimate=pl.CostEstimate(flops=flops, bytes_accessed=nbytes, transcendentals=0),
    )


def shape(dims, dtype=BF):
    return jax.ShapeDtypeStruct(dims, dtype)


def prepare_kernel(core, up, gate, down, w0, norm):
    width, hid = up.shape
    half = hid // 2
    total = []
    for w in (up, gate, down):
        full = w[...].astype(F32)
        total.append(jnp.sum(full * full))
    for i, value in enumerate(total):
        norm[i : i + 1, :] = jnp.full((1, 128), value, F32)
    norm[3:8, :] = jnp.zeros((5, 128), F32)
    for c in range(2):

        @pl.when(core[0] == c)
        def _():
            w0[0:half, :] = up[:, c * half : (c + 1) * half].T
            w0[half : 2 * half, :] = gate[:, c * half : (c + 1) * half].T
            w0[2 * half :, :] = down[c * half : (c + 1) * half, :]


def act_grads(wb, keys, targets, half):
    act = nt(wb[0:half, :], keys)
    lin = nt(wb[half : 2 * half, :], keys)
    err = nt(wb[2 * half :, :], targets)
    sig = jax.nn.sigmoid(act)
    silu = act * sig
    hidden = (silu * lin).astype(BF)
    pgrad = (err * lin * sig * (1.0 + act * (1.0 - sig))).astype(BF)
    qgrad = (err * silu).astype(BF)
    return pgrad, qgrad, hidden


def grads_into(out, wb, k_own, k_oth, u_own, u_oth):
    half = wb.shape[0] // 3
    width = wb.shape[1]
    cols = width // 2
    own = act_grads(wb, k_own[...], u_own[...], half)
    oth = act_grads(wb, k_oth[...], u_oth[...], half)
    for i in range(3):
        x, y = (k_own, k_oth) if i < 2 else (u_own, u_oth)
        for j in range(2):
            at = slice(j * cols, (j + 1) * cols)
            g = dot(own[i], x[:, at]) + dot(oth[i], y[:, at])
            out[j, i * half : (i + 1) * half, :] = g.astype(BF)


def first_kernel(w0, k_own, k_oth, u_own, u_oth, out):
    grads_into(out, w0, k_own, k_oth, u_own, u_oth)


def update_kernel(w, gathered, moved, squares):
    third = w.shape[0] // 3
    cols = w.shape[1] // 2
    for i in range(3):
        rows = slice(i * third, (i + 1) * third)
        total = jnp.zeros((), F32)
        for j in range(2):
            at = slice(j * cols, (j + 1) * cols)
            m = w[rows, at].astype(F32) + gathered[j, rows, :].astype(F32)
            moved[rows, at] = m
            total = total + jnp.sum(m * m)
        squares[i : i + 1, :] = jnp.full((1, 128), total, F32)
    squares[3:8, :] = jnp.zeros((5, 128), F32)


def scaled(i, moved, norm, own, oth):
    third = moved.shape[0] // 3
    size = jnp.sqrt(norm[i : i + 1, 0:1])
    total = own[i : i + 1, 0:1] + oth[i : i + 1, 0:1]
    return moved[i * third : (i + 1) * third, :] * size / jnp.sqrt(total + 1e-06)


def next_kernel(moved, norm, sq_own, sq_oth, k_own, k_oth, u_own, u_oth, out, w, wb):
    third = moved.shape[0] // 3
    for i in range(3):
        new = scaled(i, moved, norm, sq_own, sq_oth)
        w[i * third : (i + 1) * third, :] = new
        wb[i * third : (i + 1) * third, :] = new.astype(BF)
    grads_into(out, wb, k_own, k_oth, u_own, u_oth)


def hidden_kernel(moved, norm, sq_own, sq_oth, q_own, q_oth, w2, hq_own, hq_oth):
    b1 = scaled(0, moved, norm, sq_own, sq_oth).astype(BF)
    b3 = scaled(1, moved, norm, sq_own, sq_oth).astype(BF)
    w2[...] = scaled(2, moved, norm, sq_own, sq_oth).astype(BF)
    for q, out in ((q_oth, hq_oth), (q_own, hq_own)):
        act = nt(b1, q[...])
        lin = nt(b3, q[...])
        out[...] = (jax.nn.silu(act) * lin).astype(BF)


def piece_kernel(hq_own, hq_got, w2_own, w2_got, o):
    o[...] = (tn(hq_own[...], w2_own[...]) + tn(hq_got[...], w2_got[...])).astype(BF)


def spread_kernel(arrived, out):
    total = arrived[0].astype(F32)
    for i in range(1, arrived.shape[0]):
        total = total + arrived[i].astype(F32)
    rounded = total.astype(BF)
    for i in range(arrived.shape[0]):
        out[i] = rounded


def out_kernel(place, o, w_own, o_first, o_second, w_first, w_second, out):
    total = dot(o[...], w_own[...]) + dot(o_first[...], w_first[...])
    out[...] = (total + dot(o_second[...], w_second[...])).astype(BF)


def last_product(place, o, w_out, o_got, w_first, w_second):
    tokens, width = o.shape
    n = w_first.shape[1]
    tile = 512
    steps = n // tile
    return pl.pallas_call(
        out_kernel,
        out_shape=shape((tokens, n)),
        grid_spec=pltpu.PrefetchScalarGridSpec(
            num_scalar_prefetch=1,
            grid=(steps,),
            in_specs=[
                pl.BlockSpec((tokens, width), lambda i, s: (0, 0)),
                pl.BlockSpec((width, tile), lambda i, s: (0, s[0] * steps + i)),
                pl.BlockSpec((tokens, width // 2), lambda i, s: (0, s[1])),
                pl.BlockSpec((tokens, width // 2), lambda i, s: (0, 1 - s[1])),
                pl.BlockSpec((width // 2, tile), lambda i, s: (0, i)),
                pl.BlockSpec((width // 2, tile), lambda i, s: (0, i)),
            ],
            out_specs=pl.BlockSpec((tokens, tile), lambda i, s: (0, i)),
        ),
        compiler_params=pltpu.CompilerParams(vmem_limit_bytes=LIMIT),
        cost_estimate=pl.CostEstimate(
            flops=4 * tokens * width * n, bytes_accessed=16 << 20, transcendentals=0
        ),
    )(place, o, w_out, o_got, o_got, w_first, w_second)


def all_reduced(grads):
    peers = lax.axis_size(CHIPS)
    pieces = grads.reshape(peers, -1, grads.shape[2])
    arrived = lax.all_to_all(pieces, CHIPS, 0, 0, tiled=True)
    copies = call(spread_kernel, shape(pieces.shape), 1, pieces.size, 4 * pieces.size)(arrived)
    gathered = lax.all_to_all(copies, CHIPS, 0, 0, tiled=True)
    return gathered.reshape(grads.shape)


def swap(x):
    return lax.ppermute(x, "c", SWAP)


def shards(queries, keys, values, rates, w_up, w_gate, w_down, w_out):
    width, hid = w_up.shape[1:]
    tokens = keys.shape[0]
    half, third = hid // 2, 3 * hid // 2
    core, head = lax.axis_index("c"), lax.axis_index("h")
    n = w_out.shape[1] // 2

    k_oth = swap(keys)
    targets = (rates * values.astype(F32)).astype(BF)
    u_oth = swap(targets)
    kus = (keys, k_oth, targets, u_oth)

    place = jnp.stack([head, core]).astype(jnp.int32)
    sent = lax.dynamic_slice(w_out, (core * (width // 2), (1 - head) * n), (width // 2, n))
    w_first = lax.ppermute(sent, ("xl", "h"), ACROSS)
    w_second = swap(w_first)
    q_oth = swap(queries)

    w0, norm = call(
        prepare_kernel, (shape((third, width)), shape((8, 128), F32)), 4, 1 << 21, 5 << 20, smem=1
    )(core.reshape(1).astype(jnp.int32), w_up[0], w_gate[0], w_down[0])
    flops = 12 * 2 * tokens * width * half
    gshape = shape((2, third, width // 2))
    grads = call(first_kernel, gshape, 5, flops, 8 << 20)(w0, *kus)
    w = w0
    for step in range(STEPS):
        gathered = all_reduced(grads)
        moved, squares = call(
            update_kernel, (shape((third, width), F32), shape((8, 128), F32)), 2, 1 << 22, 8 << 20
        )(w, gathered)
        state = (moved, norm, squares, swap(squares))
        if step < STEPS - 1:
            grads, w = call(
                next_kernel,
                (gshape, shape((third, width), F32)),
                8,
                flops,
                14 << 20,
                scratch=[pltpu.VMEM((third, width), BF)],
            )(*state, *kus)
    w2, hq_own, hq_oth = call(
        hidden_kernel,
        (shape((half, width)), shape((half, tokens)), shape((half, tokens))),
        6,
        flops // 3,
        8 << 20,
    )(*state, queries, q_oth)
    o = call(piece_kernel, shape((tokens, width)), 4, 2 * tokens * hid * width, 4 << 20)(
        hq_own, swap(hq_oth), w2, swap(w2)
    )
    o_got = lax.ppermute(o, "h", SWAP)
    return last_product(place, o, w_out, o_got, w_first, w_second)


def solution(mesh):
    finer = Mesh(
        mesh.devices.reshape(4, 2, 4, 2, mesh.shape["head"]),
        ("z", "xl", "y", "c", "h"),
    )
    return jax.shard_map(
        shards,
        mesh=finer,
        in_specs=(
            P(CTX, "h"),
            P(CTX, "h"),
            P(CTX, "h"),
            P(CTX, "h"),
            P("h", None, None),
            P("h", None, None),
            P("h", None, None),
            P("h", None),
        ),
        out_specs=P(CTX, "h"),
        check_vma=False,
    )
```

```python
import functools

import jax
import jax.numpy as jnp
from jax import lax
from jax.experimental import pallas as pl
from jax.experimental.pallas import tpu as pltpu
from jax.sharding import Mesh
from jax.sharding import PartitionSpec as P

STEPS = 2
CTX = ("z", "xl", "y", "c")
CHIPS = ("z", "xl", "y")
SWAP = [(0, 1), (1, 0)]
ACROSS = [(0, 3), (3, 0), (1, 2), (2, 1)]
BF = jnp.bfloat16
F32 = jnp.float32
NT = (((1,), (1,)), ((), ()))
TN = (((0,), (0,)), ((), ()))
VMEM = pl.BlockSpec(memory_space=pltpu.VMEM)
SMEM = pl.BlockSpec(memory_space=pltpu.SMEM)
LIMIT = 24 * 1024 * 1024
CHUNKS = 2


def dot(x, y):
    return jnp.dot(x, y, preferred_element_type=F32)


def nt(x, y):
    return lax.dot_general(x, y, NT, preferred_element_type=F32)


def tn(x, y):
    return lax.dot_general(x, y, TN, preferred_element_type=F32)


def call(kernel, outs, n_in, flops, nbytes, smem=0, scratch=()):
    return pl.pallas_call(
        kernel,
        out_shape=outs,
        in_specs=[SMEM] * smem + [VMEM] * (n_in - smem),
        out_specs=jax.tree.map(lambda _: VMEM, outs),
        scratch_shapes=list(scratch),
        compiler_params=pltpu.CompilerParams(vmem_limit_bytes=LIMIT),
        cost_estimate=pl.CostEstimate(flops=flops, bytes_accessed=nbytes, transcendentals=0),
    )


def shape(dims, dtype=BF):
    return jax.ShapeDtypeStruct(dims, dtype)


def prepare_kernel(core, up, gate, down, w0, norm):
    width, hid = up.shape
    half = hid // 2
    total = []
    for w in (up, gate, down):
        full = w[...].astype(F32)
        total.append(jnp.sum(full * full))
    for i, value in enumerate(total):
        norm[i : i + 1, :] = jnp.full((1, 128), value, F32)
    norm[3:8, :] = jnp.zeros((5, 128), F32)
    for c in range(2):

        @pl.when(core[0] == c)
        def _():
            w0[0:half, :] = up[:, c * half : (c + 1) * half].T
            w0[half : 2 * half, :] = gate[:, c * half : (c + 1) * half].T
            w0[2 * half :, :] = down[c * half : (c + 1) * half, :]


def act_grads(wb, keys, targets):
    half = wb.shape[0] // 3
    act = nt(wb[0:half, :], keys)
    lin = nt(wb[half : 2 * half, :], keys)
    err = nt(wb[2 * half :, :], targets)
    sig = jax.nn.sigmoid(act)
    silu = act * sig
    hidden = (silu * lin).astype(BF)
    pgrad = (err * lin * sig * (1.0 + act * (1.0 - sig))).astype(BF)
    qgrad = (err * silu).astype(BF)
    return pgrad, qgrad, hidden


def sums_into(out, own, oth, k_own, k_oth, u_own, u_oth):
    cols = k_own.shape[1] // 2
    half = own[0].shape[0]
    for i in range(3):
        x, y = (k_own, k_oth) if i < 2 else (u_own, u_oth)
        for j in range(2):
            at = slice(j * cols, (j + 1) * cols)
            g = dot(own[i], x[:, at]) + dot(oth[i], y[:, at])
            out[j, i * half : (i + 1) * half, :] = g.astype(BF)


def own_kernel(w0, k_own, u_own, acts):
    half = w0.shape[0] // 3
    for i, x in enumerate(act_grads(w0, k_own[...], u_own[...])):
        acts[i * half : (i + 1) * half, :] = x


def first_kernel(w0, acts, k_own, k_oth, u_own, u_oth, out):
    half = w0.shape[0] // 3
    own = [acts[i * half : (i + 1) * half, :] for i in range(3)]
    oth = act_grads(w0, k_oth[...], u_oth[...])
    sums_into(out, own, oth, k_own, k_oth, u_own, u_oth)


def moved_into(moved, squares, weight, gathered):
    third = moved.shape[0] // 3
    cols = moved.shape[1] // 2
    for i in range(3):
        rows = slice(i * third, (i + 1) * third)
        total = jnp.zeros((), F32)
        for j in range(2):
            at = slice(j * cols, (j + 1) * cols)
            m = weight(i, rows, at) + gathered[j, rows, :].astype(F32)
            moved[rows, at] = m
            total = total + jnp.sum(m * m)
        squares[i : i + 1, :] = jnp.full((1, 128), total, F32)
    squares[3:8, :] = jnp.zeros((5, 128), F32)


def update_kernel(w, gathered, moved, squares):
    moved_into(moved, squares, lambda i, rows, at: w[rows, at].astype(F32), gathered)


def update_again_kernel(before, norm, sq_own, sq_oth, gathered, moved, squares):
    moved_into(
        moved,
        squares,
        lambda i, rows, at: before[rows, at] * factor(i, norm, sq_own, sq_oth),
        gathered,
    )


def factor(i, norm, own, oth):
    size = jnp.sqrt(norm[i : i + 1, 0:1])
    total = own[i : i + 1, 0:1] + oth[i : i + 1, 0:1]
    return size / jnp.sqrt(total + 1e-06)


def scaled(i, moved, norm, own, oth):
    third = moved.shape[0] // 3
    new = moved[i * third : (i + 1) * third, :] * factor(i, norm, own, oth)
    return new.astype(BF)


def next_kernel(moved, norm, sq_own, sq_oth, k_own, k_oth, u_own, u_oth, out, wb):
    third = moved.shape[0] // 3
    for i in range(3):
        wb[i * third : (i + 1) * third, :] = scaled(i, moved, norm, sq_own, sq_oth)
    own = act_grads(wb, k_own[...], u_own[...])
    oth = act_grads(wb, k_oth[...], u_oth[...])
    sums_into(out, own, oth, k_own, k_oth, u_own, u_oth)


def hidden_of(b1, b3, q):
    return (jax.nn.silu(nt(b1, q)) * nt(b3, q)).astype(BF)


def hidden_kernel(moved, norm, sq_own, sq_oth, q_oth, w2, hq_oth, b13):
    half = w2.shape[0]
    w2[...] = scaled(2, moved, norm, sq_own, sq_oth)
    b1 = scaled(0, moved, norm, sq_own, sq_oth)
    b3 = scaled(1, moved, norm, sq_own, sq_oth)
    b13[0:half, :] = b1
    b13[half:, :] = b3
    hq_oth[...] = hidden_of(b1, b3, q_oth[...])


def hidden_own_kernel(b13, q_own, hq_own):
    half = b13.shape[0] // 2
    hq_own[...] = hidden_of(b13[0:half, :], b13[half:, :], q_own[...])


def piece_kernel(hq_own, hq_got, w2_own, w2_got, *pieces):
    count = pieces[0].shape[0]
    for k, o in enumerate(pieces):
        at = slice(k * count, (k + 1) * count)
        o[...] = (tn(hq_own[:, at], w2_own[...]) + tn(hq_got[:, at], w2_got[...])).astype(BF)


def spread_kernel(arrived, out):
    total = arrived[0].astype(F32)
    for i in range(1, arrived.shape[0]):
        total = total + arrived[i].astype(F32)
    rounded = total.astype(BF)
    for i in range(arrived.shape[0]):
        out[i] = rounded


TILE = 512


def partial_kernel(place, *refs):
    *pieces, w_own, out = refs
    count = pieces[0].shape[0]
    for k, o in enumerate(pieces):
        out[k * count : (k + 1) * count, :] = dot(o[...], w_own[...])


def partial_product(place, pieces, w_out):
    count, width = pieces[0].shape
    n = w_out.shape[1] // 2
    steps = n // TILE
    tokens = count * len(pieces)
    return pl.pallas_call(
        partial_kernel,
        out_shape=shape((tokens, n), F32),
        grid_spec=pltpu.PrefetchScalarGridSpec(
            num_scalar_prefetch=1,
            grid=(steps,),
            in_specs=[pl.BlockSpec((count, width), lambda i, s: (0, 0))] * len(pieces)
            + [pl.BlockSpec((width, TILE), lambda i, s: (0, s[0] * steps + i))],
            out_specs=pl.BlockSpec((tokens, TILE), lambda i, s: (0, i)),
        ),
        compiler_params=pltpu.CompilerParams(vmem_limit_bytes=LIMIT),
        cost_estimate=pl.CostEstimate(
            flops=2 * tokens * width * n, bytes_accessed=10 << 20, transcendentals=0
        ),
    )(place, *pieces, w_out)


def finish_kernel(place, part, o_first, o_second, w_first, w_second, *rest):
    out = rest[-1]
    total = part[...] + dot(o_first[...], w_first[...]) + dot(o_second[...], w_second[...])
    out[...] = total.astype(BF)


def finish_product(place, k, part, o_got, w_first, w_second, out):
    count, width = o_got.shape
    tokens, n = part.shape
    args = (place, part, o_got, o_got, w_first, w_second)
    return pl.pallas_call(
        finish_kernel,
        out_shape=shape((tokens, n)),
        grid_spec=pltpu.PrefetchScalarGridSpec(
            num_scalar_prefetch=1,
            grid=(n // TILE,),
            in_specs=[
                pl.BlockSpec((count, TILE), lambda i, s: (k, i)),
                pl.BlockSpec((count, width // 2), lambda i, s: (0, s[1])),
                pl.BlockSpec((count, width // 2), lambda i, s: (0, 1 - s[1])),
                pl.BlockSpec((width // 2, TILE), lambda i, s: (0, i)),
                pl.BlockSpec((width // 2, TILE), lambda i, s: (0, i)),
            ]
            + [pl.BlockSpec(memory_space=pl.ANY)] * (out is not None),
            out_specs=pl.BlockSpec((count, TILE), lambda i, s: (k, i)),
        ),
        input_output_aliases={} if out is None else {len(args): 0},
        compiler_params=pltpu.CompilerParams(vmem_limit_bytes=LIMIT),
        cost_estimate=pl.CostEstimate(
            flops=2 * count * width * n, bytes_accessed=10 << 20, transcendentals=0
        ),
    )(*args, *(() if out is None else (out,)))


def all_reduced(grads):
    peers = lax.axis_size(CHIPS)
    pieces = grads.reshape(peers, -1, grads.shape[2])
    arrived = lax.all_to_all(pieces, CHIPS, 0, 0, tiled=True)
    copies = call(spread_kernel, shape(pieces.shape), 1, pieces.size, 4 * pieces.size)(arrived)
    gathered = lax.all_to_all(copies, CHIPS, 0, 0, tiled=True)
    return gathered.reshape(grads.shape)


def swap(x):
    return lax.ppermute(x, "c", SWAP)


def shards(queries, keys, values, rates, w_up, w_gate, w_down, w_out):
    width, hid = w_up.shape[1:]
    tokens = keys.shape[0]
    half, third = hid // 2, 3 * hid // 2
    core, head = lax.axis_index("c"), lax.axis_index("h")
    n = w_out.shape[1] // 2

    k_oth = swap(keys)
    targets = (rates * values.astype(F32)).astype(BF)
    u_oth = swap(targets)
    kus = (keys, k_oth, targets, u_oth)

    place = jnp.stack([head, core]).astype(jnp.int32)
    sent = lax.dynamic_slice(w_out, (core * (width // 2), (1 - head) * n), (width // 2, n))
    w_first = lax.ppermute(sent, ("xl", "h"), ACROSS)
    w_second = swap(w_first)
    q_oth = swap(queries)

    w0, norm = call(
        prepare_kernel, (shape((third, width)), shape((8, 128), F32)), 4, 1 << 21, 5 << 20, smem=1
    )(core.reshape(1).astype(jnp.int32), w_up[0], w_gate[0], w_down[0])
    flops = 12 * 2 * tokens * width * half
    gshape = shape((2, third, width // 2))
    mshape = (shape((third, width), F32), shape((8, 128), F32))
    acts = call(own_kernel, shape((third, tokens)), 3, flops // 4, 4 << 20)(w0, keys, targets)
    grads = call(first_kernel, gshape, 6, flops * 3 // 4, 8 << 20)(w0, acts, *kus)
    state = None
    for step in range(STEPS):
        gathered = all_reduced(grads)
        if step == 0:
            moved, squares = call(update_kernel, mshape, 2, 1 << 22, 8 << 20)(w0, gathered)
        else:
            moved, squares = call(update_again_kernel, mshape, 5, 1 << 22, 8 << 20)(
                *state, gathered
            )
        state = (moved, norm, squares, swap(squares))
        if step < STEPS - 1:
            grads = call(
                next_kernel, gshape, 8, flops, 14 << 20, scratch=[pltpu.VMEM((third, width), BF)]
            )(*state, *kus)
    hshape = shape((half, tokens))
    w2, hq_oth, b13 = call(
        hidden_kernel,
        (shape((half, width)), hshape, shape((2 * half, width))),
        5,
        flops // 6,
        8 << 20,
    )(*state, q_oth)
    hq_got, w2_got = swap(hq_oth), swap(w2)
    hq_own = call(hidden_own_kernel, hshape, 2, flops // 6, 3 << 20)(b13, queries)
    pieces = call(
        piece_kernel,
        (shape((tokens // CHUNKS, width)),) * CHUNKS,
        4,
        2 * tokens * hid * width,
        4 << 20,
    )(hq_own, hq_got, w2, w2_got)
    pieces_got = [lax.ppermute(o, "h", SWAP) for o in pieces]
    part = partial_product(place, pieces, w_out)
    out = None
    for k, o_got in enumerate(pieces_got):
        out = finish_product(place, k, part, o_got, w_first, w_second, out)
    return out


def solution(mesh):
    finer = Mesh(
        mesh.devices.reshape(4, 2, 4, 2, mesh.shape["head"]),
        ("z", "xl", "y", "c", "h"),
    )
    return jax.shard_map(
        shards,
        mesh=finer,
        in_specs=(
            P(CTX, "h"),
            P(CTX, "h"),
            P(CTX, "h"),
            P(CTX, "h"),
            P("h", None, None),
            P("h", None, None),
            P("h", None, None),
            P("h", None),
        ),
        out_specs=P(CTX, "h"),
        check_vma=False,
    )
```

```python
import functools

import jax
import jax.numpy as jnp
from jax import lax
from jax.experimental import pallas as pl
from jax.experimental.pallas import tpu as pltpu
from jax.sharding import Mesh
from jax.sharding import PartitionSpec as P

STEPS = 2
CTX = ("z", "xl", "y", "c")
CHIPS = ("z", "xl", "y")
SWAP = [(0, 1), (1, 0)]
ACROSS = [(0, 3), (3, 0), (1, 2), (2, 1)]
BF = jnp.bfloat16
F32 = jnp.float32
NT = (((1,), (1,)), ((), ()))
TN = (((0,), (0,)), ((), ()))
VMEM = pl.BlockSpec(memory_space=pltpu.VMEM)
SMEM = pl.BlockSpec(memory_space=pltpu.SMEM)
LIMIT = 24 * 1024 * 1024
CHUNKS = 2


def dot(x, y):
    return jnp.dot(x, y, preferred_element_type=F32)


def nt(x, y):
    return lax.dot_general(x, y, NT, preferred_element_type=F32)


def tn(x, y):
    return lax.dot_general(x, y, TN, preferred_element_type=F32)


def call(kernel, outs, n_in, flops, nbytes, smem=0, scratch=()):
    return pl.pallas_call(
        kernel,
        out_shape=outs,
        in_specs=[SMEM] * smem + [VMEM] * (n_in - smem),
        out_specs=jax.tree.map(lambda _: VMEM, outs),
        scratch_shapes=list(scratch),
        compiler_params=pltpu.CompilerParams(vmem_limit_bytes=LIMIT),
        cost_estimate=pl.CostEstimate(flops=flops, bytes_accessed=nbytes, transcendentals=0),
    )


def shape(dims, dtype=BF):
    return jax.ShapeDtypeStruct(dims, dtype)


def prepare_kernel(core, up, gate, down, w13, w2, norm):
    half = w2.shape[0]
    for i, w in enumerate((up, gate, down)):
        full = w[...].astype(F32)
        norm[i : i + 1, :] = jnp.full((1, 128), jnp.sum(full * full), F32)
    norm[3:8, :] = jnp.zeros((5, 128), F32)
    for c in range(2):

        @pl.when(core[0] == c)
        def _():
            w13[0:half, :] = up[:, c * half : (c + 1) * half].T
            w13[half:, :] = gate[:, c * half : (c + 1) * half].T
            w2[...] = down[c * half : (c + 1) * half, :]


def factor(i, norm, own, oth):
    size = jnp.sqrt(norm[i : i + 1, 0:1])
    total = own[i : i + 1, 0:1] + oth[i : i + 1, 0:1]
    return size / jnp.sqrt(total + 1e-06)


def raw_kernel(w13, w2, keys, targets, raw):
    raw[0 : w13.shape[0], :] = nt(w13[...], keys[...])
    raw[w13.shape[0] :, :] = nt(w2[...], targets[...])


def act_grads(act, lin, err, scale):
    if scale is not None:
        act, lin, err = (x * f for x, f in zip((act, lin, err), scale))
    sig = jax.nn.sigmoid(act)
    silu = act * sig
    hidden = (silu * lin).astype(BF)
    pgrad = (err * lin * sig * (1.0 + act * (1.0 - sig))).astype(BF)
    qgrad = (err * silu).astype(BF)
    return pgrad, qgrad, hidden


def grads_kernel(w13, w2, raw, k_own, k_oth, u_own, u_oth, *rest):
    *state, out = rest
    half = w2.shape[0]
    cols = k_own.shape[1] // 2
    scale = [factor(i, *state) for i in (0, 1, 2)] if state else None
    keys, targets = k_oth[...], u_oth[...]
    oth = act_grads(
        nt(w13[0:half, :], keys), nt(w13[half:, :], keys), nt(w2[...], targets), scale
    )
    own = act_grads(raw[0:half, :], raw[half : 2 * half, :], raw[2 * half :, :], scale)
    for i in range(3):
        x, y = (k_own, k_oth) if i < 2 else (u_own, u_oth)
        for j in range(2):
            at = slice(j * cols, (j + 1) * cols)
            g = dot(own[i], x[:, at]) + dot(oth[i], y[:, at])
            out[j, i * half : (i + 1) * half, :] = g.astype(BF)


ROWS = 16


def update_kernel(w13, w2, gathered, *rest):
    *again, m13, m2, squares = rest
    half = w2.shape[0]
    cols = w2.shape[1] // 2
    for i in range(3):
        src, dst = (w13, m13) if i < 2 else (w2, m2)
        base = (i % 2) * half
        if again:
            scale = jnp.broadcast_to(factor(i, *again[:3]), (ROWS, cols))

        def step(r, total):
            row = pl.multiple_of(base + r * ROWS, ROWS)
            at = pl.multiple_of(i * half + r * ROWS, ROWS)
            for j in range(2):
                side = slice(j * cols, (j + 1) * cols)
                m = src[pl.ds(row, ROWS), side].astype(F32)
                m = m + gathered[j, pl.ds(at, ROWS), :].astype(F32)
                if again:
                    m = m * scale + again[3][j, pl.ds(at, ROWS), :].astype(F32)
                dst[pl.ds(row, ROWS), side] = m.astype(BF)
                total = total + m * m
            return total

        total = lax.fori_loop(0, half // ROWS, step, jnp.zeros((ROWS, cols), F32))
        squares[i : i + 1, :] = jnp.full((1, 128), jnp.sum(total), F32)
    squares[3:8, :] = jnp.zeros((5, 128), F32)


def query_kernel(m13, q_oth, q_own, raw):
    raw[0] = nt(m13[...], q_oth[...])
    raw[1] = nt(m13[...], q_own[...])


def hidden_kernel(k, raw, norm, sq_own, sq_oth, hq):
    half = hq.shape[0]
    act = raw[k, 0:half, :] * factor(0, norm, sq_own, sq_oth)
    lin = raw[k, half:, :] * factor(1, norm, sq_own, sq_oth)
    hq[...] = (jax.nn.silu(act) * lin).astype(BF)


def piece_kernel(hq_own, hq_got, w2_own, w2_got, norm, sq_own, sq_oth, *pieces):
    count = pieces[0].shape[0]
    scale = factor(2, norm, sq_own, sq_oth)
    for k, o in enumerate(pieces):
        at = slice(k * count, (k + 1) * count)
        total = tn(hq_own[:, at], w2_own[...]) + tn(hq_got[:, at], w2_got[...])
        o[...] = (total * scale).astype(BF)


def spread_kernel(arrived, out):
    total = arrived[0].astype(F32)
    for i in range(1, arrived.shape[0]):
        total = total + arrived[i].astype(F32)
    rounded = total.astype(BF)
    for i in range(arrived.shape[0]):
        out[i] = rounded


TILE = 512


def partial_kernel(place, *refs):
    *pieces, w_own, out = refs
    count = pieces[0].shape[0]
    for k, o in enumerate(pieces):
        out[k * count : (k + 1) * count, :] = dot(o[...], w_own[...])


def partial_product(place, pieces, w_out):
    count, width = pieces[0].shape
    n = w_out.shape[1] // 2
    steps = n // TILE
    tokens = count * len(pieces)
    return pl.pallas_call(
        partial_kernel,
        out_shape=shape((tokens, n), F32),
        grid_spec=pltpu.PrefetchScalarGridSpec(
            num_scalar_prefetch=1,
            grid=(steps,),
            in_specs=[pl.BlockSpec((count, width), lambda i, s: (0, 0))] * len(pieces)
            + [pl.BlockSpec((width, TILE), lambda i, s: (0, s[0] * steps + i))],
            out_specs=pl.BlockSpec((tokens, TILE), lambda i, s: (0, i)),
        ),
        compiler_params=pltpu.CompilerParams(vmem_limit_bytes=LIMIT),
        cost_estimate=pl.CostEstimate(
            flops=2 * tokens * width * n, bytes_accessed=10 << 20, transcendentals=0
        ),
    )(place, *pieces, w_out)


def finish_kernel(k, place, part, o_got, w_first, w_second, *rest):
    *_, out, held, sems = rest
    count, width = o_got.shape
    half = width // 2
    rows = slice(k * count, (k + 1) * count)
    o_first = o_got[:, pl.ds(pl.multiple_of(place[1] * half, 128), half)]
    o_second = o_got[:, pl.ds(pl.multiple_of((1 - place[1]) * half, 128), half)]
    copies = []
    for j in range(part.shape[1] // TILE):
        at = slice(j * TILE, (j + 1) * TILE)
        total = part[rows, at] + dot(o_first, w_first[:, at]) + dot(o_second, w_second[:, at])
        held[j] = total.astype(BF)
        copies.append(pltpu.make_async_copy(held.at[j], out.at[rows, at], sems.at[j]))
        copies[-1].start()
    for copy in copies:
        copy.wait()


def finish_product(place, k, part, o_got, w_first, w_second, out):
    count, width = o_got.shape
    tokens, n = part.shape
    near = [pltpu.with_memory_space_constraint(x, pltpu.VMEM) for x in (part, o_got, w_first, w_second)]
    args = (place, *near)
    return pl.pallas_call(
        functools.partial(finish_kernel, k),
        out_shape=shape((tokens, n)),
        in_specs=[SMEM] + [VMEM] * 4 + [pl.BlockSpec(memory_space=pl.ANY)] * (out is not None),
        out_specs=pl.BlockSpec(memory_space=pl.ANY),
        scratch_shapes=[
            pltpu.VMEM((n // TILE, count, TILE), BF),
            pltpu.SemaphoreType.DMA((n // TILE,)),
        ],
        input_output_aliases={} if out is None else {len(args): 0},
        compiler_params=pltpu.CompilerParams(vmem_limit_bytes=LIMIT),
        cost_estimate=pl.CostEstimate(
            flops=2 * count * width * n, bytes_accessed=4 << 20, transcendentals=0
        ),
    )(*args, *(() if out is None else (out,)))


def all_reduced(grads):
    peers = lax.axis_size(CHIPS)
    pieces = grads.reshape(peers, -1, grads.shape[2])
    arrived = lax.all_to_all(pieces, CHIPS, 0, 0, tiled=True)
    copies = call(spread_kernel, shape(pieces.shape), 1, pieces.size, 4 * pieces.size)(arrived)
    gathered = lax.all_to_all(copies, CHIPS, 0, 0, tiled=True)
    return gathered.reshape(grads.shape)


def swap(x):
    return lax.ppermute(x, "c", SWAP)


def shards(queries, keys, values, rates, w_up, w_gate, w_down, w_out):
    width, hid = w_up.shape[1:]
    tokens = keys.shape[0]
    half, third = hid // 2, 3 * hid // 2
    core, head = lax.axis_index("c"), lax.axis_index("h")
    n = w_out.shape[1] // 2

    k_oth = swap(keys)
    targets = (rates * values.astype(F32)).astype(BF)
    u_oth = swap(targets)
    kus = (keys, k_oth, targets, u_oth)

    place = jnp.stack([head, core]).astype(jnp.int32)
    sent = lax.dynamic_slice(w_out, (core * (width // 2), (1 - head) * n), (width // 2, n))
    w_first = lax.ppermute(sent, ("xl", "h"), ACROSS)
    w_second = swap(w_first)
    q_oth = swap(queries)

    wshape = (shape((2 * half, width)), shape((half, width)))
    sshape = shape((8, 128), F32)
    *w, norm = call(prepare_kernel, (*wshape, sshape), 4, 1 << 21, 5 << 20, smem=1)(
        core.reshape(1).astype(jnp.int32), w_up[0], w_gate[0], w_down[0]
    )
    flops = 12 * 2 * tokens * width * half
    state, mats, again = (), w, ()
    for step in range(STEPS):
        raw = call(raw_kernel, shape((third, tokens), F32), 4, flops // 4, 4 << 20)(
            *mats, keys, targets
        )
        grads = call(
            grads_kernel,
            shape((2, third, width // 2)),
            7 + len(state),
            flops * 3 // 4,
            8 << 20,
        )(*mats, raw, keys, k_oth, targets, u_oth, *state)
        gathered = all_reduced(grads)
        first = gathered if step == 0 else first
        again = () if step == 0 else (*state, gathered)
        *mats, squares = call(
            update_kernel, (*wshape, sshape), 3 + len(again), 1 << 22, 5 << 20
        )(*w, first, *again)
        state = (norm, squares, swap(squares))
    w2_got = swap(mats[1])
    hshape = shape((half, tokens))
    raw = call(query_kernel, shape((2, 2 * half, tokens), F32), 3, flops // 3, 5 << 20)(
        mats[0], q_oth, queries
    )
    hq_oth, hq_own = (
        call(functools.partial(hidden_kernel, k), hshape, 4, 1 << 20, 2 << 20)(raw, *state)
        for k in range(2)
    )
    pieces = call(
        piece_kernel,
        (shape((tokens // CHUNKS, width)),) * CHUNKS,
        7,
        2 * tokens * hid * width,
        4 << 20,
    )(hq_own, swap(hq_oth), mats[1], w2_got, *state)
    pieces_got = [lax.ppermute(o, "h", SWAP) for o in pieces]
    part = partial_product(place, pieces, w_out)
    out = None
    for k, o_got in enumerate(pieces_got):
        out = finish_product(place, k, part, o_got, w_first, w_second, out)
    return out


def solution(mesh):
    finer = Mesh(
        mesh.devices.reshape(4, 2, 4, 2, mesh.shape["head"]),
        ("z", "xl", "y", "c", "h"),
    )
    return jax.shard_map(
        shards,
        mesh=finer,
        in_specs=(
            P(CTX, "h"),
            P(CTX, "h"),
            P(CTX, "h"),
            P(CTX, "h"),
            P("h", None, None),
            P("h", None, None),
            P("h", None, None),
            P("h", None),
        ),
        out_specs=P(CTX, "h"),
        check_vma=False,
    )
```

```python
import functools

import jax
import jax.numpy as jnp
from jax import lax
from jax.experimental import pallas as pl
from jax.experimental.pallas import tpu as pltpu
from jax.sharding import Mesh
from jax.sharding import PartitionSpec as P

STEPS = 2
CTX = ("z", "xl", "y", "c")
CHIPS = ("z", "xl", "y")
SWAP = [(0, 1), (1, 0)]
ACROSS = [(0, 3), (3, 0), (1, 2), (2, 1)]
BF = jnp.bfloat16
F32 = jnp.float32
NT = (((1,), (1,)), ((), ()))
TN = (((0,), (0,)), ((), ()))
VMEM = pl.BlockSpec(memory_space=pltpu.VMEM)
SMEM = pl.BlockSpec(memory_space=pltpu.SMEM)
FAR = pl.BlockSpec(memory_space=pltpu.HBM)
ANY = pl.BlockSpec(memory_space=pl.ANY)
LIMIT = 24 * 1024 * 1024
CHUNKS = 2


def dot(x, y):
    return jnp.dot(x, y, preferred_element_type=F32)


def nt(x, y):
    return lax.dot_general(x, y, NT, preferred_element_type=F32)


def tn(x, y):
    return lax.dot_general(x, y, TN, preferred_element_type=F32)


def call(kernel, outs, specs, flops, nbytes, scratch=(), far=False):
    if far:
        outs = jax.tree.map(lambda x: pltpu.HBM(x.shape, x.dtype), outs)
    run = pl.pallas_call(
        kernel,
        out_shape=outs,
        in_specs=specs,
        out_specs=jax.tree.map(lambda _: FAR if far else VMEM, outs),
        scratch_shapes=list(scratch),
        compiler_params=pltpu.CompilerParams(vmem_limit_bytes=LIMIT),
        cost_estimate=pl.CostEstimate(flops=flops, bytes_accessed=nbytes, transcendentals=0),
    )

    def with_places(*args):
        return run(
            *(
                pltpu.with_memory_space_constraint(x, pltpu.HBM) if spec is FAR else x
                for x, spec in zip(args, specs, strict=True)
            )
        )

    return with_places


def fetch(pairs, sems):
    copies = [pltpu.make_async_copy(src, dst, sems.at[i]) for i, (src, dst) in enumerate(pairs)]
    for copy in copies:
        copy.start()
    return copies


def buffer(dims, dtype=BF):
    return pltpu.VMEM(dims, dtype)


def semaphores(n):
    return pltpu.SemaphoreType.DMA((n,))


def shape(dims, dtype=BF):
    return jax.ShapeDtypeStruct(dims, dtype)


def prepare_kernel(core, up_far, gate_far, down_far, w13, w2, norm, up, gate, down, sems):
    copies = fetch(((up_far, up), (gate_far, gate), (down_far, down)), sems)
    half = w2.shape[0]
    for i, w in enumerate((up, gate, down)):
        copies[i].wait()
        full = w[...].astype(F32)
        norm[i : i + 1, :] = jnp.full((1, 128), jnp.sum(full * full), F32)
    norm[3:8, :] = jnp.zeros((5, 128), F32)
    for c in range(2):

        @pl.when(core[0] == c)
        def _():
            w13[0:half, :] = up[:, c * half : (c + 1) * half].T
            w13[half:, :] = gate[:, c * half : (c + 1) * half].T
            w2[...] = down[c * half : (c + 1) * half, :]


def factor(i, norm, own, oth):
    size = jnp.sqrt(norm[i : i + 1, 0:1])
    total = own[i : i + 1, 0:1] + oth[i : i + 1, 0:1]
    return size / jnp.sqrt(total + 1e-06)


def raw_kernel(w13, w2, keys, targets, raw):
    raw[0 : w13.shape[0], :] = nt(w13[...], keys[...])
    raw[w13.shape[0] :, :] = nt(w2[...], targets[...])


def act_grads(act, lin, err, scale):
    if scale is not None:
        act, lin, err = (x * f for x, f in zip((act, lin, err), scale))
    sig = jax.nn.sigmoid(act)
    silu = act * sig
    hidden = (silu * lin).astype(BF)
    pgrad = (err * lin * sig * (1.0 + act * (1.0 - sig))).astype(BF)
    qgrad = (err * silu).astype(BF)
    return pgrad, qgrad, hidden


def grads_kernel(w13, w2, raw, *rest):
    far, state = rest[:4], rest[4:-8]
    out, k_oth, u_oth, k_own, u_own, held, sems, out_sems = rest[-8:]
    copies = fetch(tuple(zip(far, (k_oth, u_oth, k_own, u_own))), sems)
    half = w2.shape[0]
    cols = k_own.shape[1] // 2
    scale = [factor(i, *state) for i in (0, 1, 2)] if state else None
    own = act_grads(raw[0:half, :], raw[half : 2 * half, :], raw[2 * half :, :], scale)
    copies[0].wait()
    act, lin = nt(w13[0:half, :], k_oth[...]), nt(w13[half:, :], k_oth[...])
    copies[1].wait()
    oth = act_grads(act, lin, nt(w2[...], u_oth[...]), scale)
    copies[2].wait()
    copies[3].wait()
    copies = []
    for i in range(3):
        x, y = (k_own, k_oth) if i < 2 else (u_own, u_oth)
        rows = slice(i * half, (i + 1) * half)
        for j in range(2):
            at = slice(j * cols, (j + 1) * cols)
            g = dot(own[i], x[:, at]) + dot(oth[i], y[:, at])
            held[j, rows, :] = g.astype(BF)
            copy = pltpu.make_async_copy(
                held.at[j, rows, :], out.at[j, rows, :], out_sems.at[len(copies)]
            )
            copy.start()
            copies.append(copy)
    for copy in copies:
        copy.wait()


ROWS = 16


def update_kernel(w13_far, w2_far, gathered_far, *rest):
    again, rest = rest[:-9], rest[-9:]
    m13, m2, squares, w13, w2, gathered, later, sems, more = rest
    half = w2.shape[0]
    cols = w2.shape[1] // 2
    pairs = []
    for i in range(3):
        src, dst = (w13_far, w13) if i < 2 else (w2_far, w2)
        rows = slice((i % 2) * half, (i % 2 + 1) * half)
        at = slice(i * half, (i + 1) * half)
        pairs.append(((src.at[rows, :], dst.at[rows, :]),))
        pairs[-1] += ((gathered_far.at[:, at, :], gathered.at[:, at, :]),)
        if again:
            pairs[-1] += ((again[3].at[:, at, :], later.at[:, at, :]),)
    each = len(pairs[0])
    copies = fetch([p for group in pairs for p in group], more if again else sems)
    for i in range(3):
        src, dst = (w13, m13) if i < 2 else (w2, m2)
        base = (i % 2) * half
        if again:
            scale = jnp.broadcast_to(factor(i, *again[:3]), (ROWS, cols))
        for copy in copies[i * each : (i + 1) * each]:
            copy.wait()

        def step(r, total):
            row = pl.multiple_of(base + r * ROWS, ROWS)
            at = pl.multiple_of(i * half + r * ROWS, ROWS)
            for j in range(2):
                side = slice(j * cols, (j + 1) * cols)
                m = src[pl.ds(row, ROWS), side].astype(F32)
                m = m + gathered[j, pl.ds(at, ROWS), :].astype(F32)
                if again:
                    m = m * scale + later[j, pl.ds(at, ROWS), :].astype(F32)
                dst[pl.ds(row, ROWS), side] = m.astype(BF)
                total = total + m * m
            return total

        total = lax.fori_loop(0, half // ROWS, step, jnp.zeros((ROWS, cols), F32))
        squares[i : i + 1, :] = jnp.full((1, 128), jnp.sum(total), F32)
    squares[3:8, :] = jnp.zeros((5, 128), F32)


def query_kernel(m13, oth_far, own_far, raw, oth, own, sems):
    copies = fetch(((oth_far, oth), (own_far, own)), sems)
    copies[0].wait()
    raw[0] = nt(m13[...], oth[...])
    copies[1].wait()
    raw[1] = nt(m13[...], own[...])


def hidden_kernel(k, raw, norm, sq_own, sq_oth, hq):
    half = hq.shape[0]
    act = raw[k, 0:half, :] * factor(0, norm, sq_own, sq_oth)
    lin = raw[k, half:, :] * factor(1, norm, sq_own, sq_oth)
    hq[...] = (jax.nn.silu(act) * lin).astype(BF)


def piece_kernel(hq_own, hq_got, w2_own, w2_got, norm, sq_own, sq_oth, *pieces):
    count = pieces[0].shape[0]
    scale = factor(2, norm, sq_own, sq_oth)
    for k, o in enumerate(pieces):
        at = slice(k * count, (k + 1) * count)
        total = tn(hq_own[:, at], w2_own[...]) + tn(hq_got[:, at], w2_got[...])
        o[...] = (total * scale).astype(BF)


def spread_kernel(arrived, out, rounded, sems):
    total = arrived[0].astype(F32)
    for i in range(1, arrived.shape[0]):
        total = total + arrived[i].astype(F32)
    rounded[...] = total.astype(BF)
    for copy in fetch([(rounded, out.at[i]) for i in range(arrived.shape[0])], sems):
        copy.wait()


def stage_kernel(after, first_far, second_far, first, second, sems):
    for copy in fetch(((first_far, first), (second_far, second)), sems):
        copy.wait()


TILE = 512


def partial_kernel(place, *refs):
    *pieces, w_own, out = refs
    count = pieces[0].shape[0]
    for k, o in enumerate(pieces):
        out[k * count : (k + 1) * count, :] = dot(o[...], w_own[...])


def partial_product(place, pieces, w_out):
    count, width = pieces[0].shape
    n = w_out.shape[1] // 2
    steps = n // TILE
    tokens = count * len(pieces)
    return pl.pallas_call(
        partial_kernel,
        out_shape=shape((tokens, n), F32),
        grid_spec=pltpu.PrefetchScalarGridSpec(
            num_scalar_prefetch=1,
            grid=(steps,),
            in_specs=[pl.BlockSpec((count, width), lambda i, s: (0, 0))] * len(pieces)
            + [pl.BlockSpec((width, TILE), lambda i, s: (0, s[0] * steps + i))],
            out_specs=pl.BlockSpec((tokens, TILE), lambda i, s: (0, i)),
        ),
        compiler_params=pltpu.CompilerParams(vmem_limit_bytes=LIMIT),
        cost_estimate=pl.CostEstimate(
            flops=2 * tokens * width * n, bytes_accessed=10 << 20, transcendentals=0
        ),
    )(place, *pieces, w_out)


def finish_kernel(k, place, part, o_got, w_first, w_second, *rest):
    *_, out, held, sems = rest
    count, width = o_got.shape
    half = width // 2
    rows = slice(k * count, (k + 1) * count)
    o_first = o_got[:, pl.ds(pl.multiple_of(place[1] * half, 128), half)]
    o_second = o_got[:, pl.ds(pl.multiple_of((1 - place[1]) * half, 128), half)]
    copies = []
    for j in range(part.shape[1] // TILE):
        at = slice(j * TILE, (j + 1) * TILE)
        total = part[rows, at] + dot(o_first, w_first[:, at]) + dot(o_second, w_second[:, at])
        held[j] = total.astype(BF)
        copies.append(pltpu.make_async_copy(held.at[j], out.at[rows, at], sems.at[j]))
        copies[-1].start()
    for copy in copies:
        copy.wait()


def finish_product(place, k, part, o_got, w_first, w_second, out):
    count, width = o_got.shape
    tokens, n = part.shape
    args = (place, part, o_got, w_first, w_second)
    return pl.pallas_call(
        functools.partial(finish_kernel, k),
        out_shape=shape((tokens, n)),
        in_specs=[SMEM] + [VMEM] * 4 + [FAR] * (out is not None),
        out_specs=FAR,
        scratch_shapes=[
            pltpu.VMEM((n // TILE, count, TILE), BF),
            pltpu.SemaphoreType.DMA((n // TILE,)),
        ],
        input_output_aliases={} if out is None else {len(args): 0},
        compiler_params=pltpu.CompilerParams(vmem_limit_bytes=LIMIT),
        cost_estimate=pl.CostEstimate(
            flops=2 * count * width * n, bytes_accessed=4 << 20, transcendentals=0
        ),
    )(*args, *(() if out is None else (out,)))


def all_reduced(grads):
    peers = lax.axis_size(CHIPS)
    pieces = grads.reshape(peers, -1, grads.shape[2])
    arrived = lax.all_to_all(pieces, CHIPS, 0, 0, tiled=True)
    copies = call(
        spread_kernel,
        shape(pieces.shape),
        [VMEM],
        pieces.size,
        4 * pieces.size,
        (buffer(pieces.shape[1:]), semaphores(peers)),
        True,
    )(arrived)
    gathered = lax.all_to_all(copies, CHIPS, 0, 0, tiled=True)
    return gathered.reshape(grads.shape)


def swap(x):
    return lax.ppermute(x, "c", SWAP)


def shards(queries, keys, values, rates, w_up, w_gate, w_down, w_out):
    width, hid = w_up.shape[1:]
    tokens = keys.shape[0]
    half, third = hid // 2, 3 * hid // 2
    core, head = lax.axis_index("c"), lax.axis_index("h")
    n = w_out.shape[1] // 2

    k_oth = swap(keys)
    targets = (rates * values.astype(F32)).astype(BF)
    u_oth = swap(targets)
    kus = (keys, k_oth, targets, u_oth)

    place = jnp.stack([head, core]).astype(jnp.int32)
    sent = lax.dynamic_slice(w_out, (core * (width // 2), (1 - head) * n), (width // 2, n))
    w_first = lax.ppermute(sent, ("xl", "h"), ACROSS)
    w_second = swap(w_first)
    q_oth = swap(queries)

    wshape = (shape((2 * half, width)), shape((half, width)))
    sshape = shape((8, 128), F32)
    scratch = (buffer((width, hid)), buffer((width, hid)), buffer((hid, width)), semaphores(3))
    *w, norm = call(
        prepare_kernel, (*wshape, sshape), [SMEM, FAR, FAR, FAR], 1 << 21, 5 << 20, scratch
    )(core.reshape(1).astype(jnp.int32), w_up[0], w_gate[0], w_down[0])
    flops = 12 * 2 * tokens * width * half
    gdims = (2, third, width // 2)
    pair = [buffer((tokens, width))] * 2
    state, mats = (), w
    for step in range(STEPS):
        raw = call(raw_kernel, shape((third, tokens), F32), [VMEM] * 4, flops // 4, 4 << 20)(
            *mats, keys, targets
        )
        grads = call(
            grads_kernel,
            shape(gdims),
            [VMEM] * 3 + [ANY] * 2 + [FAR] * 2 + [VMEM] * len(state),
            flops * 3 // 4,
            8 << 20,
            (*pair, *pair, buffer(gdims), semaphores(4), semaphores(6)),
            True,
        )(*mats, raw, k_oth, u_oth, keys, targets, *state)
        gathered = all_reduced(grads)
        first = gathered if step == 0 else first
        again = () if step == 0 else (*state, gathered)
        *mats, squares = call(
            update_kernel,
            (*wshape, sshape),
            [FAR] * 2 + ([FAR] + [VMEM] * 3) * step + [ANY],
            1 << 22,
            5 << 20,
            (
                buffer((2 * half, width)),
                buffer((half, width)),
                buffer(gdims),
                buffer(gdims),
                semaphores(6),
                semaphores(9),
            ),
        )(*w, first, *again)
        state = (norm, squares, swap(squares))
    w2_got = swap(mats[1])
    hshape = shape((half, tokens))
    raw = call(
        query_kernel,
        shape((2, 2 * half, tokens), F32),
        [VMEM, ANY, FAR],
        flops // 3,
        5 << 20,
        (*pair, semaphores(2)),
    )(mats[0], q_oth, queries)
    hq_oth, hq_own = (
        call(functools.partial(hidden_kernel, k), hshape, [VMEM] * 4, 1 << 20, 2 << 20)(raw, *state)
        for k in range(2)
    )
    pieces = call(
        piece_kernel,
        (shape((tokens // CHUNKS, width)),) * CHUNKS,
        [VMEM] * 7,
        2 * tokens * hid * width,
        4 << 20,
    )(hq_own, swap(hq_oth), mats[1], w2_got, *state)
    pieces_got = [lax.ppermute(o, "h", SWAP) for o in pieces]
    part = partial_product(place, pieces, w_out)
    wide = (shape(w_first.shape),) * 2
    w_first, w_second = call(stage_kernel, wide, [ANY] * 3, 1 << 20, 5 << 20, [semaphores(2)])(
        pieces[0], w_first, w_second
    )
    out = None
    for k, o_got in enumerate(pieces_got):
        out = finish_product(place, k, part, o_got, w_first, w_second, out)
    return out


def solution(mesh):
    finer = Mesh(
        mesh.devices.reshape(4, 2, 4, 2, mesh.shape["head"]),
        ("z", "xl", "y", "c", "h"),
    )
    return jax.shard_map(
        shards,
        mesh=finer,
        in_specs=(
            P(CTX, "h"),
            P(CTX, "h"),
            P(CTX, "h"),
            P(CTX, "h"),
            P("h", None, None),
            P("h", None, None),
            P("h", None, None),
            P("h", None),
        ),
        out_specs=P(CTX, "h"),
        check_vma=False,
    )
```

```python
import functools

import jax
import jax.numpy as jnp
from jax import lax
from jax.experimental import pallas as pl
from jax.experimental.pallas import tpu as pltpu
from jax.sharding import Mesh
from jax.sharding import PartitionSpec as P

STEPS = 2
CTX = ("z", "xl", "y", "c")
CHIPS = ("z", "xl", "y")
SWAP = [(0, 1), (1, 0)]
ACROSS = [(0, 3), (3, 0), (1, 2), (2, 1)]
BF = jnp.bfloat16
F32 = jnp.float32
NT = (((1,), (1,)), ((), ()))
TN = (((0,), (0,)), ((), ()))
VMEM = pl.BlockSpec(memory_space=pltpu.VMEM)
SMEM = pl.BlockSpec(memory_space=pltpu.SMEM)
FAR = pl.BlockSpec(memory_space=pltpu.HBM)
ANY = pl.BlockSpec(memory_space=pl.ANY)
NEAR = pl.BlockSpec(memory_space=pltpu.VMEM)
HELD = {id(FAR): pltpu.HBM, id(NEAR): pltpu.VMEM}
LIMIT = 24 * 1024 * 1024
CHUNKS = 2


def dot(x, y):
    return jnp.dot(x, y, preferred_element_type=F32)


def nt(x, y):
    return lax.dot_general(x, y, NT, preferred_element_type=F32)


def tn(x, y):
    return lax.dot_general(x, y, TN, preferred_element_type=F32)


def call(kernel, outs, specs, flops, nbytes, scratch=(), far=False):
    if far:
        outs = jax.tree.map(lambda x: pltpu.HBM(x.shape, x.dtype), outs)
    run = pl.pallas_call(
        kernel,
        out_shape=outs,
        in_specs=specs,
        out_specs=jax.tree.map(lambda _: FAR if far else VMEM, outs),
        scratch_shapes=list(scratch),
        compiler_params=pltpu.CompilerParams(vmem_limit_bytes=LIMIT),
        cost_estimate=pl.CostEstimate(flops=flops, bytes_accessed=nbytes, transcendentals=0),
    )

    def with_places(*args):
        return run(
            *(
                pltpu.with_memory_space_constraint(x, HELD[id(spec)]) if id(spec) in HELD else x
                for x, spec in zip(args, specs, strict=True)
            )
        )

    return with_places


def fetch(pairs, sems):
    copies = [pltpu.make_async_copy(src, dst, sems.at[i]) for i, (src, dst) in enumerate(pairs)]
    for copy in copies:
        copy.start()
    return copies


def buffer(dims, dtype=BF):
    return pltpu.VMEM(dims, dtype)


def semaphores(n):
    return pltpu.SemaphoreType.DMA((n,))


def shape(dims, dtype=BF):
    return jax.ShapeDtypeStruct(dims, dtype)


def prepare_kernel(core, up_far, gate_far, down_far, w13, w2, norm, up, gate, down, sems):
    copies = fetch(((up_far, up), (gate_far, gate), (down_far, down)), sems)
    half = w2.shape[0]
    for i, w in enumerate((up, gate, down)):
        copies[i].wait()
        full = w[...].astype(F32)
        norm[i : i + 1, :] = jnp.full((1, 128), jnp.sum(full * full), F32)
    norm[3:8, :] = jnp.zeros((5, 128), F32)
    for c in range(2):

        @pl.when(core[0] == c)
        def _():
            w13[0:half, :] = up[:, c * half : (c + 1) * half].T
            w13[half:, :] = gate[:, c * half : (c + 1) * half].T
            w2[...] = down[c * half : (c + 1) * half, :]


def factor(i, norm, own, oth):
    size = jnp.sqrt(norm[i : i + 1, 0:1])
    total = own[i : i + 1, 0:1] + oth[i : i + 1, 0:1]
    return size / jnp.sqrt(total + 1e-06)


def raw_kernel(w13, w2, keys, targets, raw):
    raw[0 : w13.shape[0], :] = nt(w13[...], keys[...])
    raw[w13.shape[0] :, :] = nt(w2[...], targets[...])


def act_grads(act, lin, err, scale):
    if scale is not None:
        act, lin, err = (x * f for x, f in zip((act, lin, err), scale))
    sig = jax.nn.sigmoid(act)
    silu = act * sig
    hidden = (silu * lin).astype(BF)
    pgrad = (err * lin * sig * (1.0 + act * (1.0 - sig))).astype(BF)
    qgrad = (err * silu).astype(BF)
    return pgrad, qgrad, hidden


def grads_kernel(w13, w2, raw, k_own, k_oth, u_own, u_oth, *rest):
    *state, out = rest
    half = w2.shape[0]
    cols = k_own.shape[1] // 2
    scale = [factor(i, *state) for i in (0, 1, 2)] if state else None
    keys, targets = k_oth[...], u_oth[...]
    oth = act_grads(
        nt(w13[0:half, :], keys), nt(w13[half:, :], keys), nt(w2[...], targets), scale
    )
    own = act_grads(raw[0:half, :], raw[half : 2 * half, :], raw[2 * half :, :], scale)
    for i in range(3):
        x, y = (k_own, k_oth) if i < 2 else (u_own, u_oth)
        for j in range(2):
            at = slice(j * cols, (j + 1) * cols)
            g = dot(own[i], x[:, at]) + dot(oth[i], y[:, at])
            out[j, i * half : (i + 1) * half, :] = g.astype(BF)


ROWS = 16


def update_kernel(w13_far, w2_far, *rest):
    *again, gathered, m13, m2, squares, w13, w2, first, sems = rest
    half = w2.shape[0]
    cols = w2.shape[1] // 2
    pairs = []
    for i in range(3):
        src, dst = (w13_far, w13) if i < 2 else (w2_far, w2)
        rows = slice((i % 2) * half, (i % 2 + 1) * half)
        at = slice(i * half, (i + 1) * half)
        pairs.append((src.at[rows, :], dst.at[rows, :]))
        if again:
            pairs.append((again[0].at[:, at, :], first.at[:, at, :]))
    each = len(pairs) // 3
    copies = fetch(pairs, sems)
    for i in range(3):
        src, dst = (w13, m13) if i < 2 else (w2, m2)
        base = (i % 2) * half
        if again:
            scale = jnp.broadcast_to(factor(i, *again[1:]), (ROWS, cols))
        for copy in copies[i * each : (i + 1) * each]:
            copy.wait()

        def step(r, total):
            row = pl.multiple_of(base + r * ROWS, ROWS)
            at = pl.multiple_of(i * half + r * ROWS, ROWS)
            for j in range(2):
                side = slice(j * cols, (j + 1) * cols)
                m = src[pl.ds(row, ROWS), side].astype(F32)
                if again:
                    m = (m + first[j, pl.ds(at, ROWS), :].astype(F32)) * scale
                m = m + gathered[j, pl.ds(at, ROWS), :].astype(F32)
                dst[pl.ds(row, ROWS), side] = m.astype(BF)
                total = total + m * m
            return total

        total = lax.fori_loop(0, half // ROWS, step, jnp.zeros((ROWS, cols), F32))
        squares[i : i + 1, :] = jnp.full((1, 128), jnp.sum(total), F32)
    squares[3:8, :] = jnp.zeros((5, 128), F32)


def query_kernel(m13, oth_far, own_far, raw, oth, own, sems):
    copies = fetch(((oth_far, oth), (own_far, own)), sems)
    copies[0].wait()
    raw[0] = nt(m13[...], oth[...])
    copies[1].wait()
    raw[1] = nt(m13[...], own[...])


def hidden_kernel(k, raw, norm, sq_own, sq_oth, hq):
    half = hq.shape[0]
    act = raw[k, 0:half, :] * factor(0, norm, sq_own, sq_oth)
    lin = raw[k, half:, :] * factor(1, norm, sq_own, sq_oth)
    hq[...] = (jax.nn.silu(act) * lin).astype(BF)


def piece_kernel(hq_own, hq_got, w2_own, w2_got, norm, sq_own, sq_oth, *pieces):
    count = pieces[0].shape[0]
    scale = factor(2, norm, sq_own, sq_oth)
    for k, o in enumerate(pieces):
        at = slice(k * count, (k + 1) * count)
        total = tn(hq_own[:, at], w2_own[...]) + tn(hq_got[:, at], w2_got[...])
        o[...] = (total * scale).astype(BF)


def spread_kernel(arrived, out):
    total = arrived[0].astype(F32)
    for i in range(1, arrived.shape[0]):
        total = total + arrived[i].astype(F32)
    rounded = total.astype(BF)
    for i in range(arrived.shape[0]):
        out[i] = rounded


def stage_kernel(after, first_far, second_far, first, second, sems):
    for copy in fetch(((first_far, first), (second_far, second)), sems):
        copy.wait()


TILE = 512


def partial_kernel(place, *refs):
    *pieces, w_own, out = refs
    count = pieces[0].shape[0]
    for k, o in enumerate(pieces):
        out[k * count : (k + 1) * count, :] = dot(o[...], w_own[...])


def partial_product(place, pieces, w_out):
    count, width = pieces[0].shape
    n = w_out.shape[1] // 2
    steps = n // TILE
    tokens = count * len(pieces)
    return pl.pallas_call(
        partial_kernel,
        out_shape=shape((tokens, n), F32),
        grid_spec=pltpu.PrefetchScalarGridSpec(
            num_scalar_prefetch=1,
            grid=(steps,),
            in_specs=[pl.BlockSpec((count, width), lambda i, s: (0, 0))] * len(pieces)
            + [pl.BlockSpec((width, TILE), lambda i, s: (0, s[0] * steps + i))],
            out_specs=pl.BlockSpec((tokens, TILE), lambda i, s: (0, i)),
        ),
        compiler_params=pltpu.CompilerParams(vmem_limit_bytes=LIMIT),
        cost_estimate=pl.CostEstimate(
            flops=2 * tokens * width * n, bytes_accessed=10 << 20, transcendentals=0
        ),
    )(place, *pieces, w_out)


def finish_kernel(k, place, part, o_got, w_first, w_second, *rest):
    *_, out, held, sems = rest
    count, width = o_got.shape
    half = width // 2
    rows = slice(k * count, (k + 1) * count)
    o_first = o_got[:, pl.ds(pl.multiple_of(place[1] * half, 128), half)]
    o_second = o_got[:, pl.ds(pl.multiple_of((1 - place[1]) * half, 128), half)]
    copies = []
    for j in range(part.shape[1] // TILE):
        at = slice(j * TILE, (j + 1) * TILE)
        total = part[rows, at] + dot(o_first, w_first[:, at]) + dot(o_second, w_second[:, at])
        held[j] = total.astype(BF)
        copies.append(pltpu.make_async_copy(held.at[j], out.at[rows, at], sems.at[j]))
        copies[-1].start()
    for copy in copies:
        copy.wait()


def finish_product(place, k, part, o_got, w_first, w_second, out):
    count, width = o_got.shape
    tokens, n = part.shape
    args = (place, part, o_got, w_first, w_second)
    return pl.pallas_call(
        functools.partial(finish_kernel, k),
        out_shape=shape((tokens, n)),
        in_specs=[SMEM] + [VMEM] * 4 + [FAR] * (out is not None),
        out_specs=FAR,
        scratch_shapes=[
            pltpu.VMEM((n // TILE, count, TILE), BF),
            pltpu.SemaphoreType.DMA((n // TILE,)),
        ],
        input_output_aliases={} if out is None else {len(args): 0},
        compiler_params=pltpu.CompilerParams(vmem_limit_bytes=LIMIT),
        cost_estimate=pl.CostEstimate(
            flops=2 * count * width * n, bytes_accessed=4 << 20, transcendentals=0
        ),
    )(*args, *(() if out is None else (out,)))


def all_reduced(grads, beside=None):
    peers = lax.axis_size(CHIPS)
    pieces = grads.reshape(peers, -1, grads.shape[2])
    arrived = lax.all_to_all(pieces, CHIPS, 0, 0, tiled=True)
    copies = call(
        spread_kernel,
        shape(pieces.shape),
        [VMEM],
        pieces.size,
        4 * pieces.size,
    )(arrived)
    if beside is not None:
        beside, _ = lax.optimization_barrier((beside, copies))
    gathered = lax.all_to_all(copies, CHIPS, 0, 0, tiled=True)
    return gathered.reshape(grads.shape), beside


def swap(x):
    return lax.ppermute(x, "c", SWAP)


def shards(queries, keys, values, rates, w_up, w_gate, w_down, w_out):
    width, hid = w_up.shape[1:]
    tokens = keys.shape[0]
    half, third = hid // 2, 3 * hid // 2
    core, head = lax.axis_index("c"), lax.axis_index("h")
    n = w_out.shape[1] // 2

    k_oth = swap(keys)
    targets = (rates * values.astype(F32)).astype(BF)
    u_oth = swap(targets)
    kus = (keys, k_oth, targets, u_oth)

    place = jnp.stack([head, core]).astype(jnp.int32)
    sent = lax.dynamic_slice(w_out, (core * (width // 2), (1 - head) * n), (width // 2, n))
    w_first = lax.ppermute(sent, ("xl", "h"), ACROSS)
    q_oth = swap(queries)

    wshape = (shape((2 * half, width)), shape((half, width)))
    sshape = shape((8, 128), F32)
    scratch = (buffer((width, hid)), buffer((width, hid)), buffer((hid, width)), semaphores(3))
    *w, norm = call(
        prepare_kernel, (*wshape, sshape), [SMEM, FAR, FAR, FAR], 1 << 21, 5 << 20, scratch
    )(core.reshape(1).astype(jnp.int32), w_up[0], w_gate[0], w_down[0])
    flops = 12 * 2 * tokens * width * half
    gdims = (2, third, width // 2)
    pair = [buffer((tokens, width))] * 2
    state, mats = (), w
    for step in range(STEPS):
        raw = call(raw_kernel, shape((third, tokens), F32), [VMEM] * 4, flops // 4, 4 << 20)(
            *mats, keys, targets
        )
        grads = call(
            grads_kernel,
            shape(gdims),
            [VMEM] * (7 + len(state)),
            flops * 3 // 4,
            8 << 20,
        )(*mats, raw, keys, k_oth, targets, u_oth, *state)
        gathered, w_late = all_reduced(grads, w_first if step else None)
        again = () if step == 0 else (first, *state)
        *mats, squares = call(
            update_kernel,
            (*wshape, sshape),
            [FAR] * 2 + ([FAR] + [VMEM] * 3) * step + [NEAR],
            1 << 22,
            5 << 20,
            (
                buffer((2 * half, width)),
                buffer((half, width)),
                buffer(gdims),
                semaphores(3 + 3 * step),
            ),
        )(*w, *again, gathered)
        first = gathered
        state = (norm, squares, swap(squares))
    w_second = swap(w_late)
    w2_got = swap(mats[1])
    hshape = shape((half, tokens))
    raw = call(
        query_kernel,
        shape((2, 2 * half, tokens), F32),
        [VMEM, ANY, FAR],
        flops // 3,
        5 << 20,
        (*pair, semaphores(2)),
    )(mats[0], q_oth, queries)
    hq_oth, hq_own = (
        call(functools.partial(hidden_kernel, k), hshape, [VMEM] * 4, 1 << 20, 2 << 20)(raw, *state)
        for k in range(2)
    )
    pieces = call(
        piece_kernel,
        (shape((tokens // CHUNKS, width)),) * CHUNKS,
        [VMEM] * 7,
        2 * tokens * hid * width,
        4 << 20,
    )(hq_own, swap(hq_oth), mats[1], w2_got, *state)
    pieces_got = [lax.ppermute(o, "h", SWAP) for o in pieces]
    part = partial_product(place, pieces, w_out)
    wide = (shape(w_first.shape),) * 2
    w_first, w_second = call(stage_kernel, wide, [ANY] * 3, 1 << 20, 5 << 20, [semaphores(2)])(
        pieces[0], w_first, w_second
    )
    out = None
    for k, o_got in enumerate(pieces_got):
        out = finish_product(place, k, part, o_got, w_first, w_second, out)
    return out


def solution(mesh):
    finer = Mesh(
        mesh.devices.reshape(4, 2, 4, 2, mesh.shape["head"]),
        ("z", "xl", "y", "c", "h"),
    )
    return jax.shard_map(
        shards,
        mesh=finer,
        in_specs=(
            P(CTX, "h"),
            P(CTX, "h"),
            P(CTX, "h"),
            P(CTX, "h"),
            P("h", None, None),
            P("h", None, None),
            P("h", None, None),
            P("h", None),
        ),
        out_specs=P(CTX, "h"),
        check_vma=False,
    )
```

```python
import functools

import jax
import jax.numpy as jnp
from jax import lax
from jax.experimental import pallas as pl
from jax.experimental.pallas import tpu as pltpu
from jax.sharding import Mesh
from jax.sharding import PartitionSpec as P

STEPS = 2
CTX = ("z", "xl", "y", "c")
CHIPS = ("z", "xl", "y")
SWAP = [(0, 1), (1, 0)]
ACROSS = [(0, 3), (3, 0), (1, 2), (2, 1)]
BF = jnp.bfloat16
F32 = jnp.float32
NT = (((1,), (1,)), ((), ()))
TN = (((0,), (0,)), ((), ()))
VMEM = pl.BlockSpec(memory_space=pltpu.VMEM)
SMEM = pl.BlockSpec(memory_space=pltpu.SMEM)
FAR = pl.BlockSpec(memory_space=pltpu.HBM)
ANY = pl.BlockSpec(memory_space=pl.ANY)
NEAR = pl.BlockSpec(memory_space=pltpu.VMEM)
HELD = {id(FAR): pltpu.HBM, id(NEAR): pltpu.VMEM}
LIMIT = 24 * 1024 * 1024


def dot(x, y):
    return jnp.dot(x, y, preferred_element_type=F32)


def nt(x, y):
    return lax.dot_general(x, y, NT, preferred_element_type=F32)


def tn(x, y):
    return lax.dot_general(x, y, TN, preferred_element_type=F32)


def call(kernel, outs, specs, flops, nbytes, scratch=(), far=False):
    if far:
        outs = jax.tree.map(lambda x: pltpu.HBM(x.shape, x.dtype), outs)
    run = pl.pallas_call(
        kernel,
        out_shape=outs,
        in_specs=specs,
        out_specs=jax.tree.map(lambda _: FAR if far else VMEM, outs),
        scratch_shapes=list(scratch),
        compiler_params=pltpu.CompilerParams(vmem_limit_bytes=LIMIT),
        cost_estimate=pl.CostEstimate(flops=flops, bytes_accessed=nbytes, transcendentals=0),
    )

    def with_places(*args):
        return run(
            *(
                pltpu.with_memory_space_constraint(x, HELD[id(spec)]) if id(spec) in HELD else x
                for x, spec in zip(args, specs, strict=True)
            )
        )

    return with_places


def fetch(pairs, sems):
    copies = [pltpu.make_async_copy(src, dst, sems.at[i]) for i, (src, dst) in enumerate(pairs)]
    for copy in copies:
        copy.start()
    return copies


def buffer(dims, dtype=BF):
    return pltpu.VMEM(dims, dtype)


def semaphores(n):
    return pltpu.SemaphoreType.DMA((n,))


def shape(dims, dtype=BF):
    return jax.ShapeDtypeStruct(dims, dtype)


def prepare_kernel(core, up_far, gate_far, down_far, w13, w2, norm, up, gate, down, sems):
    copies = fetch(((up_far, up), (gate_far, gate), (down_far, down)), sems)
    half = w2.shape[0]
    for i, w in enumerate((up, gate, down)):
        copies[i].wait()
        full = w[...].astype(F32)
        norm[i : i + 1, :] = jnp.full((1, 128), jnp.sum(full * full), F32)
    norm[3:8, :] = jnp.zeros((5, 128), F32)
    for c in range(2):

        @pl.when(core[0] == c)
        def _():
            w13[0:half, :] = up[:, c * half : (c + 1) * half].T
            w13[half:, :] = gate[:, c * half : (c + 1) * half].T
            w2[...] = down[c * half : (c + 1) * half, :]


def factor(i, norm, own, oth):
    size = jnp.sqrt(norm[i : i + 1, 0:1])
    total = own[i : i + 1, 0:1] + oth[i : i + 1, 0:1]
    return size / jnp.sqrt(total + 1e-06)


def raw_kernel(w13, w2, keys, targets, raw):
    raw[0 : w13.shape[0], :] = nt(w13[...], keys[...])
    raw[w13.shape[0] :, :] = nt(w2[...], targets[...])


def act_grads(act, lin, err, scale):
    if scale is not None:
        act, lin, err = (x * f for x, f in zip((act, lin, err), scale))
    sig = jax.nn.sigmoid(act)
    silu = act * sig
    hidden = (silu * lin).astype(BF)
    pgrad = (err * lin * sig * (1.0 + act * (1.0 - sig))).astype(BF)
    qgrad = (err * silu).astype(BF)
    return pgrad, qgrad, hidden


def grads_kernel(w13, w2, raw, k_own, k_oth, u_own, u_oth, *rest):
    *state, out = rest
    half = w2.shape[0]
    cols = k_own.shape[1] // 2
    scale = [factor(i, *state) for i in (0, 1, 2)] if state else None
    keys, targets = k_oth[...], u_oth[...]
    oth = act_grads(
        nt(w13[0:half, :], keys), nt(w13[half:, :], keys), nt(w2[...], targets), scale
    )
    own = act_grads(raw[0:half, :], raw[half : 2 * half, :], raw[2 * half :, :], scale)
    for i in range(3):
        x, y = (k_own, k_oth) if i < 2 else (u_own, u_oth)
        for j in range(2):
            at = slice(j * cols, (j + 1) * cols)
            g = dot(own[i], x[:, at]) + dot(oth[i], y[:, at])
            out[j, i * half : (i + 1) * half, :] = g.astype(BF)


ROWS = 16


def update_kernel(w13_far, w2_far, *rest):
    if len(rest) > 8:
        first_far, *state, gathered_far, m13, m2, squares, w13, w2, first, gathered, sems = rest
    else:
        gathered, m13, m2, squares, w13, w2, first, sems = rest
    again = len(rest) > 8
    half = w2.shape[0]
    cols = w2.shape[1] // 2
    pairs = []
    for i in range(3):
        src, dst = (w13_far, w13) if i < 2 else (w2_far, w2)
        rows = slice((i % 2) * half, (i % 2 + 1) * half)
        at = slice(i * half, (i + 1) * half)
        pairs.append((src.at[rows, :], dst.at[rows, :]))
        if again:
            pairs.append((first_far.at[:, at, :], first.at[:, at, :]))
            pairs.append((gathered_far.at[:, at, :], gathered.at[:, at, :]))
    each = len(pairs) // 3
    copies = fetch(pairs, sems)
    for i in range(3):
        src, dst = (w13, m13) if i < 2 else (w2, m2)
        base = (i % 2) * half
        if again:
            scale = jnp.broadcast_to(factor(i, *state), (ROWS, cols))
        for copy in copies[i * each : (i + 1) * each]:
            copy.wait()

        def step(r, total):
            row = pl.multiple_of(base + r * ROWS, ROWS)
            at = pl.multiple_of(i * half + r * ROWS, ROWS)
            for j in range(2):
                side = slice(j * cols, (j + 1) * cols)
                m = src[pl.ds(row, ROWS), side].astype(F32)
                if again:
                    m = (m + first[j, pl.ds(at, ROWS), :].astype(F32)) * scale
                m = m + gathered[j, pl.ds(at, ROWS), :].astype(F32)
                dst[pl.ds(row, ROWS), side] = m.astype(BF)
                total = total + m * m
            return total

        total = lax.fori_loop(0, half // ROWS, step, jnp.zeros((ROWS, cols), F32))
        squares[i : i + 1, :] = jnp.full((1, 128), jnp.sum(total), F32)
    squares[3:8, :] = jnp.zeros((5, 128), F32)


def query_kernel(m13, oth_far, own_far, raw, oth, own, sems):
    copies = fetch(((oth_far, oth), (own_far, own)), sems)
    copies[0].wait()
    raw[0] = nt(m13[...], oth[...])
    copies[1].wait()
    raw[1] = nt(m13[...], own[...])


def hidden_kernel(k, raw, norm, sq_own, sq_oth, hq):
    half = hq.shape[0]
    act = raw[k, 0:half, :] * factor(0, norm, sq_own, sq_oth)
    lin = raw[k, half:, :] * factor(1, norm, sq_own, sq_oth)
    hq[...] = (jax.nn.silu(act) * lin * factor(2, norm, sq_own, sq_oth)).astype(BF)


def piece_kernel(hq_own, hq_got, w2_own, w2_got, o):
    o[...] = (tn(hq_own[...], w2_own[...]) + tn(hq_got[...], w2_got[...])).astype(BF)


def spread_kernel(arrived, out):
    total = arrived[0].astype(F32)
    for i in range(1, arrived.shape[0]):
        total = total + arrived[i].astype(F32)
    rounded = total.astype(BF)
    for i in range(arrived.shape[0]):
        out[i] = rounded


def stage_kernel(after, first_far, second_far, first, second, sems):
    for copy in fetch(((first_far, first), (second_far, second)), sems):
        copy.wait()


TILE = 512


def partial_kernel(place, o, w_own, out):
    out[...] = dot(o[...], w_own[...])


def partial_product(place, o, w_out):
    tokens, width = o.shape
    n = w_out.shape[1] // 2
    steps = n // TILE
    return pl.pallas_call(
        partial_kernel,
        out_shape=shape((tokens, n), F32),
        grid_spec=pltpu.PrefetchScalarGridSpec(
            num_scalar_prefetch=1,
            grid=(steps,),
            in_specs=[
                pl.BlockSpec((tokens, width), lambda i, s: (0, 0)),
                pl.BlockSpec((width, TILE), lambda i, s: (0, s[0] * steps + i)),
            ],
            out_specs=pl.BlockSpec((tokens, TILE), lambda i, s: (0, i)),
        ),
        compiler_params=pltpu.CompilerParams(vmem_limit_bytes=LIMIT),
        cost_estimate=pl.CostEstimate(
            flops=1 << 20, bytes_accessed=1 << 16, transcendentals=0
        ),
    )(place, o, w_out)


def finish_kernel(place, part, hq_a, hq_b, *rest):
    w2_a, w2_b, w_first, w_second, out, o, held, sems = rest
    half = o.shape[1] // 2
    o[...] = (tn(hq_a[...], w2_a[...]) + tn(hq_b[...], w2_b[...])).astype(BF)
    o_first = o[:, pl.ds(pl.multiple_of(place[1] * half, half), half)]
    o_second = o[:, pl.ds(pl.multiple_of((1 - place[1]) * half, half), half)]
    copies = []
    for j in range(part.shape[1] // TILE):
        at = slice(j * TILE, (j + 1) * TILE)
        total = part[:, at] + dot(o_first, w_first[:, at]) + dot(o_second, w_second[:, at])
        held[j] = total.astype(BF)
        copies.append(pltpu.make_async_copy(held.at[j], out.at[:, at], sems.at[j]))
        copies[-1].start()
    for copy in copies:
        copy.wait()


def finish_product(place, part, hqs, w2s, w_first, w_second):
    tokens, n = part.shape
    width = w2s[0].shape[1]
    return pl.pallas_call(
        finish_kernel,
        out_shape=shape((tokens, n)),
        in_specs=[SMEM] + [VMEM] * 7,
        out_specs=FAR,
        scratch_shapes=[
            buffer((tokens, width)),
            buffer((n // TILE, tokens, TILE)),
            semaphores(n // TILE),
        ],
        compiler_params=pltpu.CompilerParams(vmem_limit_bytes=LIMIT),
        cost_estimate=pl.CostEstimate(
            flops=2 * tokens * width * (n + width // 2), bytes_accessed=6 << 20, transcendentals=0
        ),
    )(place, part, *hqs, *w2s, w_first, w_second)


def all_reduced(grads, beside=None):
    peers = lax.axis_size(CHIPS)
    pieces = grads.reshape(peers, -1, grads.shape[2])
    arrived = lax.all_to_all(pieces, CHIPS, 0, 0, tiled=True)
    copies = call(
        spread_kernel,
        shape(pieces.shape),
        [VMEM],
        pieces.size,
        4 * pieces.size,
    )(arrived)
    if beside is not None:
        beside, _ = lax.optimization_barrier((beside, copies))
    gathered = lax.all_to_all(copies, CHIPS, 0, 0, tiled=True)
    return gathered.reshape(grads.shape), beside


def swap(x):
    return lax.ppermute(x, "c", SWAP)


def shards(queries, keys, values, rates, w_up, w_gate, w_down, w_out):
    width, hid = w_up.shape[1:]
    tokens = keys.shape[0]
    half, third = hid // 2, 3 * hid // 2
    core, head = lax.axis_index("c"), lax.axis_index("h")
    n = w_out.shape[1] // 2

    k_oth = swap(keys)
    targets = (rates * values.astype(F32)).astype(BF)
    u_oth = swap(targets)
    kus = (keys, k_oth, targets, u_oth)

    place = jnp.stack([head, core]).astype(jnp.int32)
    sent = lax.dynamic_slice(w_out, (core * (width // 2), (1 - head) * n), (width // 2, n))
    w_first = lax.ppermute(sent, ("xl", "h"), ACROSS)

    wshape = (shape((2 * half, width)), shape((half, width)))
    sshape = shape((8, 128), F32)
    scratch = (buffer((width, hid)), buffer((width, hid)), buffer((hid, width)), semaphores(3))
    *w, norm = call(
        prepare_kernel, (*wshape, sshape), [SMEM, FAR, FAR, FAR], 1 << 21, 5 << 20, scratch
    )(core.reshape(1).astype(jnp.int32), w_up[0], w_gate[0], w_down[0])
    flops = 12 * 2 * tokens * width * half
    gdims = (2, third, width // 2)
    pair = [buffer((tokens, width))] * 2
    state, mats = (), w
    for step in range(STEPS):
        raw = call(raw_kernel, shape((third, tokens), F32), [VMEM] * 4, flops // 4, 4 << 20)(
            *mats, keys, targets
        )
        grads = call(
            grads_kernel,
            shape(gdims),
            [VMEM] * (7 + len(state)),
            flops * 3 // 4,
            8 << 20,
        )(*mats, raw, keys, k_oth, targets, u_oth, *state)
        gathered, w_late = all_reduced(grads, w_first if step else None)
        again = () if step == 0 else (first, *state)
        *mats, squares = call(
            update_kernel,
            (*wshape, sshape),
            [FAR] * 2 + ([FAR] + [VMEM] * 3) * step + [ANY if step else NEAR],
            1 << 22,
            5 << 20,
            (
                buffer((2 * half, width)),
                buffer((half, width)),
                buffer(gdims),
                *([buffer(gdims)] * step),
                semaphores(3 + 6 * step),
            ),
        )(*w, *again, gathered)
        first = gathered
        state = (norm, squares, swap(squares))
    crossed = lax.ppermute(mats[1], ("xl", "h"), ACROSS)
    w_second = swap(w_late)
    q_oth = swap(queries)
    w2_got = swap(mats[1])
    hshape = shape((half, tokens))
    raw = call(
        query_kernel,
        shape((2, 2 * half, tokens), F32),
        [VMEM, ANY, FAR],
        flops // 3,
        5 << 20,
        (*pair, semaphores(2)),
    )(mats[0], q_oth, queries)
    hq_oth, hq_own = (
        call(functools.partial(hidden_kernel, k), hshape, [VMEM] * 4, 1 << 20, 2 << 20)(raw, *state)
        for k in range(2)
    )
    hq_got = swap(hq_oth)
    hqs = [lax.ppermute(x, "h", SWAP) for x in (hq_own, hq_got)]
    o = call(piece_kernel, shape((tokens, width)), [VMEM] * 4, 1 << 20, 1 << 16)(
        hq_own, hq_got, mats[1], w2_got
    )
    part = partial_product(place, o, w_out)
    wide = (shape(w_first.shape),) * 2
    w_first, w_second = call(stage_kernel, wide, [ANY] * 3, 1 << 16, 1 << 16, [semaphores(2)])(
        hqs[0], w_first, w_second
    )
    crossed, *hqs, _, _ = lax.optimization_barrier((crossed, *hqs, part, w_first))
    return finish_product(place, part, hqs, (crossed, swap(crossed)), w_first, w_second)


def solution(mesh):
    finer = Mesh(
        mesh.devices.reshape(4, 2, 4, 2, mesh.shape["head"]),
        ("z", "xl", "y", "c", "h"),
    )
    return jax.shard_map(
        shards,
        mesh=finer,
        in_specs=(
            P(CTX, "h"),
            P(CTX, "h"),
            P(CTX, "h"),
            P(CTX, "h"),
            P("h", None, None),
            P("h", None, None),
            P("h", None, None),
            P("h", None),
        ),
        out_specs=P(CTX, "h"),
        check_vma=False,
    )
```

```python
import functools

import jax
import jax.numpy as jnp
from jax import lax
from jax.experimental import pallas as pl
from jax.experimental.pallas import tpu as pltpu
from jax.sharding import Mesh
from jax.sharding import PartitionSpec as P

STEPS = 2
CTX = ("z", "xl", "y", "c")
CHIPS = ("z", "xl", "y")
SWAP = [(0, 1), (1, 0)]
ACROSS = [(0, 3), (3, 0), (1, 2), (2, 1)]
BF = jnp.bfloat16
F32 = jnp.float32
NT = (((1,), (1,)), ((), ()))
TN = (((0,), (0,)), ((), ()))
VMEM = pl.BlockSpec(memory_space=pltpu.VMEM)
SMEM = pl.BlockSpec(memory_space=pltpu.SMEM)
FAR = pl.BlockSpec(memory_space=pltpu.HBM)
ANY = pl.BlockSpec(memory_space=pl.ANY)
NEAR = pl.BlockSpec(memory_space=pltpu.VMEM)
HELD = {id(FAR): pltpu.HBM, id(NEAR): pltpu.VMEM}
LIMIT = 24 * 1024 * 1024


def dot(x, y):
    return jnp.dot(x, y, preferred_element_type=F32)


def nt(x, y):
    return lax.dot_general(x, y, NT, preferred_element_type=F32)


def tn(x, y):
    return lax.dot_general(x, y, TN, preferred_element_type=F32)


def call(kernel, outs, specs, flops, nbytes, scratch=(), far=False):
    if far:
        outs = jax.tree.map(lambda x: pltpu.HBM(x.shape, x.dtype), outs)
    run = pl.pallas_call(
        kernel,
        out_shape=outs,
        in_specs=specs,
        out_specs=jax.tree.map(lambda _: FAR if far else VMEM, outs),
        scratch_shapes=list(scratch),
        compiler_params=pltpu.CompilerParams(vmem_limit_bytes=LIMIT),
        cost_estimate=pl.CostEstimate(flops=flops, bytes_accessed=nbytes, transcendentals=0),
    )

    def with_places(*args):
        return run(
            *(
                pltpu.with_memory_space_constraint(x, HELD[id(spec)]) if id(spec) in HELD else x
                for x, spec in zip(args, specs, strict=True)
            )
        )

    return with_places


def fetch(pairs, sems):
    copies = [pltpu.make_async_copy(src, dst, sems.at[i]) for i, (src, dst) in enumerate(pairs)]
    for copy in copies:
        copy.start()
    return copies


def buffer(dims, dtype=BF):
    return pltpu.VMEM(dims, dtype)


def semaphores(n):
    return pltpu.SemaphoreType.DMA((n,))


def shape(dims, dtype=BF):
    return jax.ShapeDtypeStruct(dims, dtype)


def prepare_kernel(core, up_far, gate_far, down_far, w13, w2, norm, up, gate, down, sems):
    copies = fetch(((up_far, up), (gate_far, gate), (down_far, down)), sems)
    half = w2.shape[0]
    for i, w in enumerate((up, gate, down)):
        copies[i].wait()
        full = w[...].astype(F32)
        norm[i : i + 1, :] = jnp.full((1, 128), jnp.sum(full * full), F32)
    norm[3:8, :] = jnp.zeros((5, 128), F32)
    for c in range(2):

        @pl.when(core[0] == c)
        def _():
            w13[0:half, :] = up[:, c * half : (c + 1) * half].T
            w13[half:, :] = gate[:, c * half : (c + 1) * half].T
            w2[...] = down[c * half : (c + 1) * half, :]


def factor(i, norm, own, oth):
    size = jnp.sqrt(norm[i : i + 1, 0:1])
    total = own[i : i + 1, 0:1] + oth[i : i + 1, 0:1]
    return size / jnp.sqrt(total + 1e-06)


def raw_kernel(w13, w2, keys, targets, raw):
    raw[0 : w13.shape[0], :] = nt(w13[...], keys[...])
    raw[w13.shape[0] :, :] = nt(w2[...], targets[...])


def act_grads(act, lin, err, scale):
    if scale is not None:
        act, lin, err = (x * f for x, f in zip((act, lin, err), scale))
    sig = jax.nn.sigmoid(act)
    silu = act * sig
    hidden = (silu * lin).astype(BF)
    pgrad = (err * lin * sig * (1.0 + act * (1.0 - sig))).astype(BF)
    qgrad = (err * silu).astype(BF)
    return pgrad, qgrad, hidden


def grads_kernel(w13, w2, raw, k_own, k_oth, u_own, u_oth, *rest):
    *state, out = rest
    half = w2.shape[0]
    cols = k_own.shape[1] // 2
    scale = [factor(i, *state) for i in (0, 1, 2)] if state else None
    keys, targets = k_oth[...], u_oth[...]
    oth = act_grads(
        nt(w13[0:half, :], keys), nt(w13[half:, :], keys), nt(w2[...], targets), scale
    )
    own = act_grads(raw[0:half, :], raw[half : 2 * half, :], raw[2 * half :, :], scale)
    for i in range(3):
        x, y = (k_own, k_oth) if i < 2 else (u_own, u_oth)
        for j in range(2):
            at = slice(j * cols, (j + 1) * cols)
            g = dot(own[i], x[:, at]) + dot(oth[i], y[:, at])
            out[j, i * half : (i + 1) * half, :] = g.astype(BF)


ROWS = 16


def update_kernel(w13_far, w2_far, *rest):
    if len(rest) > 8:
        first_far, *state, gathered_far, m13, m2, squares, w13, w2, first, gathered, sems = rest
    else:
        gathered, m13, m2, squares, w13, w2, first, sems = rest
    again = len(rest) > 8
    half = w2.shape[0]
    cols = w2.shape[1] // 2
    pairs = []
    for i in range(3):
        src, dst = (w13_far, w13) if i < 2 else (w2_far, w2)
        rows = slice((i % 2) * half, (i % 2 + 1) * half)
        at = slice(i * half, (i + 1) * half)
        pairs.append((src.at[rows, :], dst.at[rows, :]))
        if again:
            pairs.append((first_far.at[:, at, :], first.at[:, at, :]))
            pairs.append((gathered_far.at[:, at, :], gathered.at[:, at, :]))
    each = len(pairs) // 3
    copies = fetch(pairs, sems)
    for i in range(3):
        src, dst = (w13, m13) if i < 2 else (w2, m2)
        base = (i % 2) * half
        if again:
            scale = jnp.broadcast_to(factor(i, *state), (ROWS, cols))
        for copy in copies[i * each : (i + 1) * each]:
            copy.wait()

        def step(r, total):
            row = pl.multiple_of(base + r * ROWS, ROWS)
            at = pl.multiple_of(i * half + r * ROWS, ROWS)
            for j in range(2):
                side = slice(j * cols, (j + 1) * cols)
                m = src[pl.ds(row, ROWS), side].astype(F32)
                if again:
                    m = (m + first[j, pl.ds(at, ROWS), :].astype(F32)) * scale
                m = m + gathered[j, pl.ds(at, ROWS), :].astype(F32)
                dst[pl.ds(row, ROWS), side] = m.astype(BF)
                total = total + m * m
            return total

        total = lax.fori_loop(0, half // ROWS, step, jnp.zeros((ROWS, cols), F32))
        squares[i : i + 1, :] = jnp.full((1, 128), jnp.sum(total), F32)
    squares[3:8, :] = jnp.zeros((5, 128), F32)


def query_kernel(m13, oth_far, own_far, raw, oth, own, sems):
    copies = fetch(((oth_far, oth), (own_far, own)), sems)
    copies[0].wait()
    raw[0] = nt(m13[...], oth[...])
    copies[1].wait()
    raw[1] = nt(m13[...], own[...])


def hidden_kernel(k, raw, norm, sq_own, sq_oth, hq):
    half = hq.shape[0]
    act = raw[k, 0:half, :] * factor(0, norm, sq_own, sq_oth)
    lin = raw[k, half:, :] * factor(1, norm, sq_own, sq_oth)
    hq[...] = (jax.nn.silu(act) * lin * factor(2, norm, sq_own, sq_oth)).astype(BF)


def piece_kernel(hq_own, hq_got, w2_own, w2_got, o):
    o[...] = (tn(hq_own[...], w2_own[...]) + tn(hq_got[...], w2_got[...])).astype(BF)


def spread_kernel(arrived, out):
    total = arrived[0].astype(F32)
    for i in range(1, arrived.shape[0]):
        total = total + arrived[i].astype(F32)
    rounded = total.astype(BF)
    for i in range(arrived.shape[0]):
        out[i] = rounded


def stage_kernel(after, first_a, first_b, second_a, second_b, first, second, sems):
    rows = first_a.shape[0]
    pairs = [(first_a, first.at[0:rows, :]), (first_b, first.at[rows:, :])]
    pairs += [(second_a, second.at[0:rows, :]), (second_b, second.at[rows:, :])]
    for copy in fetch(pairs, sems):
        copy.wait()


TILE = 512


def partial_kernel(place, o, w_own, out):
    out[...] = dot(o[...], w_own[...])


def partial_product(place, o, w_out):
    tokens, width = o.shape
    n = w_out.shape[1] // 2
    steps = n // TILE
    return pl.pallas_call(
        partial_kernel,
        out_shape=shape((tokens, n), F32),
        grid_spec=pltpu.PrefetchScalarGridSpec(
            num_scalar_prefetch=1,
            grid=(steps,),
            in_specs=[
                pl.BlockSpec((tokens, width), lambda i, s: (0, 0)),
                pl.BlockSpec((width, TILE), lambda i, s: (0, s[0] * steps + i)),
            ],
            out_specs=pl.BlockSpec((tokens, TILE), lambda i, s: (0, i)),
        ),
        compiler_params=pltpu.CompilerParams(vmem_limit_bytes=LIMIT),
        cost_estimate=pl.CostEstimate(
            flops=1 << 20, bytes_accessed=1 << 16, transcendentals=0
        ),
    )(place, o, w_out)


def finish_kernel(place, part, hq_a, hq_b, *rest):
    w2_a, w2_b, w_first, w_second, out, o, held, sems = rest
    half = o.shape[1] // 2
    o[...] = (tn(hq_a[...], w2_a[...]) + tn(hq_b[...], w2_b[...])).astype(BF)
    o_first = o[:, pl.ds(pl.multiple_of(place[1] * half, half), half)]
    o_second = o[:, pl.ds(pl.multiple_of((1 - place[1]) * half, half), half)]
    copies = []
    for j in range(part.shape[1] // TILE):
        at = slice(j * TILE, (j + 1) * TILE)
        total = part[:, at] + dot(o_first, w_first[:, at]) + dot(o_second, w_second[:, at])
        held[j] = total.astype(BF)
        copies.append(pltpu.make_async_copy(held.at[j], out.at[:, at], sems.at[j]))
        copies[-1].start()
    for copy in copies:
        copy.wait()


def finish_product(place, part, hqs, w2s, w_first, w_second):
    tokens, n = part.shape
    width = w2s[0].shape[1]
    return pl.pallas_call(
        finish_kernel,
        out_shape=shape((tokens, n)),
        in_specs=[SMEM] + [VMEM] * 7,
        out_specs=FAR,
        scratch_shapes=[
            buffer((tokens, width)),
            buffer((n // TILE, tokens, TILE)),
            semaphores(n // TILE),
        ],
        compiler_params=pltpu.CompilerParams(vmem_limit_bytes=LIMIT),
        cost_estimate=pl.CostEstimate(
            flops=2 * tokens * width * (n + width // 2), bytes_accessed=6 << 20, transcendentals=0
        ),
    )(place, part, *hqs, *w2s, w_first, w_second)


def all_reduced(grads, beside=None):
    peers = lax.axis_size(CHIPS)
    pieces = grads.reshape(peers, -1, grads.shape[2])
    arrived = lax.all_to_all(pieces, CHIPS, 0, 0, tiled=True)
    copies = call(
        spread_kernel,
        shape(pieces.shape),
        [VMEM],
        pieces.size,
        4 * pieces.size,
    )(arrived)
    if beside is not None:
        beside, _ = lax.optimization_barrier((beside, copies))
    gathered = lax.all_to_all(copies, CHIPS, 0, 0, tiled=True)
    return gathered.reshape(grads.shape), beside


def swap(x):
    return lax.ppermute(x, "c", SWAP)


def shards(queries, keys, values, rates, w_up, w_gate, w_down, w_out):
    width, hid = w_up.shape[1:]
    tokens = keys.shape[0]
    half, third = hid // 2, 3 * hid // 2
    core, head = lax.axis_index("c"), lax.axis_index("h")
    n = w_out.shape[1] // 2

    k_oth = swap(keys)
    targets = (rates * values.astype(F32)).astype(BF)
    u_oth = swap(targets)
    kus = (keys, k_oth, targets, u_oth)

    place = jnp.stack([head, core]).astype(jnp.int32)
    rows = width // 4

    def sent(part):
        return lax.dynamic_slice(
            w_out, ((2 * core + part) * rows, (1 - head) * n), (rows, n)
        )

    w_a = lax.ppermute(sent(0), ("xl", "h"), ACROSS)
    w_b = lax.ppermute(lax.optimization_barrier((sent(1), w_a))[0], ("xl", "h"), ACROSS)

    wshape = (shape((2 * half, width)), shape((half, width)))
    sshape = shape((8, 128), F32)
    scratch = (buffer((width, hid)), buffer((width, hid)), buffer((hid, width)), semaphores(3))
    *w, norm = call(
        prepare_kernel, (*wshape, sshape), [SMEM, FAR, FAR, FAR], 1 << 21, 5 << 20, scratch
    )(core.reshape(1).astype(jnp.int32), w_up[0], w_gate[0], w_down[0])
    flops = 12 * 2 * tokens * width * half
    gdims = (2, third, width // 2)
    pair = [buffer((tokens, width))] * 2
    state, mats = (), w
    for step in range(STEPS):
        raw = call(raw_kernel, shape((third, tokens), F32), [VMEM] * 4, flops // 4, 4 << 20)(
            *mats, keys, targets
        )
        grads = call(
            grads_kernel,
            shape(gdims),
            [VMEM] * (7 + len(state)),
            flops * 3 // 4,
            8 << 20,
        )(*mats, raw, keys, k_oth, targets, u_oth, *state)
        gathered, w_late = all_reduced(grads, (w_a, w_b) if step else None)
        again = () if step == 0 else (first, *state)
        *mats, squares = call(
            update_kernel,
            (*wshape, sshape),
            [FAR] * 2 + ([FAR] + [VMEM] * 3) * step + [ANY if step else NEAR],
            1 << 22,
            5 << 20,
            (
                buffer((2 * half, width)),
                buffer((half, width)),
                buffer(gdims),
                *([buffer(gdims)] * step),
                semaphores(3 + 6 * step),
            ),
        )(*w, *again, gathered)
        first = gathered
        state = (norm, squares, swap(squares))
    crossed = lax.ppermute(mats[1], ("xl", "h"), ACROSS)
    w_parts = (w_a, w_b, *map(swap, w_late))
    q_oth = swap(queries)
    w2_got = swap(mats[1])
    hshape = shape((half, tokens))
    raw = call(
        query_kernel,
        shape((2, 2 * half, tokens), F32),
        [VMEM, ANY, FAR],
        flops // 3,
        5 << 20,
        (*pair, semaphores(2)),
    )(mats[0], q_oth, queries)
    hq_oth, hq_own = (
        call(functools.partial(hidden_kernel, k), hshape, [VMEM] * 4, 1 << 20, 2 << 20)(raw, *state)
        for k in range(2)
    )
    hq_got = swap(hq_oth)
    hqs = [lax.ppermute(x, "h", SWAP) for x in (hq_own, hq_got)]
    o = call(piece_kernel, shape((tokens, width)), [VMEM] * 4, 1 << 20, 1 << 16)(
        hq_own, hq_got, mats[1], w2_got
    )
    part = partial_product(place, o, w_out)
    wide = (shape((width // 2, n)),) * 2
    w_first, w_second = call(stage_kernel, wide, [ANY] * 5, 1 << 16, 1 << 16, [semaphores(4)])(
        hqs[0], *w_parts
    )
    crossed, *hqs, _, _ = lax.optimization_barrier((crossed, *hqs, part, w_first))
    return finish_product(place, part, hqs, (crossed, swap(crossed)), w_first, w_second)


def solution(mesh):
    finer = Mesh(
        mesh.devices.reshape(4, 2, 4, 2, mesh.shape["head"]),
        ("z", "xl", "y", "c", "h"),
    )
    return jax.shard_map(
        shards,
        mesh=finer,
        in_specs=(
            P(CTX, "h"),
            P(CTX, "h"),
            P(CTX, "h"),
            P(CTX, "h"),
            P("h", None, None),
            P("h", None, None),
            P("h", None, None),
            P("h", None),
        ),
        out_specs=P(CTX, "h"),
        check_vma=False,
    )
```

```python
import functools

import jax
import jax.numpy as jnp
from jax import lax
from jax.experimental import pallas as pl
from jax.experimental.pallas import tpu as pltpu
from jax.sharding import Mesh
from jax.sharding import PartitionSpec as P

STEPS = 2
CTX = ("z", "xl", "y", "c")
CHIPS = ("z", "xl", "y")
SWAP = [(0, 1), (1, 0)]
ACROSS = [(0, 3), (3, 0), (1, 2), (2, 1)]
BF = jnp.bfloat16
F32 = jnp.float32
NT = (((1,), (1,)), ((), ()))
TN = (((0,), (0,)), ((), ()))
VMEM = pl.BlockSpec(memory_space=pltpu.VMEM)
SMEM = pl.BlockSpec(memory_space=pltpu.SMEM)
FAR = pl.BlockSpec(memory_space=pltpu.HBM)
ANY = pl.BlockSpec(memory_space=pl.ANY)
NEAR = pl.BlockSpec(memory_space=pltpu.VMEM)
HELD = {id(FAR): pltpu.HBM, id(NEAR): pltpu.VMEM}
LIMIT = 24 * 1024 * 1024


def dot(x, y):
    return jnp.dot(x, y, preferred_element_type=F32)


def nt(x, y):
    return lax.dot_general(x, y, NT, preferred_element_type=F32)


def tn(x, y):
    return lax.dot_general(x, y, TN, preferred_element_type=F32)


def call(kernel, outs, specs, flops, nbytes, scratch=(), far=False):
    if far:
        outs = jax.tree.map(lambda x: pltpu.HBM(x.shape, x.dtype), outs)
    run = pl.pallas_call(
        kernel,
        out_shape=outs,
        in_specs=specs,
        out_specs=jax.tree.map(lambda _: FAR if far else VMEM, outs),
        scratch_shapes=list(scratch),
        compiler_params=pltpu.CompilerParams(vmem_limit_bytes=LIMIT),
        cost_estimate=pl.CostEstimate(flops=flops, bytes_accessed=nbytes, transcendentals=0),
    )

    def with_places(*args):
        return run(
            *(
                pltpu.with_memory_space_constraint(x, HELD[id(spec)]) if id(spec) in HELD else x
                for x, spec in zip(args, specs, strict=True)
            )
        )

    return with_places


def fetch(pairs, sems):
    copies = [pltpu.make_async_copy(src, dst, sems.at[i]) for i, (src, dst) in enumerate(pairs)]
    for copy in copies:
        copy.start()
    return copies


def buffer(dims, dtype=BF):
    return pltpu.VMEM(dims, dtype)


def semaphores(n):
    return pltpu.SemaphoreType.DMA((n,))


def shape(dims, dtype=BF):
    return jax.ShapeDtypeStruct(dims, dtype)


def prepare_kernel(core, up_far, gate_far, down_far, w13, w2, norm, up, gate, down, sems):
    copies = fetch(((up_far, up), (gate_far, gate), (down_far, down)), sems)
    half = w2.shape[0]
    for i, w in enumerate((up, gate, down)):
        copies[i].wait()
        full = w[...].astype(F32)
        norm[i : i + 1, :] = jnp.full((1, 128), jnp.sum(full * full), F32)
    norm[3:8, :] = jnp.zeros((5, 128), F32)
    for c in range(2):

        @pl.when(core[0] == c)
        def _():
            w13[0:half, :] = up[:, c * half : (c + 1) * half].T
            w13[half:, :] = gate[:, c * half : (c + 1) * half].T
            w2[...] = down[c * half : (c + 1) * half, :]


def factor(i, norm, own, oth):
    size = jnp.sqrt(norm[i : i + 1, 0:1])
    total = own[i : i + 1, 0:1] + oth[i : i + 1, 0:1]
    return size / jnp.sqrt(total + 1e-06)


def raw_kernel(w13, w2, keys, targets, raw):
    raw[0 : w13.shape[0], :] = nt(w13[...], keys[...])
    raw[w13.shape[0] :, :] = nt(w2[...], targets[...])


def act_grads(act, lin, err, scale):
    if scale is not None:
        act, lin, err = (x * f for x, f in zip((act, lin, err), scale))
    sig = jax.nn.sigmoid(act)
    silu = act * sig
    hidden = (silu * lin).astype(BF)
    pgrad = (err * lin * sig * (1.0 + act * (1.0 - sig))).astype(BF)
    qgrad = (err * silu).astype(BF)
    return pgrad, qgrad, hidden


def grads_kernel(w13, w2, raw, k_own, k_oth, u_own, u_oth, *rest):
    *state, out = rest
    half = w2.shape[0]
    cols = k_own.shape[1] // 2
    scale = [factor(i, *state) for i in (0, 1, 2)] if state else None
    keys, targets = k_oth[...], u_oth[...]
    oth = act_grads(
        nt(w13[0:half, :], keys), nt(w13[half:, :], keys), nt(w2[...], targets), scale
    )
    own = act_grads(raw[0:half, :], raw[half : 2 * half, :], raw[2 * half :, :], scale)
    for i in range(3):
        x, y = (k_own, k_oth) if i < 2 else (u_own, u_oth)
        for j in range(2):
            at = slice(j * cols, (j + 1) * cols)
            g = dot(own[i], x[:, at]) + dot(oth[i], y[:, at])
            out[j, i * half : (i + 1) * half, :] = g.astype(BF)


ROWS = 16


def update_kernel(w13_far, w2_far, *rest):
    if len(rest) > 8:
        first_far, *state, gathered_far, m13, m2, squares, w13, w2, first, gathered, sems = rest
    else:
        gathered, m13, m2, squares, w13, w2, first, sems = rest
    again = len(rest) > 8
    half = w2.shape[0]
    cols = w2.shape[1] // 2
    pairs = []
    for i in range(3):
        src, dst = (w13_far, w13) if i < 2 else (w2_far, w2)
        rows = slice((i % 2) * half, (i % 2 + 1) * half)
        at = slice(i * half, (i + 1) * half)
        pairs.append((src.at[rows, :], dst.at[rows, :]))
        if again:
            pairs.append((first_far.at[:, at, :], first.at[:, at, :]))
            pairs.append((gathered_far.at[:, at, :], gathered.at[:, at, :]))
    each = len(pairs) // 3
    copies = fetch(pairs, sems)
    for i in range(3):
        src, dst = (w13, m13) if i < 2 else (w2, m2)
        base = (i % 2) * half
        if again:
            scale = jnp.broadcast_to(factor(i, *state), (ROWS, cols))
        for copy in copies[i * each : (i + 1) * each]:
            copy.wait()

        def step(r, total):
            row = pl.multiple_of(base + r * ROWS, ROWS)
            at = pl.multiple_of(i * half + r * ROWS, ROWS)
            for j in range(2):
                side = slice(j * cols, (j + 1) * cols)
                m = src[pl.ds(row, ROWS), side].astype(F32)
                if again:
                    m = (m + first[j, pl.ds(at, ROWS), :].astype(F32)) * scale
                m = m + gathered[j, pl.ds(at, ROWS), :].astype(F32)
                dst[pl.ds(row, ROWS), side] = m.astype(BF)
                total = total + m * m
            return total

        total = lax.fori_loop(0, half // ROWS, step, jnp.zeros((ROWS, cols), F32))
        squares[i : i + 1, :] = jnp.full((1, 128), jnp.sum(total), F32)
    squares[3:8, :] = jnp.zeros((5, 128), F32)


def query_kernel(m13, oth_far, own_far, raw, oth, own, sems):
    copies = fetch(((oth_far, oth), (own_far, own)), sems)
    copies[0].wait()
    raw[0] = nt(m13[...], oth[...])
    copies[1].wait()
    raw[1] = nt(m13[...], own[...])


def hidden_kernel(k, raw, norm, sq_own, sq_oth, hq):
    half = hq.shape[0]
    act = raw[k, 0:half, :] * factor(0, norm, sq_own, sq_oth)
    lin = raw[k, half:, :] * factor(1, norm, sq_own, sq_oth)
    hq[...] = (jax.nn.silu(act) * lin * factor(2, norm, sq_own, sq_oth)).astype(BF)


def piece_kernel(hq_own, hq_got, w2_own, w2_got, o):
    o[...] = (tn(hq_own[...], w2_own[...]) + tn(hq_got[...], w2_got[...])).astype(BF)


def spread_kernel(arrived, out):
    total = arrived[0].astype(F32)
    for i in range(1, arrived.shape[0]):
        total = total + arrived[i].astype(F32)
    rounded = total.astype(BF)
    for i in range(arrived.shape[0]):
        out[i] = rounded


def stage_kernel(after, first_a, first_b, second_a, second_b, first, second, sems):
    rows = first_a.shape[0]
    pairs = [(first_a, first.at[0:rows, :]), (first_b, first.at[rows:, :])]
    pairs += [(second_a, second.at[0:rows, :]), (second_b, second.at[rows:, :])]
    for copy in fetch(pairs, sems):
        copy.wait()


TILE = 512


def partial_kernel(place, o, w_own, out):
    out[...] = dot(o[...], w_own[...])


def partial_product(place, o, w_out):
    tokens, width = o.shape
    n = w_out.shape[1] // 2
    steps = n // TILE
    return pl.pallas_call(
        partial_kernel,
        out_shape=shape((tokens, n), F32),
        grid_spec=pltpu.PrefetchScalarGridSpec(
            num_scalar_prefetch=1,
            grid=(steps,),
            in_specs=[
                pl.BlockSpec((tokens, width), lambda i, s: (0, 0)),
                pl.BlockSpec((width, TILE), lambda i, s: (0, s[0] * steps + i)),
            ],
            out_specs=pl.BlockSpec((tokens, TILE), lambda i, s: (0, i)),
        ),
        compiler_params=pltpu.CompilerParams(vmem_limit_bytes=LIMIT),
        cost_estimate=pl.CostEstimate(
            flops=1 << 20, bytes_accessed=1 << 16, transcendentals=0
        ),
    )(place, o, w_out)


def finish_kernel(place, part, hq_a, hq_b, *rest):
    w2_a, w2_b, w_first, w_second, out, o, held, sems = rest
    half = o.shape[1] // 2
    o[...] = (tn(hq_a[...], w2_a[...]) + tn(hq_b[...], w2_b[...])).astype(BF)
    o_first = o[:, pl.ds(pl.multiple_of(place[1] * half, half), half)]
    o_second = o[:, pl.ds(pl.multiple_of((1 - place[1]) * half, half), half)]
    copies = []
    for j in range(part.shape[1] // TILE):
        at = slice(j * TILE, (j + 1) * TILE)
        total = part[:, at] + dot(o_first, w_first[:, at]) + dot(o_second, w_second[:, at])
        held[j] = total.astype(BF)
        copies.append(pltpu.make_async_copy(held.at[j], out.at[:, at], sems.at[j]))
        copies[-1].start()
    for copy in copies:
        copy.wait()


def finish_product(place, part, hqs, w2s, w_first, w_second):
    tokens, n = part.shape
    width = w2s[0].shape[1]
    return pl.pallas_call(
        finish_kernel,
        out_shape=shape((tokens, n)),
        in_specs=[SMEM] + [VMEM] * 7,
        out_specs=FAR,
        scratch_shapes=[
            buffer((tokens, width)),
            buffer((n // TILE, tokens, TILE)),
            semaphores(n // TILE),
        ],
        compiler_params=pltpu.CompilerParams(vmem_limit_bytes=LIMIT),
        cost_estimate=pl.CostEstimate(
            flops=2 * tokens * width * (n + width // 2), bytes_accessed=6 << 20, transcendentals=0
        ),
    )(place, part, *hqs, *w2s, w_first, w_second)


def all_reduced(grads, beside=None):
    peers = lax.axis_size(CHIPS)
    pieces = grads.reshape(peers, -1, grads.shape[2])
    arrived = lax.all_to_all(pieces, CHIPS, 0, 0, tiled=True)
    copies = call(
        spread_kernel,
        shape(pieces.shape),
        [VMEM],
        pieces.size,
        4 * pieces.size,
    )(arrived)
    if beside is not None:
        beside, _ = lax.optimization_barrier((beside, copies))
    gathered = lax.all_to_all(copies, CHIPS, 0, 0, tiled=True)
    return gathered.reshape(grads.shape), beside


def swap(x):
    return lax.ppermute(x, "c", SWAP)


def shards(queries, keys, values, rates, w_up, w_gate, w_down, w_out):
    width, hid = w_up.shape[1:]
    tokens = keys.shape[0]
    half, third = hid // 2, 3 * hid // 2
    core, head = lax.axis_index("c"), lax.axis_index("h")
    n = w_out.shape[1] // 2

    k_oth = swap(keys)
    targets = (rates * values.astype(F32)).astype(BF)
    u_oth = swap(targets)
    kus = (keys, k_oth, targets, u_oth)

    place = jnp.stack([head, core]).astype(jnp.int32)
    rows = width // 4

    def sent(part):
        return lax.dynamic_slice(
            w_out, ((2 * core + part) * rows, (1 - head) * n), (rows, n)
        )

    w_a = lax.ppermute(sent(0), ("xl", "h"), ACROSS)
    w_b = lax.ppermute(lax.optimization_barrier((sent(1), w_a))[0], ("xl", "h"), ACROSS)

    wshape = (shape((2 * half, width)), shape((half, width)))
    sshape = shape((8, 128), F32)
    scratch = (buffer((width, hid)), buffer((width, hid)), buffer((hid, width)), semaphores(3))
    *w, norm = call(
        prepare_kernel, (*wshape, sshape), [SMEM, FAR, FAR, FAR], 1 << 21, 5 << 20, scratch
    )(core.reshape(1).astype(jnp.int32), w_up[0], w_gate[0], w_down[0])
    flops = 12 * 2 * tokens * width * half
    gdims = (2, third, width // 2)
    pair = [buffer((tokens, width))] * 2
    state, mats = (), w
    for step in range(STEPS):
        raw = call(raw_kernel, shape((third, tokens), F32), [VMEM] * 4, flops // 4, 4 << 20)(
            *mats, keys, targets
        )
        grads = call(
            grads_kernel,
            shape(gdims),
            [VMEM] * (7 + len(state)),
            flops * 3 // 4,
            8 << 20,
        )(*mats, raw, keys, k_oth, targets, u_oth, *state)
        gathered, w_late = all_reduced(grads, (w_a, w_b) if step else None)
        again = () if step == 0 else (first, *state)
        *mats, squares = call(
            update_kernel,
            (*wshape, sshape),
            [FAR] * 2 + ([FAR] + [VMEM] * 3) * step + [ANY if step else NEAR],
            1 << 22,
            5 << 20,
            (
                buffer((2 * half, width)),
                buffer((half, width)),
                buffer(gdims),
                *([buffer(gdims)] * step),
                semaphores(3 + 6 * step),
            ),
        )(*w, *again, gathered)
        first = gathered
        state = (norm, squares, swap(squares))
    crossed = lax.ppermute(mats[1], ("xl", "h"), ACROSS)
    w_parts = (w_a, w_b, *map(swap, w_late))
    q_oth = swap(queries)
    w2_got = swap(mats[1])
    hshape = shape((half, tokens))
    raw = call(
        query_kernel,
        shape((2, 2 * half, tokens), F32),
        [VMEM, ANY, FAR],
        1 << 16,
        1 << 16,
        (*pair, semaphores(2)),
    )(mats[0], q_oth, queries)
    hq_oth, hq_own = (
        call(functools.partial(hidden_kernel, k), hshape, [VMEM] * 4, 1 << 16, 1 << 16)(raw, *state)
        for k in range(2)
    )
    hq_got = swap(hq_oth)
    hqs = [lax.ppermute(x, "h", SWAP) for x in (hq_own, hq_got)]
    o = call(piece_kernel, shape((tokens, width)), [VMEM] * 4, 1 << 20, 1 << 16)(
        hq_own, hq_got, mats[1], w2_got
    )
    part = partial_product(place, lax.optimization_barrier((o, crossed))[0], w_out)
    wide = (shape((width // 2, n)),) * 2
    w_first, w_second = call(stage_kernel, wide, [ANY] * 5, 1 << 16, 1 << 16, [semaphores(4)])(
        o, *w_parts
    )
    crossed, *hqs, _, _ = lax.optimization_barrier((crossed, *hqs, part, w_first))
    return finish_product(place, part, hqs, (crossed, swap(crossed)), w_first, w_second)


def solution(mesh):
    finer = Mesh(
        mesh.devices.reshape(4, 2, 4, 2, mesh.shape["head"]),
        ("z", "xl", "y", "c", "h"),
    )
    return jax.shard_map(
        shards,
        mesh=finer,
        in_specs=(
            P(CTX, "h"),
            P(CTX, "h"),
            P(CTX, "h"),
            P(CTX, "h"),
            P("h", None, None),
            P("h", None, None),
            P("h", None, None),
            P("h", None),
        ),
        out_specs=P(CTX, "h"),
        check_vma=False,
    )
```

```python
import functools

import jax
import jax.numpy as jnp
from jax import lax
from jax.experimental import pallas as pl
from jax.experimental.pallas import tpu as pltpu
from jax.sharding import Mesh
from jax.sharding import PartitionSpec as P

STEPS = 2
CTX = ("z", "xl", "y", "c")
CHIPS = ("z", "xl", "y")
SWAP = [(0, 1), (1, 0)]
ACROSS = [(0, 3), (3, 0), (1, 2), (2, 1)]
BF = jnp.bfloat16
F32 = jnp.float32
NT = (((1,), (1,)), ((), ()))
TN = (((0,), (0,)), ((), ()))
VMEM = pl.BlockSpec(memory_space=pltpu.VMEM)
SMEM = pl.BlockSpec(memory_space=pltpu.SMEM)
FAR = pl.BlockSpec(memory_space=pltpu.HBM)
ANY = pl.BlockSpec(memory_space=pl.ANY)
NEAR = pl.BlockSpec(memory_space=pltpu.VMEM)
HELD = {id(FAR): pltpu.HBM, id(NEAR): pltpu.VMEM}
LIMIT = 24 * 1024 * 1024


def dot(x, y):
    return jnp.dot(x, y, preferred_element_type=F32)


def nt(x, y):
    return lax.dot_general(x, y, NT, preferred_element_type=F32)


def tn(x, y):
    return lax.dot_general(x, y, TN, preferred_element_type=F32)


def call(kernel, outs, specs, flops, nbytes, scratch=(), far=False):
    if far:
        outs = jax.tree.map(lambda x: pltpu.HBM(x.shape, x.dtype), outs)
    run = pl.pallas_call(
        kernel,
        out_shape=outs,
        in_specs=specs,
        out_specs=jax.tree.map(lambda _: FAR if far else VMEM, outs),
        scratch_shapes=list(scratch),
        compiler_params=pltpu.CompilerParams(vmem_limit_bytes=LIMIT),
        cost_estimate=pl.CostEstimate(flops=flops, bytes_accessed=nbytes, transcendentals=0),
    )

    def with_places(*args):
        return run(
            *(
                pltpu.with_memory_space_constraint(x, HELD[id(spec)]) if id(spec) in HELD else x
                for x, spec in zip(args, specs, strict=True)
            )
        )

    return with_places


def fetch(pairs, sems):
    copies = [pltpu.make_async_copy(src, dst, sems.at[i]) for i, (src, dst) in enumerate(pairs)]
    for copy in copies:
        copy.start()
    return copies


def buffer(dims, dtype=BF):
    return pltpu.VMEM(dims, dtype)


def semaphores(n):
    return pltpu.SemaphoreType.DMA((n,))


def shape(dims, dtype=BF):
    return jax.ShapeDtypeStruct(dims, dtype)


def prepare_kernel(core, up_far, gate_far, down_far, w13, w2, norm, up, gate, down, sems):
    copies = fetch(((up_far, up), (gate_far, gate), (down_far, down)), sems)
    half = w2.shape[0]
    for i, w in enumerate((up, gate, down)):
        copies[i].wait()
        full = w[...].astype(F32)
        norm[i : i + 1, :] = jnp.full((1, 128), jnp.sum(full * full), F32)
    norm[3:8, :] = jnp.zeros((5, 128), F32)
    for c in range(2):

        @pl.when(core[0] == c)
        def _():
            w13[0:half, :] = up[:, c * half : (c + 1) * half].T
            w13[half:, :] = gate[:, c * half : (c + 1) * half].T
            w2[...] = down[c * half : (c + 1) * half, :]


def factor(i, norm, own, oth):
    size = jnp.sqrt(norm[i : i + 1, 0:1])
    total = own[i : i + 1, 0:1] + oth[i : i + 1, 0:1]
    return size / jnp.sqrt(total + 1e-06)


def raw_kernel(w13, w2, keys, targets, raw):
    raw[0 : w13.shape[0], :] = nt(w13[...], keys[...])
    raw[w13.shape[0] :, :] = nt(w2[...], targets[...])


def act_grads(act, lin, err, scale):
    if scale is not None:
        act, lin, err = (x * f for x, f in zip((act, lin, err), scale))
    sig = jax.nn.sigmoid(act)
    silu = act * sig
    hidden = (silu * lin).astype(BF)
    pgrad = (err * lin * sig * (1.0 + act * (1.0 - sig))).astype(BF)
    qgrad = (err * silu).astype(BF)
    return pgrad, qgrad, hidden


def grads_kernel(w13, w2, raw, k_own, k_oth, u_own, u_oth, *rest):
    *state, out = rest
    half = w2.shape[0]
    cols = k_own.shape[1] // 2
    scale = [factor(i, *state) for i in (0, 1, 2)] if state else None
    keys, targets = k_oth[...], u_oth[...]
    oth = act_grads(
        nt(w13[0:half, :], keys), nt(w13[half:, :], keys), nt(w2[...], targets), scale
    )
    own = act_grads(raw[0:half, :], raw[half : 2 * half, :], raw[2 * half :, :], scale)
    for i in range(3):
        x, y = (k_own, k_oth) if i < 2 else (u_own, u_oth)
        for j in range(2):
            at = slice(j * cols, (j + 1) * cols)
            g = dot(own[i], x[:, at]) + dot(oth[i], y[:, at])
            out[j, i * half : (i + 1) * half, :] = g.astype(BF)


ROWS = 16


def update_kernel(w13_far, w2_far, *rest):
    if len(rest) > 8:
        first_far, *state, gathered_far, m13, m2, squares, w13, w2, first, gathered, sems = rest
    else:
        gathered, m13, m2, squares, w13, w2, first, sems = rest
    again = len(rest) > 8
    half = w2.shape[0]
    cols = w2.shape[1] // 2
    pairs = []
    for i in range(3):
        src, dst = (w13_far, w13) if i < 2 else (w2_far, w2)
        rows = slice((i % 2) * half, (i % 2 + 1) * half)
        at = slice(i * half, (i + 1) * half)
        pairs.append((src.at[rows, :], dst.at[rows, :]))
        if again:
            pairs.append((first_far.at[:, at, :], first.at[:, at, :]))
            pairs.append((gathered_far.at[:, at, :], gathered.at[:, at, :]))
    each = len(pairs) // 3
    copies = fetch(pairs, sems)
    for i in range(3):
        src, dst = (w13, m13) if i < 2 else (w2, m2)
        base = (i % 2) * half
        if again:
            scale = jnp.broadcast_to(factor(i, *state), (ROWS, cols))
        for copy in copies[i * each : (i + 1) * each]:
            copy.wait()

        def step(r, total):
            row = pl.multiple_of(base + r * ROWS, ROWS)
            at = pl.multiple_of(i * half + r * ROWS, ROWS)
            for j in range(2):
                side = slice(j * cols, (j + 1) * cols)
                m = src[pl.ds(row, ROWS), side].astype(F32)
                if again:
                    m = (m + first[j, pl.ds(at, ROWS), :].astype(F32)) * scale
                m = m + gathered[j, pl.ds(at, ROWS), :].astype(F32)
                dst[pl.ds(row, ROWS), side] = m.astype(BF)
                total = total + m * m
            return total

        total = lax.fori_loop(0, half // ROWS, step, jnp.zeros((ROWS, cols), F32))
        squares[i : i + 1, :] = jnp.full((1, 128), jnp.sum(total), F32)
    squares[3:8, :] = jnp.zeros((5, 128), F32)


def query_kernel(m13, oth_far, own_far, raw, oth, own, sems):
    copies = fetch(((oth_far, oth), (own_far, own)), sems)
    copies[0].wait()
    raw[0] = nt(m13[...], oth[...])
    copies[1].wait()
    raw[1] = nt(m13[...], own[...])


def hidden_kernel(k, raw, norm, sq_own, sq_oth, hq):
    half = hq.shape[0]
    act = raw[k, 0:half, :] * factor(0, norm, sq_own, sq_oth)
    lin = raw[k, half:, :] * factor(1, norm, sq_own, sq_oth)
    hq[...] = (jax.nn.silu(act) * lin * factor(2, norm, sq_own, sq_oth)).astype(BF)


def piece_kernel(hq_own, hq_got, w2_own, w2_got, o):
    o[...] = (tn(hq_own[...], w2_own[...]) + tn(hq_got[...], w2_got[...])).astype(BF)


def spread_kernel(arrived, out):
    total = arrived[0].astype(F32)
    for i in range(1, arrived.shape[0]):
        total = total + arrived[i].astype(F32)
    rounded = total.astype(BF)
    for i in range(arrived.shape[0]):
        out[i] = rounded


def stage_kernel(after, first_a, first_b, second_a, second_b, first, second, sems):
    rows = first_a.shape[0]
    pairs = [(first_a, first.at[0:rows, :]), (first_b, first.at[rows:, :])]
    pairs += [(second_a, second.at[0:rows, :]), (second_b, second.at[rows:, :])]
    for copy in fetch(pairs, sems):
        copy.wait()


TILE = 512


def partial_kernel(place, o, w_own, out):
    out[...] = dot(o[...], w_own[...])


def partial_product(place, o, w_out):
    tokens, width = o.shape
    n = w_out.shape[1] // 2
    steps = n // TILE
    return pl.pallas_call(
        partial_kernel,
        out_shape=shape((tokens, n), F32),
        grid_spec=pltpu.PrefetchScalarGridSpec(
            num_scalar_prefetch=1,
            grid=(steps,),
            in_specs=[
                pl.BlockSpec((tokens, width), lambda i, s: (0, 0)),
                pl.BlockSpec((width, TILE), lambda i, s: (0, s[0] * steps + i)),
            ],
            out_specs=pl.BlockSpec((tokens, TILE), lambda i, s: (0, i)),
        ),
        compiler_params=pltpu.CompilerParams(vmem_limit_bytes=LIMIT),
        cost_estimate=pl.CostEstimate(
            flops=1 << 20, bytes_accessed=1 << 16, transcendentals=0
        ),
    )(place, o, w_out)


def finish_kernel(place, part, hq_a, hq_b, *rest):
    w2_a, w2_b, w_first, w_second, out, o, held, sems = rest
    half = o.shape[1] // 2
    o[...] = (tn(hq_a[...], w2_a[...]) + tn(hq_b[...], w2_b[...])).astype(BF)
    o_first = o[:, pl.ds(pl.multiple_of(place[1] * half, half), half)]
    o_second = o[:, pl.ds(pl.multiple_of((1 - place[1]) * half, half), half)]
    copies = []
    for j in range(part.shape[1] // TILE):
        at = slice(j * TILE, (j + 1) * TILE)
        total = part[:, at] + dot(o_first, w_first[:, at]) + dot(o_second, w_second[:, at])
        held[j] = total.astype(BF)
        copies.append(pltpu.make_async_copy(held.at[j], out.at[:, at], sems.at[j]))
        copies[-1].start()
    for copy in copies:
        copy.wait()


def finish_product(place, part, hqs, w2s, w_first, w_second):
    tokens, n = part.shape
    width = w2s[0].shape[1]
    return pl.pallas_call(
        finish_kernel,
        out_shape=shape((tokens, n)),
        in_specs=[SMEM] + [VMEM] * 7,
        out_specs=FAR,
        scratch_shapes=[
            buffer((tokens, width)),
            buffer((n // TILE, tokens, TILE)),
            semaphores(n // TILE),
        ],
        compiler_params=pltpu.CompilerParams(vmem_limit_bytes=LIMIT),
        cost_estimate=pl.CostEstimate(
            flops=2 * tokens * width * (n + width // 2), bytes_accessed=6 << 20, transcendentals=0
        ),
    )(place, part, *hqs, *w2s, w_first, w_second)


def all_reduced(grads, beside=None):
    peers = lax.axis_size(CHIPS)
    pieces = grads.reshape(peers, -1, grads.shape[2])
    arrived = lax.all_to_all(pieces, CHIPS, 0, 0, tiled=True)
    copies = call(
        spread_kernel,
        shape(pieces.shape),
        [VMEM],
        pieces.size,
        4 * pieces.size,
    )(arrived)
    if beside is not None:
        beside, _ = lax.optimization_barrier((beside, copies))
    gathered = lax.all_to_all(copies, CHIPS, 0, 0, tiled=True)
    return gathered.reshape(grads.shape), beside


def swap(x):
    return lax.ppermute(x, "c", SWAP)


def shards(queries, keys, values, rates, w_up, w_gate, w_down, w_out):
    width, hid = w_up.shape[1:]
    tokens = keys.shape[0]
    half, third = hid // 2, 3 * hid // 2
    core, head = lax.axis_index("c"), lax.axis_index("h")
    n = w_out.shape[1] // 2

    k_oth = swap(keys)
    targets = (rates * values.astype(F32)).astype(BF)
    u_oth = swap(targets)
    kus = (keys, k_oth, targets, u_oth)

    place = jnp.stack([head, core]).astype(jnp.int32)
    rows = width // 4

    def sent(part):
        return lax.dynamic_slice(
            w_out, ((2 * core + part) * rows, (1 - head) * n), (rows, n)
        )

    w_a = lax.ppermute(sent(0), ("xl", "h"), ACROSS)
    w_b = lax.ppermute(lax.optimization_barrier((sent(1), w_a))[0], ("xl", "h"), ACROSS)

    wshape = (shape((2 * half, width)), shape((half, width)))
    sshape = shape((8, 128), F32)
    scratch = (buffer((width, hid)), buffer((width, hid)), buffer((hid, width)), semaphores(3))
    *w, norm = call(
        prepare_kernel, (*wshape, sshape), [SMEM, FAR, FAR, FAR], 1 << 21, 5 << 20, scratch
    )(core.reshape(1).astype(jnp.int32), w_up[0], w_gate[0], w_down[0])
    flops = 12 * 2 * tokens * width * half
    gdims = (2, third, width // 2)
    pair = [buffer((tokens, width))] * 2
    state, mats = (), w
    for step in range(STEPS):
        raw = call(raw_kernel, shape((third, tokens), F32), [VMEM] * 4, flops // 4, 4 << 20)(
            *mats, keys, targets
        )
        grads = call(
            grads_kernel,
            shape(gdims),
            [VMEM] * (7 + len(state)),
            flops * 3 // 4,
            8 << 20,
        )(*mats, raw, keys, k_oth, targets, u_oth, *state)
        gathered, w_late = all_reduced(grads, (w_a, w_b) if step else None)
        again = () if step == 0 else (first, *state)
        *mats, squares = call(
            update_kernel,
            (*wshape, sshape),
            [FAR] * 2 + ([FAR] + [VMEM] * 3) * step + [ANY if step else NEAR],
            1 << 22,
            5 << 20,
            (
                buffer((2 * half, width)),
                buffer((half, width)),
                buffer(gdims),
                *([buffer(gdims)] * step),
                semaphores(3 + 6 * step),
            ),
        )(*w, *again, gathered)
        first = gathered
        state = (norm, squares, swap(squares))
    crossed = lax.ppermute(mats[1], ("xl", "h"), ACROSS)
    w_parts = (w_a, w_b, *map(swap, w_late))
    q_oth = swap(queries)
    w2_got = swap(mats[1])
    hshape = shape((half, tokens))
    raw = call(
        query_kernel,
        shape((2, 2 * half, tokens), F32),
        [VMEM, ANY, FAR],
        1 << 16,
        1 << 16,
        (*pair, semaphores(2)),
    )(mats[0], q_oth, queries)
    hq_oth, hq_own = (
        call(functools.partial(hidden_kernel, k), hshape, [VMEM] * 4, 1 << 16, 1 << 16)(raw, *state)
        for k in range(2)
    )
    hq_got = swap(hq_oth)
    hqs = [lax.ppermute(x, "h", SWAP) for x in (hq_own, hq_got)]
    o = call(piece_kernel, shape((tokens, width)), [VMEM] * 4, 1 << 20, 1 << 16)(
        hq_own, hq_got, mats[1], w2_got
    )
    part = partial_product(place, o, w_out)
    wide = (shape((width // 2, n)),) * 2
    w_first, w_second = call(stage_kernel, wide, [ANY] * 5, 1 << 16, 1 << 16, [semaphores(4)])(
        hq_got, *w_parts
    )
    crossed, *hqs, _, _ = lax.optimization_barrier((crossed, *hqs, part, w_first))
    return finish_product(place, part, hqs, (crossed, swap(crossed)), w_first, w_second)


def solution(mesh):
    finer = Mesh(
        mesh.devices.reshape(4, 2, 4, 2, mesh.shape["head"]),
        ("z", "xl", "y", "c", "h"),
    )
    return jax.shard_map(
        shards,
        mesh=finer,
        in_specs=(
            P(CTX, "h"),
            P(CTX, "h"),
            P(CTX, "h"),
            P(CTX, "h"),
            P("h", None, None),
            P("h", None, None),
            P("h", None, None),
            P("h", None),
        ),
        out_specs=P(CTX, "h"),
        check_vma=False,
    )
```

```python
import functools

import jax
import jax.numpy as jnp
from jax import lax
from jax.experimental import pallas as pl
from jax.experimental.pallas import tpu as pltpu
from jax.sharding import Mesh
from jax.sharding import PartitionSpec as P

STEPS = 2
CTX = ("z", "xl", "y", "c")
CHIPS = ("z", "xl", "y")
SWAP = [(0, 1), (1, 0)]
ACROSS = [(0, 3), (3, 0), (1, 2), (2, 1)]
BF = jnp.bfloat16
F32 = jnp.float32
NT = (((1,), (1,)), ((), ()))
TN = (((0,), (0,)), ((), ()))
VMEM = pl.BlockSpec(memory_space=pltpu.VMEM)
SMEM = pl.BlockSpec(memory_space=pltpu.SMEM)
FAR = pl.BlockSpec(memory_space=pltpu.HBM)
ANY = pl.BlockSpec(memory_space=pl.ANY)
NEAR = pl.BlockSpec(memory_space=pltpu.VMEM)
HELD = {id(FAR): pltpu.HBM, id(NEAR): pltpu.VMEM}
LIMIT = 24 * 1024 * 1024


def dot(x, y):
    return jnp.dot(x, y, preferred_element_type=F32)


def nt(x, y):
    return lax.dot_general(x, y, NT, preferred_element_type=F32)


def tn(x, y):
    return lax.dot_general(x, y, TN, preferred_element_type=F32)


def call(kernel, outs, specs, flops, nbytes, scratch=(), far=False):
    if far:
        outs = jax.tree.map(lambda x: pltpu.HBM(x.shape, x.dtype), outs)
    run = pl.pallas_call(
        kernel,
        out_shape=outs,
        in_specs=specs,
        out_specs=jax.tree.map(lambda _: FAR if far else VMEM, outs),
        scratch_shapes=list(scratch),
        compiler_params=pltpu.CompilerParams(vmem_limit_bytes=LIMIT),
        cost_estimate=pl.CostEstimate(flops=flops, bytes_accessed=nbytes, transcendentals=0),
    )

    def with_places(*args):
        return run(
            *(
                pltpu.with_memory_space_constraint(x, HELD[id(spec)]) if id(spec) in HELD else x
                for x, spec in zip(args, specs, strict=True)
            )
        )

    return with_places


def fetch(pairs, sems):
    copies = [pltpu.make_async_copy(src, dst, sems.at[i]) for i, (src, dst) in enumerate(pairs)]
    for copy in copies:
        copy.start()
    return copies


def buffer(dims, dtype=BF):
    return pltpu.VMEM(dims, dtype)


def semaphores(n):
    return pltpu.SemaphoreType.DMA((n,))


def shape(dims, dtype=BF):
    return jax.ShapeDtypeStruct(dims, dtype)


def prepare_kernel(core, up_far, gate_far, down_far, w13, w2, norm, up, gate, down, sems):
    copies = fetch(((up_far, up), (gate_far, gate), (down_far, down)), sems)
    half = w2.shape[0]
    for i, w in enumerate((up, gate, down)):
        copies[i].wait()
        full = w[...].astype(F32)
        norm[i : i + 1, :] = jnp.full((1, 128), jnp.sum(full * full), F32)
    norm[3:8, :] = jnp.zeros((5, 128), F32)
    for c in range(2):

        @pl.when(core[0] == c)
        def _():
            w13[0:half, :] = up[:, c * half : (c + 1) * half].T
            w13[half:, :] = gate[:, c * half : (c + 1) * half].T
            w2[...] = down[c * half : (c + 1) * half, :]


def factor(i, norm, own, oth):
    size = jnp.sqrt(norm[i : i + 1, 0:1])
    total = own[i : i + 1, 0:1] + oth[i : i + 1, 0:1]
    return size / jnp.sqrt(total + 1e-06)


def raw_kernel(w13, w2, keys, targets, raw):
    raw[0 : w13.shape[0], :] = nt(w13[...], keys[...])
    raw[w13.shape[0] :, :] = nt(w2[...], targets[...])


def act_grads(act, lin, err, scale):
    if scale is not None:
        act, lin, err = (x * f for x, f in zip((act, lin, err), scale))
    sig = jax.nn.sigmoid(act)
    silu = act * sig
    hidden = (silu * lin).astype(BF)
    pgrad = (err * lin * sig * (1.0 + act * (1.0 - sig))).astype(BF)
    qgrad = (err * silu).astype(BF)
    return pgrad, qgrad, hidden


def grads_kernel(w13, w2, raw, k_own, k_oth, u_own, u_oth, *rest):
    *state, out = rest
    half = w2.shape[0]
    cols = k_own.shape[1] // 2
    scale = [factor(i, *state) for i in (0, 1, 2)] if state else None
    keys, targets = k_oth[...], u_oth[...]
    oth = act_grads(
        nt(w13[0:half, :], keys), nt(w13[half:, :], keys), nt(w2[...], targets), scale
    )
    own = act_grads(raw[0:half, :], raw[half : 2 * half, :], raw[2 * half :, :], scale)
    for i in range(3):
        x, y = (k_own, k_oth) if i < 2 else (u_own, u_oth)
        for j in range(2):
            at = slice(j * cols, (j + 1) * cols)
            g = dot(own[i], x[:, at]) + dot(oth[i], y[:, at])
            out[j, i * half : (i + 1) * half, :] = g.astype(BF)


ROWS = 16


def moved_rows(i, base, src, terms, scale, dst, cols, half):
    def step(r, total):
        row = pl.multiple_of(base + r * ROWS, ROWS)
        at = pl.multiple_of(i * half + r * ROWS, ROWS)
        for j in range(2):
            side = slice(j * cols, (j + 1) * cols)
            m = src[pl.ds(row, ROWS), side].astype(F32)
            m = m + terms[0][j, pl.ds(at, ROWS), :].astype(F32)
            if scale is not None:
                m = m * scale + terms[1][j, pl.ds(at, ROWS), :].astype(F32)
            dst[pl.ds(row, ROWS), side] = m.astype(BF)
            total = total + m * m
        return total

    total = lax.fori_loop(0, half // ROWS, step, jnp.zeros((ROWS, cols), F32))
    return jnp.full((1, 128), jnp.sum(total), F32)


def update_kernel(w13_far, w2_far, gathered, m13, m2, squares, w13, w2, sems):
    half = w2.shape[0]
    cols = w2.shape[1] // 2
    pairs = [(w13_far.at[r, :], w13.at[r, :]) for r in (slice(0, half), slice(half, 2 * half))]
    copies = fetch([*pairs, (w2_far, w2)], sems)
    for i in range(3):
        src, dst = (w13, m13) if i < 2 else (w2, m2)
        copies[i].wait()
        squares[i : i + 1, :] = moved_rows(
            i, (i % 2) * half, src, (gathered,), None, dst, cols, half
        )
    squares[3:8, :] = jnp.zeros((5, 128), F32)


def later_kernel(parts, w_far, first_far, norm, own, oth, gathered_far, *rest):
    *before, m, squares, w, first, gathered, sems = rest
    half = w.shape[0] // len(parts)
    cols = w.shape[1] // 2
    pairs = []
    for k, i in enumerate(parts):
        rows, at = slice(k * half, (k + 1) * half), slice(i * half, (i + 1) * half)
        pairs.append((w_far.at[rows, :], w.at[rows, :]))
        pairs.append((first_far.at[:, at, :], first.at[:, at, :]))
        pairs.append((gathered_far.at[:, at, :], gathered.at[:, at, :]))
    copies = fetch(pairs, sems)
    squares[...] = before[0][...] if before else jnp.zeros(squares.shape, F32)
    for k, i in enumerate(parts):
        scale = jnp.broadcast_to(factor(i, norm, own, oth), (ROWS, cols))
        for copy in copies[3 * k : 3 * k + 3]:
            copy.wait()
        squares[i : i + 1, :] = moved_rows(
            i, k * half, w, (first, gathered), scale, m, cols, half
        )


def query_kernel(m13, oth_far, own_far, raw, oth, own, sems):
    copies = fetch(((oth_far, oth), (own_far, own)), sems)
    copies[0].wait()
    raw[0] = nt(m13[...], oth[...])
    copies[1].wait()
    raw[1] = nt(m13[...], own[...])


def hidden_kernel(k, raw, norm, sq_own, sq_oth, hq):
    half = hq.shape[0]
    act = raw[k, 0:half, :] * factor(0, norm, sq_own, sq_oth)
    lin = raw[k, half:, :] * factor(1, norm, sq_own, sq_oth)
    hq[...] = (jax.nn.silu(act) * lin * factor(2, norm, sq_own, sq_oth)).astype(BF)


def piece_kernel(hq_own, hq_got, w2_own, w2_got, o):
    o[...] = (tn(hq_own[...], w2_own[...]) + tn(hq_got[...], w2_got[...])).astype(BF)


def spread_kernel(arrived, out):
    total = arrived[0].astype(F32)
    for i in range(1, arrived.shape[0]):
        total = total + arrived[i].astype(F32)
    rounded = total.astype(BF)
    for i in range(arrived.shape[0]):
        out[i] = rounded


def stage_kernel(after, first_a, first_b, second_a, second_b, first, second, sems):
    rows = first_a.shape[0]
    pairs = [(first_a, first.at[0:rows, :]), (first_b, first.at[rows:, :])]
    pairs += [(second_a, second.at[0:rows, :]), (second_b, second.at[rows:, :])]
    for copy in fetch(pairs, sems):
        copy.wait()


TILE = 512


def partial_kernel(place, o, w_own, out):
    out[...] = dot(o[...], w_own[...])


def partial_product(place, o, w_out):
    tokens, width = o.shape
    n = w_out.shape[1] // 2
    steps = n // TILE
    return pl.pallas_call(
        partial_kernel,
        out_shape=shape((tokens, n), F32),
        grid_spec=pltpu.PrefetchScalarGridSpec(
            num_scalar_prefetch=1,
            grid=(steps,),
            in_specs=[
                pl.BlockSpec((tokens, width), lambda i, s: (0, 0)),
                pl.BlockSpec((width, TILE), lambda i, s: (0, s[0] * steps + i)),
            ],
            out_specs=pl.BlockSpec((tokens, TILE), lambda i, s: (0, i)),
        ),
        compiler_params=pltpu.CompilerParams(vmem_limit_bytes=LIMIT),
        cost_estimate=pl.CostEstimate(
            flops=1 << 20, bytes_accessed=1 << 16, transcendentals=0
        ),
    )(place, o, w_out)


def finish_kernel(place, part, hq_a, hq_b, *rest):
    w2_a, w2_b, w_first, w_second, out, o, held, sems = rest
    half = o.shape[1] // 2
    o[...] = (tn(hq_a[...], w2_a[...]) + tn(hq_b[...], w2_b[...])).astype(BF)
    o_first = o[:, pl.ds(pl.multiple_of(place[1] * half, half), half)]
    o_second = o[:, pl.ds(pl.multiple_of((1 - place[1]) * half, half), half)]
    copies = []
    for j in range(part.shape[1] // TILE):
        at = slice(j * TILE, (j + 1) * TILE)
        total = part[:, at] + dot(o_first, w_first[:, at]) + dot(o_second, w_second[:, at])
        held[j] = total.astype(BF)
        copies.append(pltpu.make_async_copy(held.at[j], out.at[:, at], sems.at[j]))
        copies[-1].start()
    for copy in copies:
        copy.wait()


def finish_product(place, part, hqs, w2s, w_first, w_second):
    tokens, n = part.shape
    width = w2s[0].shape[1]
    return pl.pallas_call(
        finish_kernel,
        out_shape=shape((tokens, n)),
        in_specs=[SMEM] + [VMEM] * 7,
        out_specs=FAR,
        scratch_shapes=[
            buffer((tokens, width)),
            buffer((n // TILE, tokens, TILE)),
            semaphores(n // TILE),
        ],
        compiler_params=pltpu.CompilerParams(vmem_limit_bytes=LIMIT),
        cost_estimate=pl.CostEstimate(
            flops=2 * tokens * width * (n + width // 2), bytes_accessed=6 << 20, transcendentals=0
        ),
    )(place, part, *hqs, *w2s, w_first, w_second)


def all_reduced(grads, beside=None):
    peers = lax.axis_size(CHIPS)
    pieces = grads.reshape(peers, -1, grads.shape[2])
    arrived = lax.all_to_all(pieces, CHIPS, 0, 0, tiled=True)
    copies = call(
        spread_kernel,
        shape(pieces.shape),
        [VMEM],
        pieces.size,
        4 * pieces.size,
    )(arrived)
    if beside is not None:
        beside, _ = lax.optimization_barrier((beside, copies))
    gathered = lax.all_to_all(copies, CHIPS, 0, 0, tiled=True)
    return gathered.reshape(grads.shape), beside


def swap(x):
    return lax.ppermute(x, "c", SWAP)


def shards(queries, keys, values, rates, w_up, w_gate, w_down, w_out):
    width, hid = w_up.shape[1:]
    tokens = keys.shape[0]
    half, third = hid // 2, 3 * hid // 2
    core, head = lax.axis_index("c"), lax.axis_index("h")
    n = w_out.shape[1] // 2

    k_oth = swap(keys)
    targets = (rates * values.astype(F32)).astype(BF)
    u_oth = swap(targets)
    kus = (keys, k_oth, targets, u_oth)

    place = jnp.stack([head, core]).astype(jnp.int32)
    rows = width // 4

    def sent(part):
        return lax.dynamic_slice(
            w_out, ((2 * core + part) * rows, (1 - head) * n), (rows, n)
        )

    w_a = lax.ppermute(sent(0), ("xl", "h"), ACROSS)
    w_b = lax.ppermute(lax.optimization_barrier((sent(1), w_a))[0], ("xl", "h"), ACROSS)

    wshape = (shape((2 * half, width)), shape((half, width)))
    sshape = shape((8, 128), F32)
    scratch = (buffer((width, hid)), buffer((width, hid)), buffer((hid, width)), semaphores(3))
    *w, norm = call(
        prepare_kernel, (*wshape, sshape), [SMEM, FAR, FAR, FAR], 1 << 21, 5 << 20, scratch
    )(core.reshape(1).astype(jnp.int32), w_up[0], w_gate[0], w_down[0])
    flops = 12 * 2 * tokens * width * half
    gdims = (2, third, width // 2)
    pair = [buffer((tokens, width))] * 2
    state, mats = (), w
    for step in range(STEPS):
        raw = call(raw_kernel, shape((third, tokens), F32), [VMEM] * 4, flops // 4, 4 << 20)(
            *mats, keys, targets
        )
        grads = call(
            grads_kernel,
            shape(gdims),
            [VMEM] * (7 + len(state)),
            flops * 3 // 4,
            8 << 20,
        )(*mats, raw, keys, k_oth, targets, u_oth, *state)
        gathered, w_late = all_reduced(grads, (w_a, w_b) if step else None)
        if step == 0:
            *mats, squares = call(
                update_kernel,
                (*wshape, sshape),
                [FAR] * 2 + [NEAR],
                1 << 22,
                5 << 20,
                (buffer((2 * half, width)), buffer((half, width)), semaphores(3)),
            )(*w, gathered)
            first = gathered
        else:
            before, mats = (), []
            for k, parts in ((1, (2,)), (0, (0, 1))):
                m, *before = call(
                    functools.partial(later_kernel, parts),
                    (wshape[k], sshape),
                    [FAR] * 2 + [VMEM] * 3 + [ANY] + [VMEM] * len(before),
                    1 << 20,
                    1 << 20,
                    (
                        buffer(wshape[k].shape),
                        buffer(gdims),
                        buffer(gdims),
                        semaphores(3 * len(parts)),
                    ),
                )(w[k], first, *state, gathered, *before)
                mats.insert(0, m)
            squares = before[0]
        state = (norm, squares, swap(squares))
    crossed = lax.ppermute(mats[1], ("xl", "h"), ACROSS)
    w_parts = (w_a, w_b, *map(swap, w_late))
    q_oth = swap(queries)
    w2_got = swap(mats[1])
    hshape = shape((half, tokens))
    raw = call(
        query_kernel,
        shape((2, 2 * half, tokens), F32),
        [VMEM, ANY, FAR],
        flops // 3,
        5 << 20,
        (*pair, semaphores(2)),
    )(mats[0], q_oth, queries)
    hq_oth, hq_own = (
        call(functools.partial(hidden_kernel, k), hshape, [VMEM] * 4, 1 << 20, 2 << 20)(raw, *state)
        for k in range(2)
    )
    hq_got = swap(hq_oth)
    hqs = [lax.ppermute(x, "h", SWAP) for x in (hq_own, hq_got)]
    o = call(piece_kernel, shape((tokens, width)), [VMEM] * 4, 1 << 20, 1 << 16)(
        hq_own, hq_got, mats[1], w2_got
    )
    part = partial_product(place, o, w_out)
    wide = (shape((width // 2, n)),) * 2
    w_first, w_second = call(stage_kernel, wide, [ANY] * 5, 1 << 16, 1 << 16, [semaphores(4)])(
        hq_got, *w_parts
    )
    crossed, *hqs, _, _ = lax.optimization_barrier((crossed, *hqs, part, w_first))
    return finish_product(place, part, hqs, (crossed, swap(crossed)), w_first, w_second)


def solution(mesh):
    finer = Mesh(
        mesh.devices.reshape(4, 2, 4, 2, mesh.shape["head"]),
        ("z", "xl", "y", "c", "h"),
    )
    return jax.shard_map(
        shards,
        mesh=finer,
        in_specs=(
            P(CTX, "h"),
            P(CTX, "h"),
            P(CTX, "h"),
            P(CTX, "h"),
            P("h", None, None),
            P("h", None, None),
            P("h", None, None),
            P("h", None),
        ),
        out_specs=P(CTX, "h"),
        check_vma=False,
    )
```

```python
import functools

import jax
import jax.numpy as jnp
from jax import lax
from jax.experimental import pallas as pl
from jax.experimental.pallas import tpu as pltpu
from jax.sharding import Mesh
from jax.sharding import PartitionSpec as P

STEPS = 2
CTX = ("z", "xl", "y", "c")
CHIPS = ("z", "xl", "y")
SWAP = [(0, 1), (1, 0)]
ACROSS = [(0, 3), (3, 0), (1, 2), (2, 1)]
BF = jnp.bfloat16
F32 = jnp.float32
NT = (((1,), (1,)), ((), ()))
TN = (((0,), (0,)), ((), ()))
VMEM = pl.BlockSpec(memory_space=pltpu.VMEM)
SMEM = pl.BlockSpec(memory_space=pltpu.SMEM)
FAR = pl.BlockSpec(memory_space=pltpu.HBM)
ANY = pl.BlockSpec(memory_space=pl.ANY)
NEAR = pl.BlockSpec(memory_space=pltpu.VMEM)
HELD = {id(FAR): pltpu.HBM, id(NEAR): pltpu.VMEM}
LIMIT = 24 * 1024 * 1024


def dot(x, y):
    return jnp.dot(x, y, preferred_element_type=F32)


def nt(x, y):
    return lax.dot_general(x, y, NT, preferred_element_type=F32)


def tn(x, y):
    return lax.dot_general(x, y, TN, preferred_element_type=F32)


def call(kernel, outs, specs, flops, nbytes, scratch=(), far=False):
    if far:
        outs = jax.tree.map(lambda x: pltpu.HBM(x.shape, x.dtype), outs)
    run = pl.pallas_call(
        kernel,
        out_shape=outs,
        in_specs=specs,
        out_specs=jax.tree.map(lambda _: FAR if far else VMEM, outs),
        scratch_shapes=list(scratch),
        compiler_params=pltpu.CompilerParams(vmem_limit_bytes=LIMIT),
        cost_estimate=pl.CostEstimate(flops=flops, bytes_accessed=nbytes, transcendentals=0),
    )

    def with_places(*args):
        return run(
            *(
                pltpu.with_memory_space_constraint(x, HELD[id(spec)]) if id(spec) in HELD else x
                for x, spec in zip(args, specs, strict=True)
            )
        )

    return with_places


def fetch(pairs, sems):
    copies = [pltpu.make_async_copy(src, dst, sems.at[i]) for i, (src, dst) in enumerate(pairs)]
    for copy in copies:
        copy.start()
    return copies


def buffer(dims, dtype=BF):
    return pltpu.VMEM(dims, dtype)


def semaphores(n):
    return pltpu.SemaphoreType.DMA((n,))


def shape(dims, dtype=BF):
    return jax.ShapeDtypeStruct(dims, dtype)


def prepare_kernel(core, up_far, gate_far, down_far, w13, w2, norm, up, gate, down, sems):
    copies = fetch(((up_far, up), (gate_far, gate), (down_far, down)), sems)
    half = w2.shape[0]
    for i, w in enumerate((up, gate, down)):
        copies[i].wait()
        full = w[...].astype(F32)
        norm[i : i + 1, :] = jnp.full((1, 128), jnp.sum(full * full), F32)
    norm[3:8, :] = jnp.zeros((5, 128), F32)
    for c in range(2):

        @pl.when(core[0] == c)
        def _():
            w13[0:half, :] = up[:, c * half : (c + 1) * half].T
            w13[half:, :] = gate[:, c * half : (c + 1) * half].T
            w2[...] = down[c * half : (c + 1) * half, :]


def factor(i, norm, own, oth):
    size = jnp.sqrt(norm[i : i + 1, 0:1])
    total = own[i : i + 1, 0:1] + oth[i : i + 1, 0:1]
    return size / jnp.sqrt(total + 1e-06)


def raw_kernel(w13, w2, keys, targets, raw):
    raw[0 : w13.shape[0], :] = nt(w13[...], keys[...])
    raw[w13.shape[0] :, :] = nt(w2[...], targets[...])


def act_grads(act, lin, err, scale):
    if scale is not None:
        act, lin, err = (x * f for x, f in zip((act, lin, err), scale))
    sig = jax.nn.sigmoid(act)
    silu = act * sig
    hidden = (silu * lin).astype(BF)
    pgrad = (err * lin * sig * (1.0 + act * (1.0 - sig))).astype(BF)
    qgrad = (err * silu).astype(BF)
    return pgrad, qgrad, hidden


def grads_kernel(w13, w2, raw, k_own, k_oth, u_own, u_oth, *rest):
    *state, out = rest
    half = w2.shape[0]
    cols = k_own.shape[1] // 2
    scale = [factor(i, *state) for i in (0, 1, 2)] if state else None
    keys, targets = k_oth[...], u_oth[...]
    oth = act_grads(
        nt(w13[0:half, :], keys), nt(w13[half:, :], keys), nt(w2[...], targets), scale
    )
    own = act_grads(raw[0:half, :], raw[half : 2 * half, :], raw[2 * half :, :], scale)
    for i in range(3):
        x, y = (k_own, k_oth) if i < 2 else (u_own, u_oth)
        for j in range(2):
            at = slice(j * cols, (j + 1) * cols)
            g = dot(own[i], x[:, at]) + dot(oth[i], y[:, at])
            out[j, i * half : (i + 1) * half, :] = g.astype(BF)


ROWS = 16


def moved_rows(i, base, src, terms, scale, dst, cols, half):
    def step(r, total):
        row = pl.multiple_of(base + r * ROWS, ROWS)
        at = pl.multiple_of(i * half + r * ROWS, ROWS)
        for j in range(2):
            side = slice(j * cols, (j + 1) * cols)
            m = src[pl.ds(row, ROWS), side].astype(F32)
            m = m + terms[0][j, pl.ds(at, ROWS), :].astype(F32)
            if scale is not None:
                m = m * scale + terms[1][j, pl.ds(at, ROWS), :].astype(F32)
            dst[pl.ds(row, ROWS), side] = m.astype(BF)
            total = total + m * m
        return total

    total = lax.fori_loop(0, half // ROWS, step, jnp.zeros((ROWS, cols), F32))
    return jnp.full((1, 128), jnp.sum(total), F32)


def update_kernel(w13_far, w2_far, gathered, m13, m2, squares, w13, w2, sems):
    half = w2.shape[0]
    cols = w2.shape[1] // 2
    pairs = [(w13_far.at[r, :], w13.at[r, :]) for r in (slice(0, half), slice(half, 2 * half))]
    copies = fetch([*pairs, (w2_far, w2)], sems)
    for i in range(3):
        src, dst = (w13, m13) if i < 2 else (w2, m2)
        copies[i].wait()
        squares[i : i + 1, :] = moved_rows(
            i, (i % 2) * half, src, (gathered,), None, dst, cols, half
        )
    squares[3:8, :] = jnp.zeros((5, 128), F32)


def later_kernel(parts, w_far, first_far, norm, own, oth, gathered_far, *rest):
    *before, m, squares, w, first, gathered, sems = rest
    half = w.shape[0] // len(parts)
    cols = w.shape[1] // 2
    pairs = []
    for k, i in enumerate(parts):
        rows, at = slice(k * half, (k + 1) * half), slice(i * half, (i + 1) * half)
        pairs.append((w_far.at[rows, :], w.at[rows, :]))
        pairs.append((first_far.at[:, at, :], first.at[:, at, :]))
        pairs.append((gathered_far.at[:, at, :], gathered.at[:, at, :]))
    copies = fetch(pairs, sems)
    squares[...] = before[0][...] if before else jnp.zeros(squares.shape, F32)
    for k, i in enumerate(parts):
        scale = jnp.broadcast_to(factor(i, norm, own, oth), (ROWS, cols))
        for copy in copies[3 * k : 3 * k + 3]:
            copy.wait()
        squares[i : i + 1, :] = moved_rows(
            i, k * half, w, (first, gathered), scale, m, cols, half
        )


def query_kernel(m13, oth_far, own_far, raw, oth, own, sems):
    copies = fetch(((oth_far, oth), (own_far, own)), sems)
    copies[0].wait()
    raw[0] = nt(m13[...], oth[...])
    copies[1].wait()
    raw[1] = nt(m13[...], own[...])


def hidden_kernel(k, raw, norm, sq_own, sq_oth, hq):
    half = hq.shape[0]
    act = raw[k, 0:half, :] * factor(0, norm, sq_own, sq_oth)
    lin = raw[k, half:, :] * factor(1, norm, sq_own, sq_oth)
    hq[...] = (jax.nn.silu(act) * lin * factor(2, norm, sq_own, sq_oth)).astype(BF)


def piece_kernel(hq_own, hq_got, w2_own, w2_got, o):
    o[...] = (tn(hq_own[...], w2_own[...]) + tn(hq_got[...], w2_got[...])).astype(BF)


def spread_kernel(arrived, out):
    total = arrived[0].astype(F32)
    for i in range(1, arrived.shape[0]):
        total = total + arrived[i].astype(F32)
    rounded = total.astype(BF)
    for i in range(arrived.shape[0]):
        out[i] = rounded


def stage_kernel(place, after, first_a, first_b, second_a, second_b, w, sems):
    rows = first_a.shape[0]
    for c in range(2):

        @pl.when(place[1] == c)
        def _():
            parts = (first_a, first_b, second_a, second_b)
            if c == 1:
                parts = parts[2:] + parts[:2]
            pairs = [(x, w.at[k * rows : (k + 1) * rows, :]) for k, x in enumerate(parts)]
            for copy in fetch(pairs, sems):
                copy.wait()


TILE = 512


def partial_kernel(place, o, w_own, out):
    out[...] = dot(o[...], w_own[...])


def partial_product(place, o, w_out):
    tokens, width = o.shape
    n = w_out.shape[1] // 2
    steps = n // TILE
    return pl.pallas_call(
        partial_kernel,
        out_shape=shape((tokens, n), F32),
        grid_spec=pltpu.PrefetchScalarGridSpec(
            num_scalar_prefetch=1,
            grid=(steps,),
            in_specs=[
                pl.BlockSpec((tokens, width), lambda i, s: (0, 0)),
                pl.BlockSpec((width, TILE), lambda i, s: (0, s[0] * steps + i)),
            ],
            out_specs=pl.BlockSpec((tokens, TILE), lambda i, s: (0, i)),
        ),
        compiler_params=pltpu.CompilerParams(vmem_limit_bytes=LIMIT),
        cost_estimate=pl.CostEstimate(
            flops=1 << 20, bytes_accessed=1 << 16, transcendentals=0
        ),
    )(place, o, w_out)


def finish_kernel(part, hq_a, hq_b, *rest):
    w2_a, w2_b, w, out, o, held, sems = rest
    o[...] = (tn(hq_a[...], w2_a[...]) + tn(hq_b[...], w2_b[...])).astype(BF)
    copies = []
    for j in range(part.shape[1] // TILE):
        at = slice(j * TILE, (j + 1) * TILE)
        total = part[:, at] + dot(o[...], w[:, at])
        held[j] = total.astype(BF)
        copies.append(pltpu.make_async_copy(held.at[j], out.at[:, at], sems.at[j]))
        copies[-1].start()
    for copy in copies:
        copy.wait()


def finish_product(part, hqs, w2s, w):
    tokens, n = part.shape
    width = w2s[0].shape[1]
    return pl.pallas_call(
        finish_kernel,
        out_shape=shape((tokens, n)),
        in_specs=[VMEM] * 6,
        out_specs=FAR,
        scratch_shapes=[
            buffer((tokens, width)),
            buffer((n // TILE, tokens, TILE)),
            semaphores(n // TILE),
        ],
        compiler_params=pltpu.CompilerParams(vmem_limit_bytes=LIMIT),
        cost_estimate=pl.CostEstimate(
            flops=2 * tokens * width * (n + width // 2), bytes_accessed=6 << 20, transcendentals=0
        ),
    )(part, *hqs, *w2s, w)


def all_reduced(grads, beside=None):
    peers = lax.axis_size(CHIPS)
    pieces = grads.reshape(peers, -1, grads.shape[2])
    arrived = lax.all_to_all(pieces, CHIPS, 0, 0, tiled=True)
    copies = call(
        spread_kernel,
        shape(pieces.shape),
        [VMEM],
        pieces.size,
        4 * pieces.size,
    )(arrived)
    if beside is not None:
        beside, _ = lax.optimization_barrier((beside, copies))
    gathered = lax.all_to_all(copies, CHIPS, 0, 0, tiled=True)
    return gathered.reshape(grads.shape), beside


def swap(x):
    return lax.ppermute(x, "c", SWAP)


def shards(queries, keys, values, rates, w_up, w_gate, w_down, w_out):
    width, hid = w_up.shape[1:]
    tokens = keys.shape[0]
    half, third = hid // 2, 3 * hid // 2
    core, head = lax.axis_index("c"), lax.axis_index("h")
    n = w_out.shape[1] // 2

    k_oth = swap(keys)
    targets = (rates * values.astype(F32)).astype(BF)
    u_oth = swap(targets)
    kus = (keys, k_oth, targets, u_oth)

    place = jnp.stack([head, core]).astype(jnp.int32)
    rows = width // 4

    def sent(part):
        return lax.dynamic_slice(
            w_out, ((2 * core + part) * rows, (1 - head) * n), (rows, n)
        )

    w_a = lax.ppermute(sent(0), ("xl", "h"), ACROSS)
    w_b = lax.ppermute(lax.optimization_barrier((sent(1), w_a))[0], ("xl", "h"), ACROSS)

    wshape = (shape((2 * half, width)), shape((half, width)))
    sshape = shape((8, 128), F32)
    scratch = (buffer((width, hid)), buffer((width, hid)), buffer((hid, width)), semaphores(3))
    *w, norm = call(
        prepare_kernel, (*wshape, sshape), [SMEM, FAR, FAR, FAR], 1 << 21, 5 << 20, scratch
    )(core.reshape(1).astype(jnp.int32), w_up[0], w_gate[0], w_down[0])
    flops = 12 * 2 * tokens * width * half
    gdims = (2, third, width // 2)
    pair = [buffer((tokens, width))] * 2
    state, mats = (), w
    for step in range(STEPS):
        raw = call(raw_kernel, shape((third, tokens), F32), [VMEM] * 4, flops // 4, 4 << 20)(
            *mats, keys, targets
        )
        grads = call(
            grads_kernel,
            shape(gdims),
            [VMEM] * (7 + len(state)),
            flops * 3 // 4,
            8 << 20,
        )(*mats, raw, keys, k_oth, targets, u_oth, *state)
        gathered, w_late = all_reduced(grads, (w_a, w_b) if step else None)
        if step == 0:
            *mats, squares = call(
                update_kernel,
                (*wshape, sshape),
                [FAR] * 2 + [NEAR],
                1 << 22,
                5 << 20,
                (buffer((2 * half, width)), buffer((half, width)), semaphores(3)),
            )(*w, gathered)
            first = gathered
        else:
            before, mats = (), []
            for k, parts in ((1, (2,)), (0, (0, 1))):
                m, *before = call(
                    functools.partial(later_kernel, parts),
                    (wshape[k], sshape),
                    [FAR] * 2 + [VMEM] * 3 + [ANY] + [VMEM] * len(before),
                    1 << 20,
                    1 << 20,
                    (
                        buffer(wshape[k].shape),
                        buffer(gdims),
                        buffer(gdims),
                        semaphores(3 * len(parts)),
                    ),
                )(w[k], first, *state, gathered, *before)
                mats.insert(0, m)
            squares = before[0]
        state = (norm, squares, swap(squares))
    crossed = lax.ppermute(mats[1], ("xl", "h"), ACROSS)
    w_parts = (w_a, w_b, *map(swap, w_late))
    q_oth = swap(queries)
    w2_got = swap(mats[1])
    hshape = shape((half, tokens))
    raw = call(
        query_kernel,
        shape((2, 2 * half, tokens), F32),
        [VMEM, ANY, FAR],
        flops // 3,
        5 << 20,
        (*pair, semaphores(2)),
    )(mats[0], q_oth, queries)
    hq_oth, hq_own = (
        call(functools.partial(hidden_kernel, k), hshape, [VMEM] * 4, 1 << 20, 2 << 20)(raw, *state)
        for k in range(2)
    )
    hq_got = swap(hq_oth)
    hqs = [lax.ppermute(x, "h", SWAP) for x in (hq_own, hq_got)]
    o = call(piece_kernel, shape((tokens, width)), [VMEM] * 4, 1 << 20, 1 << 16)(
        hq_own, hq_got, mats[1], w2_got
    )
    part = partial_product(place, o, w_out)
    w_other = call(
        stage_kernel, shape((width, n)), [SMEM] + [ANY] * 5, 1 << 16, 1 << 16, [semaphores(4)]
    )(place, hq_got, *w_parts)
    crossed, *hqs, _, _ = lax.optimization_barrier((crossed, *hqs, part, w_other))
    return finish_product(part, hqs, (crossed, swap(crossed)), w_other)


def solution(mesh):
    finer = Mesh(
        mesh.devices.reshape(4, 2, 4, 2, mesh.shape["head"]),
        ("z", "xl", "y", "c", "h"),
    )
    return jax.shard_map(
        shards,
        mesh=finer,
        in_specs=(
            P(CTX, "h"),
            P(CTX, "h"),
            P(CTX, "h"),
            P(CTX, "h"),
            P("h", None, None),
            P("h", None, None),
            P("h", None, None),
            P("h", None),
        ),
        out_specs=P(CTX, "h"),
        check_vma=False,
    )
```

```python
import functools

import jax
import jax.numpy as jnp
from jax import lax
from jax.experimental import pallas as pl
from jax.experimental.pallas import tpu as pltpu
from jax.sharding import Mesh
from jax.sharding import PartitionSpec as P

STEPS = 2
CTX = ("z", "xl", "y", "c")
CHIPS = ("z", "xl", "y")
SWAP = [(0, 1), (1, 0)]
ACROSS = [(0, 3), (3, 0), (1, 2), (2, 1)]
BF = jnp.bfloat16
F32 = jnp.float32
NT = (((1,), (1,)), ((), ()))
TN = (((0,), (0,)), ((), ()))
VMEM = pl.BlockSpec(memory_space=pltpu.VMEM)
SMEM = pl.BlockSpec(memory_space=pltpu.SMEM)
FAR = pl.BlockSpec(memory_space=pltpu.HBM)
ANY = pl.BlockSpec(memory_space=pl.ANY)
NEAR = pl.BlockSpec(memory_space=pltpu.VMEM)
HELD = {id(FAR): pltpu.HBM, id(NEAR): pltpu.VMEM}
LIMIT = 24 * 1024 * 1024


def dot(x, y):
    return jnp.dot(x, y, preferred_element_type=F32)


def nt(x, y):
    return lax.dot_general(x, y, NT, preferred_element_type=F32)


def tn(x, y):
    return lax.dot_general(x, y, TN, preferred_element_type=F32)


def call(kernel, outs, specs, flops, nbytes, scratch=(), far=False):
    if far:
        outs = jax.tree.map(lambda x: pltpu.HBM(x.shape, x.dtype), outs)
    run = pl.pallas_call(
        kernel,
        out_shape=outs,
        in_specs=specs,
        out_specs=jax.tree.map(lambda _: FAR if far else VMEM, outs),
        scratch_shapes=list(scratch),
        compiler_params=pltpu.CompilerParams(vmem_limit_bytes=LIMIT),
        cost_estimate=pl.CostEstimate(flops=flops, bytes_accessed=nbytes, transcendentals=0),
    )

    def with_places(*args):
        return run(
            *(
                pltpu.with_memory_space_constraint(x, HELD[id(spec)]) if id(spec) in HELD else x
                for x, spec in zip(args, specs, strict=True)
            )
        )

    return with_places


def fetch(pairs, sems):
    copies = [pltpu.make_async_copy(src, dst, sems.at[i]) for i, (src, dst) in enumerate(pairs)]
    for copy in copies:
        copy.start()
    return copies


def buffer(dims, dtype=BF):
    return pltpu.VMEM(dims, dtype)


def semaphores(n):
    return pltpu.SemaphoreType.DMA((n,))


def shape(dims, dtype=BF):
    return jax.ShapeDtypeStruct(dims, dtype)


def prepare_kernel(core, up_far, gate_far, down_far, w13, w2, norm, up, gate, down, sems):
    copies = fetch(((up_far, up), (gate_far, gate), (down_far, down)), sems)
    half = w2.shape[0]
    for i, w in enumerate((up, gate, down)):
        copies[i].wait()
        full = w[...].astype(F32)
        norm[i : i + 1, :] = jnp.full((1, 128), jnp.sum(full * full), F32)
    norm[3:8, :] = jnp.zeros((5, 128), F32)
    for c in range(2):

        @pl.when(core[0] == c)
        def _():
            w13[0:half, :] = up[:, c * half : (c + 1) * half].T
            w13[half:, :] = gate[:, c * half : (c + 1) * half].T
            w2[...] = down[c * half : (c + 1) * half, :]


def factor(i, norm, own, oth):
    size = jnp.sqrt(norm[i : i + 1, 0:1])
    total = own[i : i + 1, 0:1] + oth[i : i + 1, 0:1]
    return size / jnp.sqrt(total + 1e-06)


def raw_kernel(w13, w2, keys, targets, raw):
    raw[0 : w13.shape[0], :] = nt(w13[...], keys[...])
    raw[w13.shape[0] :, :] = nt(w2[...], targets[...])


def act_grads(act, lin, err, scale):
    if scale is not None:
        act, lin, err = (x * f for x, f in zip((act, lin, err), scale))
    sig = jax.nn.sigmoid(act)
    silu = act * sig
    hidden = (silu * lin).astype(BF)
    pgrad = (err * lin * sig * (1.0 + act * (1.0 - sig))).astype(BF)
    qgrad = (err * silu).astype(BF)
    return pgrad, qgrad, hidden


def grads_kernel(w13, w2, raw, k_own, k_oth, u_own, u_oth, *rest):
    *state, out = rest
    half = w2.shape[0]
    cols = k_own.shape[1] // 2
    scale = [factor(i, *state) for i in (0, 1, 2)] if state else None
    keys, targets = k_oth[...], u_oth[...]
    oth = act_grads(
        nt(w13[0:half, :], keys), nt(w13[half:, :], keys), nt(w2[...], targets), scale
    )
    own = act_grads(raw[0:half, :], raw[half : 2 * half, :], raw[2 * half :, :], scale)
    for i in range(3):
        x, y = (k_own, k_oth) if i < 2 else (u_own, u_oth)
        for j in range(2):
            at = slice(j * cols, (j + 1) * cols)
            g = dot(own[i], x[:, at]) + dot(oth[i], y[:, at])
            out[j, i * half : (i + 1) * half, :] = g.astype(BF)


ROWS = 16


def moved_rows(i, base, src, terms, scale, dst, cols, half):
    def step(r, total):
        row = pl.multiple_of(base + r * ROWS, ROWS)
        at = pl.multiple_of(i * half + r * ROWS, ROWS)
        for j in range(2):
            side = slice(j * cols, (j + 1) * cols)
            m = src[pl.ds(row, ROWS), side].astype(F32)
            m = m + terms[0][j, pl.ds(at, ROWS), :].astype(F32)
            if scale is not None:
                m = m * scale + terms[1][j, pl.ds(at, ROWS), :].astype(F32)
            dst[pl.ds(row, ROWS), side] = m.astype(BF)
            total = total + m * m
        return total

    total = lax.fori_loop(0, half // ROWS, step, jnp.zeros((ROWS, cols), F32))
    return jnp.full((1, 128), jnp.sum(total), F32)


def update_kernel(w13_far, w2_far, gathered, m13, m2, squares, w13, w2, sems):
    half = w2.shape[0]
    cols = w2.shape[1] // 2
    pairs = [(w13_far.at[r, :], w13.at[r, :]) for r in (slice(0, half), slice(half, 2 * half))]
    copies = fetch([*pairs, (w2_far, w2)], sems)
    for i in range(3):
        src, dst = (w13, m13) if i < 2 else (w2, m2)
        copies[i].wait()
        squares[i : i + 1, :] = moved_rows(
            i, (i % 2) * half, src, (gathered,), None, dst, cols, half
        )
    squares[3:8, :] = jnp.zeros((5, 128), F32)


def later_kernel(parts, w_far, first_far, norm, own, oth, gathered_far, *rest):
    *before, m, squares, w, first, gathered, sems = rest
    half = w.shape[0] // len(parts)
    cols = w.shape[1] // 2
    pairs = []
    for k, i in enumerate(parts):
        rows, at = slice(k * half, (k + 1) * half), slice(i * half, (i + 1) * half)
        pairs.append((w_far.at[rows, :], w.at[rows, :]))
        pairs.append((first_far.at[:, at, :], first.at[:, at, :]))
        pairs.append((gathered_far.at[:, at, :], gathered.at[:, at, :]))
    copies = fetch(pairs, sems)
    squares[...] = before[0][...] if before else jnp.zeros(squares.shape, F32)
    for k, i in enumerate(parts):
        scale = jnp.broadcast_to(factor(i, norm, own, oth), (ROWS, cols))
        for copy in copies[3 * k : 3 * k + 3]:
            copy.wait()
        squares[i : i + 1, :] = moved_rows(
            i, k * half, w, (first, gathered), scale, m, cols, half
        )


def query_kernel(m13, oth_far, own_far, raw, oth, own, sems):
    copies = fetch(((oth_far, oth), (own_far, own)), sems)
    copies[0].wait()
    raw[0] = nt(m13[...], oth[...])
    copies[1].wait()
    raw[1] = nt(m13[...], own[...])


def hidden_kernel(k, raw, norm, sq_own, sq_oth, hq):
    half = hq.shape[0]
    act = raw[k, 0:half, :] * factor(0, norm, sq_own, sq_oth)
    lin = raw[k, half:, :] * factor(1, norm, sq_own, sq_oth)
    hq[...] = (jax.nn.silu(act) * lin * factor(2, norm, sq_own, sq_oth)).astype(BF)


def piece_kernel(hq_own, hq_got, w2_own, w2_got, o):
    o[...] = (tn(hq_own[...], w2_own[...]) + tn(hq_got[...], w2_got[...])).astype(BF)


def spread_kernel(arrived, out):
    total = arrived[0].astype(F32)
    for i in range(1, arrived.shape[0]):
        total = total + arrived[i].astype(F32)
    rounded = total.astype(BF)
    for i in range(arrived.shape[0]):
        out[i] = rounded


def stage_kernel(place, after, first_a, first_b, second_a, second_b, w, sems):
    rows = first_a.shape[0]
    for c in range(2):

        @pl.when(place[1] == c)
        def _():
            parts = (first_a, first_b, second_a, second_b)
            if c == 1:
                parts = parts[2:] + parts[:2]
            pairs = [(x, w.at[k * rows : (k + 1) * rows, :]) for k, x in enumerate(parts)]
            for copy in fetch(pairs, sems):
                copy.wait()


TILE = 512


def partial_kernel(place, o, w_own, out):
    out[...] = dot(o[...], w_own[...])


def partial_product(place, o, w_out):
    tokens, width = o.shape
    n = w_out.shape[1] // 2
    steps = n // TILE
    return pl.pallas_call(
        partial_kernel,
        out_shape=shape((tokens, n), F32),
        grid_spec=pltpu.PrefetchScalarGridSpec(
            num_scalar_prefetch=1,
            grid=(steps,),
            in_specs=[
                pl.BlockSpec((tokens, width), lambda i, s: (0, 0)),
                pl.BlockSpec((width, TILE), lambda i, s: (0, s[0] * steps + i)),
            ],
            out_specs=pl.BlockSpec((tokens, TILE), lambda i, s: (0, i)),
        ),
        compiler_params=pltpu.CompilerParams(vmem_limit_bytes=LIMIT),
        cost_estimate=pl.CostEstimate(
            flops=1 << 20, bytes_accessed=1 << 16, transcendentals=0
        ),
    )(place, o, pltpu.with_memory_space_constraint(w_out, pltpu.HBM))


def finish_kernel(part, hq_a, hq_b, *rest):
    w2_a, w2_b, w, out, o, held, sems = rest
    o[...] = (tn(hq_a[...], w2_a[...]) + tn(hq_b[...], w2_b[...])).astype(BF)
    copies = []
    for j in range(part.shape[1] // TILE):
        at = slice(j * TILE, (j + 1) * TILE)
        total = part[:, at] + dot(o[...], w[:, at])
        held[j] = total.astype(BF)
        copies.append(pltpu.make_async_copy(held.at[j], out.at[:, at], sems.at[j]))
        copies[-1].start()
    for copy in copies:
        copy.wait()


def finish_product(part, hqs, w2s, w):
    tokens, n = part.shape
    width = w2s[0].shape[1]
    return pl.pallas_call(
        finish_kernel,
        out_shape=shape((tokens, n)),
        in_specs=[VMEM] * 6,
        out_specs=FAR,
        scratch_shapes=[
            buffer((tokens, width)),
            buffer((n // TILE, tokens, TILE)),
            semaphores(n // TILE),
        ],
        compiler_params=pltpu.CompilerParams(vmem_limit_bytes=LIMIT),
        cost_estimate=pl.CostEstimate(
            flops=2 * tokens * width * (n + width // 2), bytes_accessed=6 << 20, transcendentals=0
        ),
    )(part, *hqs, *w2s, w)


def all_reduced(grads, beside=None):
    peers = lax.axis_size(CHIPS)
    pieces = grads.reshape(peers, -1, grads.shape[2])
    arrived = lax.all_to_all(pieces, CHIPS, 0, 0, tiled=True)
    copies = call(
        spread_kernel,
        shape(pieces.shape),
        [VMEM],
        pieces.size,
        4 * pieces.size,
    )(arrived)
    if beside is not None:
        beside, _ = lax.optimization_barrier((beside, copies))
    gathered = lax.all_to_all(copies, CHIPS, 0, 0, tiled=True)
    return gathered.reshape(grads.shape), beside


def swap(x):
    return lax.ppermute(x, "c", SWAP)


def shards(queries, keys, values, rates, w_up, w_gate, w_down, w_out):
    width, hid = w_up.shape[1:]
    tokens = keys.shape[0]
    half, third = hid // 2, 3 * hid // 2
    core, head = lax.axis_index("c"), lax.axis_index("h")
    n = w_out.shape[1] // 2

    k_oth = swap(keys)
    targets = (rates * values.astype(F32)).astype(BF)
    u_oth = swap(targets)
    kus = (keys, k_oth, targets, u_oth)

    place = jnp.stack([head, core]).astype(jnp.int32)
    rows = width // 4

    def sent(part):
        return lax.dynamic_slice(
            w_out, ((2 * core + part) * rows, (1 - head) * n), (rows, n)
        )

    w_a = lax.ppermute(sent(0), ("xl", "h"), ACROSS)
    w_b = lax.ppermute(lax.optimization_barrier((sent(1), w_a))[0], ("xl", "h"), ACROSS)

    wshape = (shape((2 * half, width)), shape((half, width)))
    sshape = shape((8, 128), F32)
    scratch = (buffer((width, hid)), buffer((width, hid)), buffer((hid, width)), semaphores(3))
    *w, norm = call(
        prepare_kernel, (*wshape, sshape), [SMEM, FAR, FAR, FAR], 1 << 21, 5 << 20, scratch
    )(core.reshape(1).astype(jnp.int32), w_up[0], w_gate[0], w_down[0])
    flops = 12 * 2 * tokens * width * half
    gdims = (2, third, width // 2)
    pair = [buffer((tokens, width))] * 2
    state, mats = (), w
    for step in range(STEPS):
        raw = call(raw_kernel, shape((third, tokens), F32), [VMEM] * 4, flops // 4, 4 << 20)(
            *mats, keys, targets
        )
        grads = call(
            grads_kernel,
            shape(gdims),
            [VMEM] * (7 + len(state)),
            flops * 3 // 4,
            8 << 20,
        )(*mats, raw, keys, k_oth, targets, u_oth, *state)
        gathered, w_late = all_reduced(grads, (w_a, w_b) if step else None)
        if step == 0:
            *mats, squares = call(
                update_kernel,
                (*wshape, sshape),
                [FAR] * 2 + [NEAR],
                1 << 22,
                5 << 20,
                (buffer((2 * half, width)), buffer((half, width)), semaphores(3)),
            )(*w, gathered)
            first = gathered
        else:
            before, mats = (), []
            for k, parts in ((1, (2,)), (0, (0, 1))):
                m, *before = call(
                    functools.partial(later_kernel, parts),
                    (wshape[k], sshape),
                    [FAR] * 2 + [VMEM] * 3 + [ANY] + [VMEM] * len(before),
                    1 << 20,
                    1 << 20,
                    (
                        buffer(wshape[k].shape),
                        buffer(gdims),
                        buffer(gdims),
                        semaphores(3 * len(parts)),
                    ),
                )(w[k], first, *state, gathered, *before)
                mats.insert(0, m)
            squares = before[0]
        state = (norm, squares, swap(squares))
    crossed = lax.ppermute(mats[1], ("xl", "h"), ACROSS)
    w_parts = (w_a, w_b, *map(swap, w_late))
    q_oth = swap(queries)
    w2_got = swap(mats[1])
    hshape = shape((half, tokens))
    raw = call(
        query_kernel,
        shape((2, 2 * half, tokens), F32),
        [VMEM, ANY, FAR],
        flops // 3,
        5 << 20,
        (*pair, semaphores(2)),
    )(mats[0], q_oth, queries)
    hq_oth, hq_own = (
        call(functools.partial(hidden_kernel, k), hshape, [VMEM] * 4, 1 << 20, 2 << 20)(raw, *state)
        for k in range(2)
    )
    hq_got = swap(hq_oth)
    hqs = [lax.ppermute(x, "h", SWAP) for x in (hq_own, hq_got)]
    o = call(piece_kernel, shape((tokens, width)), [VMEM] * 4, 1 << 20, 1 << 16)(
        hq_own, hq_got, mats[1], w2_got
    )
    part = partial_product(place, o, w_out)
    w_other = call(
        stage_kernel, shape((width, n)), [SMEM] + [ANY] * 5, 1 << 16, 1 << 16, [semaphores(4)]
    )(place, hq_got, *w_parts)
    crossed, *hqs, _, _ = lax.optimization_barrier((crossed, *hqs, part, w_other))
    return finish_product(part, hqs, (crossed, swap(crossed)), w_other)


def solution(mesh):
    finer = Mesh(
        mesh.devices.reshape(4, 2, 4, 2, mesh.shape["head"]),
        ("z", "xl", "y", "c", "h"),
    )
    return jax.shard_map(
        shards,
        mesh=finer,
        in_specs=(
            P(CTX, "h"),
            P(CTX, "h"),
            P(CTX, "h"),
            P(CTX, "h"),
            P("h", None, None),
            P("h", None, None),
            P("h", None, None),
            P("h", None),
        ),
        out_specs=P(CTX, "h"),
        check_vma=False,
    )
```

```python
import functools

import jax
import jax.numpy as jnp
from jax import lax
from jax.experimental import pallas as pl
from jax.experimental.pallas import tpu as pltpu
from jax.sharding import Mesh
from jax.sharding import PartitionSpec as P

STEPS = 2
CTX = ("z", "xl", "y", "c")
CHIPS = ("z", "xl", "y")
SWAP = [(0, 1), (1, 0)]
ACROSS = [(0, 3), (3, 0), (1, 2), (2, 1)]
BF = jnp.bfloat16
F32 = jnp.float32
NT = (((1,), (1,)), ((), ()))
TN = (((0,), (0,)), ((), ()))
VMEM = pl.BlockSpec(memory_space=pltpu.VMEM)
SMEM = pl.BlockSpec(memory_space=pltpu.SMEM)
FAR = pl.BlockSpec(memory_space=pltpu.HBM)
ANY = pl.BlockSpec(memory_space=pl.ANY)
NEAR = pl.BlockSpec(memory_space=pltpu.VMEM)
HELD = {id(FAR): pltpu.HBM, id(NEAR): pltpu.VMEM}
LIMIT = 24 * 1024 * 1024


def dot(x, y):
    return jnp.dot(x, y, preferred_element_type=F32)


def nt(x, y):
    return lax.dot_general(x, y, NT, preferred_element_type=F32)


def tn(x, y):
    return lax.dot_general(x, y, TN, preferred_element_type=F32)


def call(kernel, outs, specs, flops, nbytes, scratch=(), far=False):
    if far:
        outs = jax.tree.map(lambda x: pltpu.HBM(x.shape, x.dtype), outs)
    run = pl.pallas_call(
        kernel,
        out_shape=outs,
        in_specs=specs,
        out_specs=jax.tree.map(lambda _: FAR if far else VMEM, outs),
        scratch_shapes=list(scratch),
        compiler_params=pltpu.CompilerParams(vmem_limit_bytes=LIMIT),
        cost_estimate=pl.CostEstimate(flops=flops, bytes_accessed=nbytes, transcendentals=0),
    )

    def with_places(*args):
        return run(
            *(
                pltpu.with_memory_space_constraint(x, HELD[id(spec)]) if id(spec) in HELD else x
                for x, spec in zip(args, specs, strict=True)
            )
        )

    return with_places


def fetch(pairs, sems):
    copies = [pltpu.make_async_copy(src, dst, sems.at[i]) for i, (src, dst) in enumerate(pairs)]
    for copy in copies:
        copy.start()
    return copies


def buffer(dims, dtype=BF):
    return pltpu.VMEM(dims, dtype)


def semaphores(n):
    return pltpu.SemaphoreType.DMA((n,))


def shape(dims, dtype=BF):
    return jax.ShapeDtypeStruct(dims, dtype)


def prepare_kernel(core, up_far, gate_far, down_far, w13, w2, norm, up, gate, down, sems):
    copies = fetch(((up_far, up), (gate_far, gate), (down_far, down)), sems)
    half = w2.shape[0]
    norm[3:8, :] = jnp.zeros((5, 128), F32)
    for i, w in enumerate((up, gate, down)):
        copies[i].wait()
        for c in range(2):
            at = slice(c * half, (c + 1) * half)

            @pl.when(core[0] == c)
            def _():
                if i < 2:
                    w13[i * half : (i + 1) * half, :] = w[:, at].T
                else:
                    w2[...] = w[at, :]

        full = w[...].astype(F32)
        norm[i : i + 1, :] = jnp.full((1, 128), jnp.sum(full * full), F32)


def factor(i, norm, own, oth):
    size = jnp.sqrt(norm[i : i + 1, 0:1])
    total = own[i : i + 1, 0:1] + oth[i : i + 1, 0:1]
    return size / jnp.sqrt(total + 1e-06)


def raw_kernel(w13, w2, keys, targets, raw):
    raw[0 : w13.shape[0], :] = nt(w13[...], keys[...])
    raw[w13.shape[0] :, :] = nt(w2[...], targets[...])


def act_grads(act, lin, err, scale):
    if scale is not None:
        act, lin, err = (x * f for x, f in zip((act, lin, err), scale))
    sig = jax.nn.sigmoid(act)
    silu = act * sig
    hidden = (silu * lin).astype(BF)
    pgrad = (err * lin * sig * (1.0 + act * (1.0 - sig))).astype(BF)
    qgrad = (err * silu).astype(BF)
    return pgrad, qgrad, hidden


def grads_kernel(w13, w2, raw, k_own, k_oth, u_own, u_oth, *rest):
    *state, out = rest
    half = w2.shape[0]
    cols = k_own.shape[1] // 2
    scale = [factor(i, *state) for i in (0, 1, 2)] if state else None
    keys, targets = k_oth[...], u_oth[...]
    oth = act_grads(
        nt(w13[0:half, :], keys), nt(w13[half:, :], keys), nt(w2[...], targets), scale
    )
    own = act_grads(raw[0:half, :], raw[half : 2 * half, :], raw[2 * half :, :], scale)
    for i in range(3):
        x, y = (k_own, k_oth) if i < 2 else (u_own, u_oth)
        for j in range(2):
            at = slice(j * cols, (j + 1) * cols)
            g = dot(own[i], x[:, at]) + dot(oth[i], y[:, at])
            out[j, i * half : (i + 1) * half, :] = g.astype(BF)


ROWS = 16


def moved_rows(i, base, src, terms, scale, dst, cols, half):
    def step(r, total):
        row = pl.multiple_of(base + r * ROWS, ROWS)
        at = pl.multiple_of(i * half + r * ROWS, ROWS)
        for j in range(2):
            side = slice(j * cols, (j + 1) * cols)
            m = src[pl.ds(row, ROWS), side].astype(F32)
            m = m + terms[0][j, pl.ds(at, ROWS), :].astype(F32)
            if scale is not None:
                m = m * scale + terms[1][j, pl.ds(at, ROWS), :].astype(F32)
            dst[pl.ds(row, ROWS), side] = m.astype(BF)
            total = total + m * m
        return total

    total = lax.fori_loop(0, half // ROWS, step, jnp.zeros((ROWS, cols), F32))
    return jnp.full((1, 128), jnp.sum(total), F32)


def update_kernel(w13_far, w2_far, gathered, m13, m2, squares, w13, w2, sems):
    half = w2.shape[0]
    cols = w2.shape[1] // 2
    pairs = [(w13_far.at[r, :], w13.at[r, :]) for r in (slice(0, half), slice(half, 2 * half))]
    copies = fetch([*pairs, (w2_far, w2)], sems)
    for i in range(3):
        src, dst = (w13, m13) if i < 2 else (w2, m2)
        copies[i].wait()
        squares[i : i + 1, :] = moved_rows(
            i, (i % 2) * half, src, (gathered,), None, dst, cols, half
        )
    squares[3:8, :] = jnp.zeros((5, 128), F32)


def later_kernel(parts, w_far, first_far, norm, own, oth, gathered_far, *rest):
    *before, m, squares, w, first, gathered, sems = rest
    half = w.shape[0] // len(parts)
    cols = w.shape[1] // 2
    pairs = []
    for k, i in enumerate(parts):
        rows, at = slice(k * half, (k + 1) * half), slice(i * half, (i + 1) * half)
        pairs.append((w_far.at[rows, :], w.at[rows, :]))
        pairs.append((first_far.at[:, at, :], first.at[:, at, :]))
        pairs.append((gathered_far.at[:, at, :], gathered.at[:, at, :]))
    copies = fetch(pairs, sems)
    squares[...] = before[0][...] if before else jnp.zeros(squares.shape, F32)
    for k, i in enumerate(parts):
        scale = jnp.broadcast_to(factor(i, norm, own, oth), (ROWS, cols))
        for copy in copies[3 * k : 3 * k + 3]:
            copy.wait()
        squares[i : i + 1, :] = moved_rows(
            i, k * half, w, (first, gathered), scale, m, cols, half
        )


def query_kernel(m13, oth_far, own_far, raw, oth, own, sems):
    copies = fetch(((oth_far, oth), (own_far, own)), sems)
    copies[0].wait()
    raw[0] = nt(m13[...], oth[...])
    copies[1].wait()
    raw[1] = nt(m13[...], own[...])


def hidden_kernel(k, raw, norm, sq_own, sq_oth, hq):
    half = hq.shape[0]
    act = raw[k, 0:half, :] * factor(0, norm, sq_own, sq_oth)
    lin = raw[k, half:, :] * factor(1, norm, sq_own, sq_oth)
    hq[...] = (jax.nn.silu(act) * lin * factor(2, norm, sq_own, sq_oth)).astype(BF)


def piece_kernel(hq_own, hq_got, w2_own, w2_got, o):
    o[...] = (tn(hq_own[...], w2_own[...]) + tn(hq_got[...], w2_got[...])).astype(BF)


def spread_kernel(arrived, out):
    total = arrived[0].astype(F32)
    for i in range(1, arrived.shape[0]):
        total = total + arrived[i].astype(F32)
    rounded = total.astype(BF)
    for i in range(arrived.shape[0]):
        out[i] = rounded


def stage_kernel(place, after, first_a, first_b, second_a, second_b, w, sems):
    rows = first_a.shape[0]
    for c in range(2):

        @pl.when(place[1] == c)
        def _():
            parts = (first_a, first_b, second_a, second_b)
            if c == 1:
                parts = parts[2:] + parts[:2]
            pairs = [(x, w.at[k * rows : (k + 1) * rows, :]) for k, x in enumerate(parts)]
            for copy in fetch(pairs, sems):
                copy.wait()


TILE = 512


def partial_kernel(place, o, w_own, out):
    out[...] = dot(o[...], w_own[...])


def partial_product(place, o, w_out):
    tokens, width = o.shape
    n = w_out.shape[1] // 2
    steps = n // TILE
    return pl.pallas_call(
        partial_kernel,
        out_shape=shape((tokens, n), F32),
        grid_spec=pltpu.PrefetchScalarGridSpec(
            num_scalar_prefetch=1,
            grid=(steps,),
            in_specs=[
                pl.BlockSpec((tokens, width), lambda i, s: (0, 0)),
                pl.BlockSpec((width, TILE), lambda i, s: (0, s[0] * steps + i)),
            ],
            out_specs=pl.BlockSpec((tokens, TILE), lambda i, s: (0, i)),
        ),
        compiler_params=pltpu.CompilerParams(vmem_limit_bytes=LIMIT),
        cost_estimate=pl.CostEstimate(
            flops=1 << 20, bytes_accessed=1 << 16, transcendentals=0
        ),
    )(place, o, pltpu.with_memory_space_constraint(w_out, pltpu.HBM))


def finish_kernel(part, hq_a, hq_b, *rest):
    w2_a, w2_b, w, out, o, held, sems = rest
    o[...] = (tn(hq_a[...], w2_a[...]) + tn(hq_b[...], w2_b[...])).astype(BF)
    copies = []
    for j in range(part.shape[1] // TILE):
        at = slice(j * TILE, (j + 1) * TILE)
        total = part[:, at] + dot(o[...], w[:, at])
        held[j] = total.astype(BF)
        copies.append(pltpu.make_async_copy(held.at[j], out.at[:, at], sems.at[j]))
        copies[-1].start()
    for copy in copies:
        copy.wait()


def finish_product(part, hqs, w2s, w):
    tokens, n = part.shape
    width = w2s[0].shape[1]
    return pl.pallas_call(
        finish_kernel,
        out_shape=shape((tokens, n)),
        in_specs=[VMEM] * 6,
        out_specs=FAR,
        scratch_shapes=[
            buffer((tokens, width)),
            buffer((n // TILE, tokens, TILE)),
            semaphores(n // TILE),
        ],
        compiler_params=pltpu.CompilerParams(vmem_limit_bytes=LIMIT),
        cost_estimate=pl.CostEstimate(
            flops=2 * tokens * width * (n + width // 2), bytes_accessed=6 << 20, transcendentals=0
        ),
    )(part, *hqs, *w2s, w)


def all_reduced(grads, beside=None):
    peers = lax.axis_size(CHIPS)
    pieces = grads.reshape(peers, -1, grads.shape[2])
    arrived = lax.all_to_all(pieces, CHIPS, 0, 0, tiled=True)
    copies = call(
        spread_kernel,
        shape(pieces.shape),
        [VMEM],
        pieces.size,
        4 * pieces.size,
    )(arrived)
    if beside is not None:
        beside, _ = lax.optimization_barrier((beside, copies))
    gathered = lax.all_to_all(copies, CHIPS, 0, 0, tiled=True)
    return gathered.reshape(grads.shape), beside


def swap(x):
    return lax.ppermute(x, "c", SWAP)


def shards(queries, keys, values, rates, w_up, w_gate, w_down, w_out):
    width, hid = w_up.shape[1:]
    tokens = keys.shape[0]
    half, third = hid // 2, 3 * hid // 2
    core, head = lax.axis_index("c"), lax.axis_index("h")
    n = w_out.shape[1] // 2

    k_oth = swap(keys)
    targets = (rates * values.astype(F32)).astype(BF)
    u_oth = swap(targets)
    kus = (keys, k_oth, targets, u_oth)

    place = jnp.stack([head, core]).astype(jnp.int32)
    rows = width // 4

    def sent(part):
        return lax.dynamic_slice(
            w_out, ((2 * core + part) * rows, (1 - head) * n), (rows, n)
        )

    w_a = lax.ppermute(sent(0), ("xl", "h"), ACROSS)
    w_b = lax.ppermute(lax.optimization_barrier((sent(1), w_a))[0], ("xl", "h"), ACROSS)

    wshape = (shape((2 * half, width)), shape((half, width)))
    sshape = shape((8, 128), F32)
    scratch = (buffer((width, hid)), buffer((width, hid)), buffer((hid, width)), semaphores(3))
    *w, norm = call(
        prepare_kernel, (*wshape, sshape), [SMEM, FAR, FAR, FAR], 1 << 21, 5 << 20, scratch
    )(core.reshape(1).astype(jnp.int32), w_up[0], w_gate[0], w_down[0])
    flops = 12 * 2 * tokens * width * half
    gdims = (2, third, width // 2)
    pair = [buffer((tokens, width))] * 2
    state, mats = (), w
    for step in range(STEPS):
        raw = call(raw_kernel, shape((third, tokens), F32), [VMEM] * 4, flops // 4, 4 << 20)(
            *mats, keys, targets
        )
        grads = call(
            grads_kernel,
            shape(gdims),
            [VMEM] * (7 + len(state)),
            flops * 3 // 4,
            8 << 20,
        )(*mats, raw, keys, k_oth, targets, u_oth, *state)
        gathered, w_late = all_reduced(grads, (w_a, w_b) if step else None)
        if step == 0:
            *mats, squares = call(
                update_kernel,
                (*wshape, sshape),
                [FAR] * 2 + [NEAR],
                1 << 22,
                5 << 20,
                (buffer((2 * half, width)), buffer((half, width)), semaphores(3)),
            )(*w, gathered)
            first = gathered
        else:
            before, mats = (), []
            for k, parts in ((1, (2,)), (0, (0, 1))):
                m, *before = call(
                    functools.partial(later_kernel, parts),
                    (wshape[k], sshape),
                    [FAR] * 2 + [VMEM] * 3 + [ANY] + [VMEM] * len(before),
                    1 << 20,
                    1 << 20,
                    (
                        buffer(wshape[k].shape),
                        buffer(gdims),
                        buffer(gdims),
                        semaphores(3 * len(parts)),
                    ),
                )(w[k], first, *state, gathered, *before)
                mats.insert(0, m)
            squares = before[0]
        state = (norm, squares, swap(squares))
    crossed = lax.ppermute(mats[1], ("xl", "h"), ACROSS)
    w_parts = (w_a, w_b, *map(swap, w_late))
    q_oth = swap(queries)
    w2_got = swap(mats[1])
    hshape = shape((half, tokens))
    raw = call(
        query_kernel,
        shape((2, 2 * half, tokens), F32),
        [VMEM, ANY, FAR],
        flops // 3,
        5 << 20,
        (*pair, semaphores(2)),
    )(mats[0], q_oth, queries)
    hq_oth, hq_own = (
        call(functools.partial(hidden_kernel, k), hshape, [VMEM] * 4, 1 << 20, 2 << 20)(raw, *state)
        for k in range(2)
    )
    hq_got = swap(hq_oth)
    hqs = [lax.ppermute(x, "h", SWAP) for x in (hq_own, hq_got)]
    o = call(piece_kernel, shape((tokens, width)), [VMEM] * 4, 1 << 20, 1 << 16)(
        hq_own, hq_got, mats[1], w2_got
    )
    part = partial_product(place, o, w_out)
    w_other = call(
        stage_kernel, shape((width, n)), [SMEM] + [ANY] * 5, 1 << 16, 1 << 16, [semaphores(4)]
    )(place, hq_got, *w_parts)
    crossed, *hqs, _, _ = lax.optimization_barrier((crossed, *hqs, part, w_other))
    return finish_product(part, hqs, (crossed, swap(crossed)), w_other)


def solution(mesh):
    finer = Mesh(
        mesh.devices.reshape(4, 2, 4, 2, mesh.shape["head"]),
        ("z", "xl", "y", "c", "h"),
    )
    return jax.shard_map(
        shards,
        mesh=finer,
        in_specs=(
            P(CTX, "h"),
            P(CTX, "h"),
            P(CTX, "h"),
            P(CTX, "h"),
            P("h", None, None),
            P("h", None, None),
            P("h", None, None),
            P("h", None),
        ),
        out_specs=P(CTX, "h"),
        check_vma=False,
    )
```
